32 devices in a mesh: rows: 8 (over y, x, core), seq: 4 (over z).
Axes of the slice: x: 2, y: 2, z: 4, core: 2. Of those that a mesh axis runs over, the one named last changes fastest.
Arguments:
- resid_in: bfloat16 [96, 256, 768], P('rows', 'seq'), may hold values from -6 to 6
- mask: int32 [96, 256], P('rows', 'seq'), may hold values from 0 to 1, as said below
- steps_row: int32 [96], P('rows'), may hold values from 0 to 999
- cotangent: bfloat16 [96, 256, 768], P('rows', 'seq'), may hold values from -6 to 6
- attn_master: float32 [2359296], P(('rows', 'seq')), may hold values from -1.7320508 to 1.7320508, as said below
- attn_first: float32 [2359296], P(('rows', 'seq')), may hold values from -224 to 224
- attn_second: float32 [2359296], P(('rows', 'seq')), may hold values from 384 to 12288
- mlp_master: float32 [4718592], P(('rows', 'seq')), may hold values from -0.21875 to 0.21875
- mlp_first: float32 [4718592], P(('rows', 'seq')), may hold values from -224 to 224
- mlp_second: float32 [4718592], P(('rows', 'seq')), may hold values from 384 to 12288
- norm_master: float32 [5, 768], replicated, may hold values from -6 to 6, as said below
- norm_first: float32 [5, 768], replicated, may hold values from -224 to 224
- norm_second: float32 [5, 768], replicated, may hold values from 384 to 12288
- time_master: float32 [1000, 768], replicated, may hold values from -6 to 6
- time_first: float32 [1000, 768], replicated, may hold values from -4 to 4
- time_second: float32 [1000, 768], replicated, may hold values from 1 to 12
Outputs:
- resid_out: bfloat16 [96, 256, 768], P('rows', 'seq')
- grad_in: bfloat16 [96, 256, 768], P('rows', 'seq')
- attn_new: float32 [2359296], P(('rows', 'seq'))
- attn_first_new: float32 [2359296], P(('rows', 'seq'))
- attn_second_new: float32 [2359296], P(('rows', 'seq'))
- attn_copy: bfloat16 [2359296], P(('rows', 'seq'))
- mlp_new: float32 [4718592], P(('rows', 'seq'))
- mlp_first_new: float32 [4718592], P(('rows', 'seq'))
- mlp_second_new: float32 [4718592], P(('rows', 'seq'))
- perceptron_half_precision: bfloat16 [4718592], P(('rows', 'seq'))
- norm_new: float32 [5, 768], replicated
- norm_first_new: float32 [5, 768], replicated
- norm_second_new: float32 [5, 768], replicated
- time_new: float32 [1000, 768], replicated
- time_first_new: float32 [1000, 768], replicated
- time_second_new: float32 [1000, 768], replicated
The draws below stay inside these ranges and needn't reach their ends.
Inputs may be any that keep to these rules, and one draw needn't show every extreme that they name: `mask`: 1 marks an absorbed token; how many are absorbed varies strongly from sequence to sequence. `attn_master`: truncated normal entries. `norm_master`: gains about 1, biases and the absorbed-token vector of both signs.
All inputs are finite; a program needn't handle non-finite values.
Results may differ from the reference program's by a relative error of at most 0.0095.
Values may be sent and summed in bfloat16 or wider, within the bound.
A program may use at most 192 MiB of HBM per device.

```python
import math
import jax
import jax.numpy as jnp
from jax import lax

D = 768
HEADS = 12
HEAD_DIM = 64
FF = 3072
TSTEPS = 1000
LENGTH = 256
STEP = 10
ROWS = 96
ATTN_FLAT = 2359296
MLP_FLAT = 4718592


def shared_steps(key):
    first_key, second_key, third_key = jax.random.split(key, 3)
    step_rows = jax.random.randint(first_key, (ROWS,), 0, TSTEPS)
    top_row = jax.random.randint(second_key, (), 0, ROWS)
    bottom_row = (top_row + 1 + jax.random.randint(third_key, (), 0, ROWS - 1)) % ROWS
    step_rows = step_rows.at[top_row].set(TSTEPS - 1)
    return step_rows.at[bottom_row].set(0)


def draw_steps_row(key, part):
    return shared_steps(key).astype(jnp.int32)


def draw_mask(key, part):
    step_rows = shared_steps(key)
    key = jax.random.fold_in(key, 7)
    tickets = jax.random.randint(key, (ROWS, LENGTH), 0, TSTEPS * TSTEPS)
    limits = (step_rows[:, None] + 1) * (step_rows[:, None] + 1)
    return (tickets < limits).astype(jnp.int32)


def draw_attn_master(key, part):
    key = jax.random.fold_in(key, 11)
    position = jnp.arange(ATTN_FLAT)
    factor = jnp.where(position < 3 * D * D, D ** (-0.5), 2.0 * LENGTH ** 0.25 * D ** (-0.5))
    values = jax.random.truncated_normal(key, -6.0, 6.0, (ATTN_FLAT,), jnp.float32)
    return (values * factor).astype(jnp.float32)


def draw_norm_master(key, part):
    key = jax.random.fold_in(key, 13)
    values = jax.random.truncated_normal(key, -6.0, 6.0, (5, D), jnp.float32)
    row_index = jnp.arange(5)[:, None]
    factor = jnp.where(row_index == 4, 1.0, jnp.where(row_index % 2 == 1, 0.3, 0.15))
    offset = jnp.where((row_index == 0) | (row_index == 2), 1.0, 0.0)
    return (values * factor + offset).astype(jnp.float32)


def shard_levels(own_key, extent, shards, low, largest):
    factor_of, own = 1.0, jax.random.fold_in(own_key, 6)
    for dim, parts in shards:
        steps = jnp.exp(jax.random.uniform(jax.random.fold_in(own, dim), (parts,), jnp.float32, low / len(shards), largest / len(shards)))
        factor_of = factor_of * jnp.repeat(steps, extent[dim] // parts).reshape([-1 if axis == dim else 1 for axis in range(len(extent))])
    return factor_of


def noise(stream_key, shape, deviation, bound, cuts=(), held_as=jnp.bfloat16):
    loudness = shard_levels(stream_key, shape, cuts, -0.22, 0.18) if cuts else 1.0
    values = jax.random.normal(stream_key, shape, jnp.float32) * deviation * loudness
    return jnp.minimum(jnp.maximum(values, -bound), bound).astype(held_as)


def setup_inputs(seed: int = 0) -> dict:
    streams_of = jax.random.split(jax.random.key(seed), 17)
    return {
        "resid_in": noise(streams_of[0], (ROWS, LENGTH, D), 1.0, 6.0, ((0, 8), (1, 4))),
        "mask": draw_mask(jax.random.fold_in(streams_of[16], 71), 0),
        "steps_row": draw_steps_row(jax.random.fold_in(streams_of[16], 71), 0),
        "cotangent": noise(streams_of[3], (ROWS, LENGTH, D), 1.0, 6.0, ((0, 8), (1, 4))),
        "attn_master": draw_attn_master(jax.random.fold_in(streams_of[16], 71), 0),
        "attn_first": noise(streams_of[5], (ATTN_FLAT,), ((ROWS * LENGTH // 16) ** 0.5), 224.0, ((0, 32),), jnp.float32),
        "attn_second": jnp.clip(jnp.exp(math.log(12288.0) - 3.465736 * jax.random.uniform(streams_of[6], (ATTN_FLAT,), jnp.float32) ** shard_levels(streams_of[6], (ATTN_FLAT,), ((0, 32),), -0.2, 0.2)), 384.0, 12288.0),
        "mlp_master": noise(streams_of[7], (MLP_FLAT,), D ** -0.5, 0.21875, ((0, 32),), jnp.float32),
        "mlp_first": noise(streams_of[8], (MLP_FLAT,), ((ROWS * LENGTH // 16) ** 0.5), 224.0, ((0, 32),), jnp.float32),
        "mlp_second": jnp.clip(jnp.exp(math.log(12288.0) - 3.465736 * jax.random.uniform(streams_of[9], (MLP_FLAT,), jnp.float32) ** shard_levels(streams_of[9], (MLP_FLAT,), ((0, 32),), -0.2, 0.2)), 384.0, 12288.0),
        "norm_master": draw_norm_master(jax.random.fold_in(streams_of[16], 71), 0),
        "norm_first": noise(streams_of[11], (5, D), ((ROWS * LENGTH // 16) ** 0.5), 224.0, (), jnp.float32),
        "norm_second": jnp.clip(jnp.exp(jax.random.uniform(streams_of[12], (5, D), jnp.float32, math.log(384.0), math.log(12288.0))), 384.0, 12288.0),
        "time_master": noise(streams_of[13], (TSTEPS, D), 0.5, 6.0, (), jnp.float32),
        "time_first": noise(streams_of[14], (TSTEPS, D), (max(1, ROWS * LENGTH // (16 * TSTEPS)) ** 0.5), 4.0, (), jnp.float32),
        "time_second": jnp.clip(jnp.exp(jax.random.uniform(streams_of[15], (TSTEPS, D), jnp.float32, math.log(1.0), math.log(12.0))), 1.0, 12.0),
    }


@jax.custom_vjp
def low(v):
    return lax.optimization_barrier(v.astype(jnp.bfloat16)).astype(jnp.float32)

@jax.custom_vjp
def reduced_backward(v):
    return v

def low_keep(v):
    return (low(v), None)

def low_pass(kept, grad):
    return (grad,)

def back_keep(v):
    return (v, None)

def back_low(kept, grad):
    return (low(grad),)
low.defvjp(low_keep, low_pass)
reduced_backward.defvjp(back_keep, back_low)
PRODUCT_EXACTNESS = lax.Precision.HIGHEST
NORM_EPSILON = 1e-05

def layer_norm(stream, gain, bias):
    centre = lax.optimization_barrier(jnp.mean(stream, axis=-1, keepdims=True))
    centred = stream - centre
    spread = lax.optimization_barrier(jnp.mean(centred * centred, axis=-1, keepdims=True))
    return centred * lax.rsqrt(spread + NORM_EPSILON) * gain + bias

def attend_sequence(query_rows, key_rows, value_rows):
    scores = reduced_backward(jnp.einsum('qhe,khe->hqk', query_rows, key_rows, precision=PRODUCT_EXACTNESS) * HEAD_DIM ** (-0.5))
    soft_weights = jax.nn.softmax(scores, axis=-1)
    return jnp.einsum('hqk,khe->qhe', low(soft_weights), value_rows, precision=PRODUCT_EXACTNESS)

def forward(params_in, resid_rows, mask_rows, step_rows):
    attn_weights, mlp_weights, norm_weights, time_weights = params_in
    hidden_weight_table = low(attn_weights[:3 * D * D]).reshape(D, 3 * D)
    expansion_weight_table = low(attn_weights[3 * D * D:]).reshape(D, D)
    up_matrix = low(mlp_weights[:D * FF]).reshape(D, FF)
    down_matrix = low(mlp_weights[D * FF:]).reshape(FF, D)
    group_rows = resid_rows.shape[0]
    stream_in = resid_rows + mask_rows[..., None] * norm_weights[4] + time_weights[step_rows][:, None, :]
    first_normalized = low(layer_norm(stream_in, norm_weights[0], norm_weights[1]))
    projection_rows = jnp.einsum('frm,mk->frk', first_normalized, hidden_weight_table, precision=PRODUCT_EXACTNESS)
    projection_rows = reduced_backward(low(projection_rows))
    query_rows = projection_rows[..., :D].reshape(group_rows, LENGTH, HEADS, HEAD_DIM)
    key_rows = projection_rows[..., D:2 * D].reshape(group_rows, LENGTH, HEADS, HEAD_DIM)
    value_rows = projection_rows[..., 2 * D:].reshape(group_rows, LENGTH, HEADS, HEAD_DIM)
    attention_result = lax.map(jax.checkpoint(lambda pieces: attend_sequence(*pieces)), (query_rows, key_rows, value_rows))
    attention_result = reduced_backward(low(attention_result.reshape(group_rows, LENGTH, D)))
    branch_output = reduced_backward(jnp.einsum('frm,mk->frk', attention_result, expansion_weight_table, precision=PRODUCT_EXACTNESS))
    residual_middle = stream_in + branch_output
    second_normalized = low(layer_norm(residual_middle, norm_weights[2], norm_weights[3]))
    preactivation_rows = reduced_backward(jnp.einsum('nqz,za->nqa', second_normalized, up_matrix, precision=PRODUCT_EXACTNESS))
    activation_rows = low(jax.nn.gelu(preactivation_rows, approximate=True))
    return residual_middle + jnp.einsum('ozj,ji->ozi', activation_rows, down_matrix, precision=PRODUCT_EXACTNESS)

def adamw(master, moment_one, moment_two, gradient, step_rate):
    first_new = 0.5 * moment_one + 0.5 * gradient
    second_new = 0.5 * moment_two + 0.5 * gradient * gradient
    correct = 1.0 - 0.5 ** STEP
    update = first_new / correct / (jnp.sqrt(second_new / correct) + 1e-08)
    return (master - step_rate * (update + 0.1 * master), first_new, second_new)

def reference(resid_in, mask, steps_row, cotangent, attn_master, attn_first, attn_second, mlp_master, mlp_first, mlp_second, norm_master, norm_first, norm_second, time_master, time_first, time_second):
    params_in = (attn_master, mlp_master, norm_master, time_master)
    group_rows = math.gcd(ROWS, max(1, 4096 // LENGTH))
    group_count = ROWS // group_rows

    def group_step(totals, block_index):
        start = block_index * group_rows

        def take_rows(array):
            return lax.dynamic_slice_in_dim(array, start, group_rows, 0)
        resid_rows = take_rows(resid_in).astype(jnp.float32)
        mask_rows = take_rows(mask).astype(jnp.float32)
        step_rows = take_rows(steps_row)
        grad_rows = take_rows(cotangent).astype(jnp.float32) * mask_rows[..., None]
        output, adjoint_function = jax.vjp(lambda prm_in, stream: forward(prm_in, stream, mask_rows, step_rows), params_in, resid_rows)
        grads, grad_stream = adjoint_function(grad_rows)
        totals = jax.tree.map(jnp.add, totals, grads)
        return (totals, (output.astype(jnp.bfloat16), grad_stream.astype(jnp.bfloat16)))
    zeros = jax.tree.map(jnp.zeros_like, params_in)
    totals, (outputs, grad_streams) = lax.scan(group_step, zeros, jnp.arange(group_count, dtype=jnp.int32))
    resid_out = outputs.reshape(ROWS, LENGTH, D)
    grad_in = grad_streams.reshape(ROWS, LENGTH, D)
    attn_grad, mlp_grad, norm_grad, time_grad = totals
    attn_new, attn_first_new, attn_second_new = adamw(attn_master, attn_first, attn_second, attn_grad, 0.05)
    mlp_new, mlp_first_new, mlp_second_new = adamw(mlp_master, mlp_first, mlp_second, mlp_grad, 0.03)
    norm_new, norm_first_new, norm_second_new = adamw(norm_master, norm_first, norm_second, norm_grad, 0.2)
    time_new, time_first_new, time_second_new = adamw(time_master, time_first, time_second, time_grad, 0.3)
    return (resid_out, grad_in, attn_new, attn_first_new, attn_second_new, attn_new.astype(jnp.bfloat16), mlp_new, mlp_first_new, mlp_second_new, mlp_new.astype(jnp.bfloat16), norm_new, norm_first_new, norm_second_new, time_new, time_first_new, time_second_new)
```

```python
import functools

import jax
import jax.numpy as jnp
from jax import lax
from jax.experimental import pallas as pl
from jax.experimental.pallas import tpu as pltpu
from jax.sharding import PartitionSpec as P

HEAD_DIM = 64
FF = 3072
STEP = 10
NORM_EPSILON = 1e-05
GROUPS = 32
LANES = 128
TILE = 256
ROW_BLOCK = 64
GELU_C = 0.7978845608028654
GELU_A = 0.044715
LOG2E = 1.4426950408889634
BF = jnp.bfloat16
F32 = jnp.float32

NN = (((1,), (0,)), ((), ()))
NT = (((1,), (1,)), ((), ()))
TN = (((0,), (0,)), ((), ()))


def dot(a, b, dims=NN):
    return lax.dot_general(a, b, dims, preferred_element_type=F32)


def norm_stats(h):
    mean = jnp.mean(h, axis=-1, keepdims=True)
    centred = h - mean
    var = jnp.mean(centred * centred, axis=-1, keepdims=True)
    rs = lax.rsqrt(var + NORM_EPSILON)
    return centred * rs, rs


def fold(x):
    return jnp.sum(x.reshape(x.shape[0] // 8, 8, x.shape[1]), axis=0)


def add_small(small, which, x):
    small[which] = small[which] + fold(x)


class Layer:
    def __init__(self, **refs):
        self.__dict__.update(refs)
        self.T, self.D = self.h.shape
        self.L = self.mask.shape[0]
        self.S = self.T // self.L
        self.PAIRS = self.D // LANES
        self.NJ = FF // self.D

    def qkv_part(self, ref, j, c, n):
        rows = ref.shape[1] // 3
        used = self.D // rows
        return ref.at[pl.ds(0, used), pl.ds(pl.multiple_of(j * rows, rows), rows), pl.ds(pl.multiple_of(c, n), n)]

    def out_part(self, ref, c, n):
        rows = ref.shape[1]
        used = self.D // rows
        return ref.at[pl.ds(ref.shape[0] - used, used), :, pl.ds(pl.multiple_of(c, n), n)]

    def up_part(self, ref, j, c, n):
        rows = ref.shape[1] // self.NJ
        used = self.D // rows
        return ref.at[pl.ds(0, used), pl.ds(pl.multiple_of(j * rows, rows), rows), pl.ds(pl.multiple_of(c, n), n)]

    def down_part(self, ref, j, c, n):
        rows = ref.shape[1]
        used = self.D // rows
        return ref.at[pl.ds(ref.shape[0] // 2 + j * used, used), :, pl.ds(pl.multiple_of(c, n), n)]

    def mask_col(self, s, base, n):
        return self.mask[pl.ds(base, n), s : s + 1].astype(F32)

    def embed(self, s):
        def body(i, _):
            base = pl.multiple_of(i * ROW_BLOCK, ROW_BLOCK)
            rows = pl.ds(pl.multiple_of(s * self.L + base, ROW_BLOCK), ROW_BLOCK)
            m = self.mask_col(s, base, ROW_BLOCK)
            h = self.x[rows, :].astype(F32) + m * self.norm[4:5, :] + self.time[s : s + 1, :]
            self.h[rows, :] = h
            xhat, _ = norm_stats(h)
            self.n1[rows, :] = (xhat * self.norm[0:1, :] + self.norm[1:2, :]).astype(BF)
            return 0

        lax.fori_loop(0, self.L // ROW_BLOCK, body, 0)

    def project(self, s):
        per = self.D // TILE
        rows = pl.ds(s * self.L, self.L)

        def body(i, _):
            j, c = lax.div(i, per), lax.rem(i, per) * TILE
            w = self.qkv_part(self.wa, j, c, TILE)[...].reshape(self.D, TILE)
            y = dot(self.n1[rows, :], w)
            self.qkv[rows, pl.ds(pl.multiple_of(i * TILE, TILE), TILE)] = y.astype(BF)
            return 0

        lax.fori_loop(0, 3 * per, body, 0)

    def pair_slices(self, s, p):
        rows = pl.ds(pl.multiple_of(s * self.L, self.L), self.L)
        cols = [pl.ds(pl.multiple_of(k * self.D + p * LANES, LANES), LANES) for k in range(3)]
        return rows, cols

    def half(self, x, hh):
        first = lax.broadcasted_iota(jnp.int32, x.shape, 1) < HEAD_DIM
        zero = jnp.zeros_like(x)
        return jnp.where(first, zero, x) if hh else jnp.where(first, x, zero)

    def attend(self, s, p):
        rows, cols = self.pair_slices(s, p)
        q, k, v = (self.qkv[rows, c] for c in cols)
        total = None
        for hh in range(2):
            sc = dot(self.half(q, hh), k, NT)
            top = jnp.max(sc, axis=-1, keepdims=True)
            e = jnp.exp2((sc - top) * (HEAD_DIM**-0.5 * LOG2E))
            w = (e * (1.0 / jnp.sum(e, axis=-1, keepdims=True))).astype(BF)
            self.soft[s * 2 * self.PAIRS + p * 2 + hh] = w
            o = dot(w, self.half(v, hh))
            total = o if total is None else total + o
        self.att[rows, cols[0]] = total.astype(BF)

    def attend_sequence(self, s):
        def body(p, _):
            self.attend(s, p)
            return 0

        lax.fori_loop(0, self.PAIRS, body, 0)

    def outer(self, s):
        rows = pl.ds(s * self.L, self.L)

        def body(i, _):
            c = i * TILE
            cols = pl.ds(pl.multiple_of(c, TILE), TILE)
            w = self.out_part(self.wa, c, TILE)[...].reshape(self.D, TILE)
            self.mid[rows, cols] = self.h[rows, cols] + dot(self.att[rows, :], w)
            return 0

        lax.fori_loop(0, self.D // TILE, body, 0)

    def second_norm(self, s):
        def body(i, _):
            rows = pl.ds(pl.multiple_of(s * self.L + i * ROW_BLOCK, ROW_BLOCK), ROW_BLOCK)
            xhat, _ = norm_stats(self.mid[rows, :])
            self.n2[rows, :] = (xhat * self.norm[2:3, :] + self.norm[3:4, :]).astype(BF)
            return 0

        lax.fori_loop(0, self.L // ROW_BLOCK, body, 0)

    def up(self):
        per = self.D // TILE

        def body(i, _):
            j, c = lax.div(i, per), lax.rem(i, per) * TILE
            cols = pl.ds(pl.multiple_of(i * TILE, TILE), TILE)
            w = self.up_part(self.wm, j, c, TILE)[...].reshape(self.D, TILE)
            for s in range(self.S):
                rows = pl.ds(s * self.L, self.L)
                u = dot(self.n2[rows, :], w)
                uu = u * u
                t = jnp.tanh(GELU_C * (u * (1.0 + GELU_A * uu)))
                left = 0.5 * (1.0 + t)
                self.act[rows, cols] = (u * left).astype(BF)
                slope = left + (0.5 * GELU_C) * u * (1.0 - t * t) * (1.0 + 3.0 * GELU_A * uu)
                self.du[rows, cols] = slope.astype(BF)
            return 0

        lax.fori_loop(0, self.NJ * per, body, 0)

    def down(self):
        per = self.D // TILE

        def body(i, _):
            c = i * TILE
            cols = pl.ds(pl.multiple_of(c, TILE), TILE)
            for s in range(self.S):
                rows = pl.ds(s * self.L, self.L)
                total = self.mid[rows, cols]
                for j in range(self.NJ):
                    w = self.down_part(self.wm, j, c, TILE)[...].reshape(self.D, TILE)
                    total = total + dot(self.act[rows, pl.ds(j * self.D, self.D)], w)
                self.out[rows, cols] = total.astype(BF)
            return 0

        lax.fori_loop(0, per, body, 0)

    def mask_cotangent(self):
        for s in range(self.S):
            def body(i, _, s=s):
                base = pl.multiple_of(i * ROW_BLOCK, ROW_BLOCK)
                rows = pl.ds(pl.multiple_of(s * self.L + base, ROW_BLOCK), ROW_BLOCK)
                m = self.mask_col(s, base, ROW_BLOCK)
                self.g[rows, :] = (self.g[rows, :].astype(F32) * m).astype(BF)
                return 0

            lax.fori_loop(0, self.L // ROW_BLOCK, body, 0)

    def grad_pre(self):
        per = self.D // TILE

        def body(i, _):
            cols = pl.ds(pl.multiple_of(i * (self.D // 2), self.D // 2), self.D // 2)
            rows_w = self.wm.shape[1]
            used = self.D // 2 // rows_w
            w = self.wm[pl.ds(self.wm.shape[0] // 2 + i * used, used)].reshape(self.D // 2, self.D)
            for s in range(self.S):
                rows = pl.ds(s * self.L, self.L)
                d = dot(self.g[rows, :], w, NT)
                self.du[rows, cols] = (d * self.du[rows, cols].astype(F32)).astype(BF)
            return 0

        lax.fori_loop(0, 2 * self.NJ, body, 0)

    def grad_down(self):
        per = self.D // TILE
        for j in range(self.NJ):
            self.turn[...] = self.act[:, pl.ds(j * self.D, self.D)].T

            def body(i, _, j=j):
                c = pl.multiple_of(i * TILE, TILE)
                y = dot(self.turn[...], self.g[:, pl.ds(c, TILE)])
                ref = self.down_part(self.gm_down, j, c, TILE)
                ref[...] = y.astype(BF).reshape(ref.shape)
                return 0

            lax.fori_loop(0, per, body, 0)

    def grad_up(self):
        per = self.D // TILE
        self.turn[...] = self.n2[...].T

        def body(i, _):
            j, c = lax.div(i, per), lax.rem(i, per) * TILE
            y = dot(self.turn[...], self.du[:, pl.ds(pl.multiple_of(i * TILE, TILE), TILE)])
            ref = self.up_part(self.gm_up, j, c, TILE)
            ref[...] = y.astype(BF).reshape(ref.shape)
            return 0

        lax.fori_loop(0, self.NJ * per, body, 0)

    def grad_normed_two(self):
        rows_w = self.wm.shape[1] // self.NJ
        n = self.D // 2
        used = n // rows_w

        def body(i, _):
            cols = pl.ds(pl.multiple_of(i * n, n), n)
            for s in range(self.S):
                rows = pl.ds(s * self.L, self.L)
                total = None
                for j in range(self.NJ):
                    w = self.wm[pl.ds(i * used, used), pl.ds(j * rows_w, rows_w), :].reshape(n, self.D)
                    y = dot(self.du[rows, pl.ds(j * self.D, self.D)], w, NT)
                    total = y if total is None else total + y
                self.dn[rows, cols] = total
            return 0

        lax.fori_loop(0, 2, body, 0)

    def norm_two_back(self):
        def body(i, _):
            rows = pl.ds(pl.multiple_of(i * ROW_BLOCK, ROW_BLOCK), ROW_BLOCK)
            xhat, rs = norm_stats(self.mid[rows, :])
            dy = self.dn[rows, :]
            add_small(self.small, 5, dy * xhat)
            add_small(self.small, 6, dy)
            e = dy * self.norm[2:3, :]
            back = (e - jnp.mean(e, -1, keepdims=True) - xhat * jnp.mean(e * xhat, -1, keepdims=True)) * rs
            gm = self.g[rows, :].astype(F32) + back
            self.dn[rows, :] = gm
            self.gb[rows, :] = gm.astype(BF)
            return 0

        lax.fori_loop(0, self.T // ROW_BLOCK, body, 0)

    def grad_outer(self):
        self.turn[...] = self.att[...].T

        def body(i, _):
            c = pl.multiple_of(i * TILE, TILE)
            y = dot(self.turn[...], self.gb[:, pl.ds(c, TILE)])
            ref = self.out_part(self.ga, c, TILE)
            ref[...] = y.astype(BF).reshape(ref.shape)
            return 0

        lax.fori_loop(0, self.D // TILE, body, 0)

    def grad_attended(self):
        n = self.D // 2
        rows_w = self.wa.shape[1]
        used = n // rows_w
        first = self.wa.shape[0] - 2 * used

        def body(i, _):
            w = self.wa[pl.ds(first + i * used, used)].reshape(n, self.D)
            for s in range(self.S):
                rows = pl.ds(s * self.L, self.L)
                self.att[rows, pl.ds(pl.multiple_of(i * n, n), n)] = dot(self.gb[rows, :], w, NT).astype(BF)
            return 0

        lax.fori_loop(0, 2, body, 0)

    def attend_back(self, s, p):
        rows, cols = self.pair_slices(s, p)
        q, k, v = (self.qkv[rows, c] for c in cols)
        da = self.att[rows, cols[0]]
        dq = dk = dv = None
        for hh in range(2):
            w = self.soft[s * 2 * self.PAIRS + p * 2 + hh]
            da_h = self.half(da, hh)
            dp = dot(da_h, v, NT)
            wf = w.astype(F32)
            t = wf * dp
            ds = (t - wf * jnp.sum(t, axis=-1, keepdims=True)).astype(BF)
            parts = (dot(ds, self.half(k, hh)), dot(ds, self.half(q, hh), TN), dot(w, da_h, TN))
            dq, dk, dv = parts if dq is None else (dq + parts[0], dk + parts[1], dv + parts[2])
        scale = HEAD_DIM**-0.5
        self.qkv[rows, cols[0]] = (dq * scale).astype(BF)
        self.qkv[rows, cols[1]] = (dk * scale).astype(BF)
        self.qkv[rows, cols[2]] = dv.astype(BF)

    def attend_back_sequence(self, s):
        def body(p, _):
            self.attend_back(s, p)
            return 0

        lax.fori_loop(0, self.PAIRS, body, 0)

    def grad_normed_one(self, s):
        n = self.D // 3
        rows_w = self.wa.shape[1] // 3
        used = n // rows_w
        rows = pl.ds(s * self.L, self.L)

        def body(i, _):
            total = None
            for j in range(3):
                w = self.wa[pl.ds(i * used, used), pl.ds(j * rows_w, rows_w), :].reshape(n, self.D)
                y = dot(self.qkv[rows, pl.ds(j * self.D, self.D)], w, NT)
                total = y if total is None else total + y
            self.mid[rows, pl.ds(pl.multiple_of(i * n, n), n)] = total
            return 0

        lax.fori_loop(0, 3, body, 0)

    def norm_one_back(self, s):
        def body(i, _):
            base = pl.multiple_of(i * ROW_BLOCK, ROW_BLOCK)
            rows = pl.ds(pl.multiple_of(s * self.L + base, ROW_BLOCK), ROW_BLOCK)
            xhat, rs = norm_stats(self.h[rows, :])
            dy = self.mid[rows, :]
            add_small(self.small, 3, dy * xhat)
            add_small(self.small, 4, dy)
            e = dy * self.norm[0:1, :]
            back = (e - jnp.mean(e, -1, keepdims=True) - xhat * jnp.mean(e * xhat, -1, keepdims=True)) * rs
            gs = self.dn[rows, :] + back
            add_small(self.small, s, gs)
            add_small(self.small, 7, gs * self.mask_col(s, base, ROW_BLOCK))
            self.x[rows, :] = gs.astype(BF)
            return 0

        lax.fori_loop(0, self.L // ROW_BLOCK, body, 0)

    def grad_inner(self):
        per = self.D // TILE
        self.turn[...] = self.n1[...].T

        def body(i, _):
            j, c = lax.div(i, per), lax.rem(i, per) * TILE
            y = dot(self.turn[...], self.qkv[:, pl.ds(pl.multiple_of(i * TILE, TILE), TILE)])
            ref = self.qkv_part(self.ga, j, c, TILE)
            ref[...] = y.astype(BF).reshape(ref.shape)
            return 0

        lax.fori_loop(0, 3 * per, body, 0)


def run_all(k):
    for i in range(8):
        k.small[i] = jnp.zeros(k.small.shape[1:], F32)
    for s in range(k.S):
        k.embed(s)
        k.project(s)
        k.attend_sequence(s)
        k.outer(s)
        k.second_norm(s)
    k.up()
    k.down()
    k.mask_cotangent()
    k.grad_pre()
    k.grad_down()
    k.grad_up()
    k.grad_normed_two()
    k.norm_two_back()
    k.grad_outer()
    k.grad_attended()
    for s in range(k.S):
        k.attend_back_sequence(s)
        k.grad_normed_one(s)
        k.norm_one_back(s)
    k.grad_inner()


def compute_kernel(x, mask, g_in, time, norm, wa, wm, out, gin, ga, gm, small, *scratch):
    names = ("g", "h", "n1", "qkv", "att", "mid", "n2", "act", "du", "soft", "dn", "gb", "turn", "sums")
    refs = dict(zip(names, scratch))
    sums = refs.pop("sums")
    pltpu.sync_copy(x, gin)
    pltpu.sync_copy(g_in, refs["g"])
    layer = Layer(
        x=gin, mask=mask, time=time, norm=norm, wa=wa, wm=wm, out=out, ga=ga, gm_down=gm, gm_up=gm, small=sums, **refs
    )
    run_all(layer)
    for i in range(8):
        small[i : i + 1, :] = jnp.sum(sums[i], axis=0, keepdims=True)


def layer_scratch(T, D, S, L):
    heads = D // HEAD_DIM
    return dict(
        h=pltpu.VMEM((T, D), F32),
        n1=pltpu.VMEM((T, D), BF),
        qkv=pltpu.VMEM((T, 3 * D), BF),
        att=pltpu.VMEM((T, D), BF),
        mid=pltpu.VMEM((T, D), F32),
        n2=pltpu.VMEM((T, D), BF),
        act=pltpu.VMEM((T, FF), BF),
        du=pltpu.VMEM((T, FF), BF),
        soft=pltpu.VMEM((S * heads, L, L), BF),
        dn=pltpu.VMEM((T, D), F32),
        gb=pltpu.VMEM((T, D), BF),
        turn=pltpu.VMEM((D, D), BF),
        sums=pltpu.VMEM((8, 8, D), F32),
    )


def pad_rows(x):
    return jnp.pad(x, ((0, 8 - x.shape[0]), (0, 0)))


def rows_split(flat, groups, parts, D):
    return flat.reshape(groups, -1, parts, D).transpose(0, 2, 1, 3).reshape(groups, -1, D)


def rows_join(block, parts, D):
    groups = block.shape[0]
    return block.reshape(groups, parts, -1, D).transpose(0, 2, 1, 3).reshape(-1)


def adamw(master, moment_one, moment_two, gradient, step_rate):
    first_new = 0.5 * moment_one + 0.5 * gradient
    second_new = 0.5 * moment_two + 0.5 * gradient * gradient
    correct = 1.0 - 0.5**STEP
    update = first_new / correct / (jnp.sqrt(second_new / correct) + 1e-08)
    return (master - step_rate * (update + 0.1 * master), first_new, second_new)


def general(
    resid_in,
    mask,
    steps_row,
    cotangent,
    attn_master,
    attn_first,
    attn_second,
    mlp_master,
    mlp_first,
    mlp_second,
    norm_master,
    norm_first,
    norm_second,
    time_master,
    time_first,
    time_second,
):
    D = resid_in.shape[2]
    axes = ("rows", "seq")
    seq_count = lax.axis_size("seq")
    S = resid_in.shape[0] // seq_count
    L = resid_in.shape[1] * seq_count
    T = S * L
    attn_full = lax.all_gather(attn_master.astype(BF), axes, axis=0, tiled=True)
    mlp_full = lax.all_gather(mlp_master.astype(BF), axes, axis=0, tiled=True)
    inner = 3 * D * D
    wide = D * FF
    wa = jnp.concatenate(
        (rows_split(attn_full[:inner], 24, 3, D), attn_full[inner:].reshape(8, -1, D))
    )
    wm = jnp.concatenate((rows_split(mlp_full[:wide], 16, FF // D, D), mlp_full[wide:].reshape(16, -1, D)))
    exchange = functools.partial(lax.all_to_all, axis_name="seq", split_axis=0, concat_axis=1, tiled=True)
    x = exchange(resid_in).reshape(T, D)
    g = exchange(cotangent).reshape(T, D)
    mask_t = jnp.pad(exchange(mask.astype(BF)).T, ((0, 0), (0, LANES - S)))
    steps_use = lax.dynamic_slice_in_dim(steps_row, lax.axis_index("seq") * S, S, 0)
    time_rows = pad_rows(jnp.take(time_master, steps_use, axis=0))
    V = pl.BlockSpec(memory_space=pltpu.VMEM)
    A = pl.BlockSpec(memory_space=pl.ANY)
    shape = jax.ShapeDtypeStruct
    scratch = layer_scratch(T, D, S, L)
    out, gin, ga, gm, small = pl.pallas_call(
        compute_kernel,
        out_shape=(shape((T, D), BF), shape((T, D), BF), shape(wa.shape, BF), shape(wm.shape, BF), shape((8, D), F32)),
        in_specs=[A, V, A, V, V, V, V],
        out_specs=(V,) * 5,
        scratch_shapes=[pltpu.VMEM((T, D), BF)] + list(scratch.values()),
        compiler_params=pltpu.CompilerParams(vmem_limit_bytes=62 << 20),
    )(x, mask_t, g, time_rows, pad_rows(norm_master), wa, wm)
    attn_flat = jnp.concatenate((rows_join(ga[:24], 3, D), ga[24:].reshape(-1))).astype(F32)
    mlp_flat = jnp.concatenate((rows_join(gm[:16], FF // D, D), gm[16:].reshape(-1))).astype(F32)
    attn_grad = lax.psum_scatter(attn_flat, axes, scatter_dimension=0, tiled=True)
    mlp_grad = lax.psum_scatter(mlp_flat, axes, scatter_dimension=0, tiled=True)
    every = lax.all_gather(small, axes, axis=0)
    spread = functools.partial(lax.all_to_all, axis_name="seq", split_axis=1, concat_axis=0, tiled=True)
    return finish(
        spread(out.reshape(S, L, D)),
        spread(gin.reshape(S, L, D)),
        lax.all_gather(steps_row, "rows", axis=0, tiled=True),
        every,
        adamw(attn_master, attn_first, attn_second, attn_grad, 0.05),
        adamw(mlp_master, mlp_first, mlp_second, mlp_grad, 0.03),
        (norm_master, norm_first, norm_second),
        (time_master, time_first, time_second),
        S,
    )


def finish(resid_out, grad_in, steps, every, attn, mlp, norm, time, S):
    D = every.shape[2]
    norm_grad = jnp.sum(every[:, 3:8], axis=0)
    chosen = (jnp.arange(time[0].shape[0], dtype=jnp.int32)[:, None] == steps[None, :]).astype(F32)
    time_grad = jnp.dot(chosen, every[:, :S].reshape(-1, D), precision=lax.Precision.HIGHEST)
    return (
        resid_out,
        grad_in,
        *attn,
        attn[0].astype(BF),
        *mlp,
        mlp[0].astype(BF),
        *adamw(*norm, norm_grad, 0.2),
        *adamw(*time, time_grad, 0.3),
    )


def solution(mesh):
    flat, whole, tokens = P(("rows", "seq")), P(), P("rows", "seq", None)
    return jax.shard_map(
        general,
        mesh=mesh,
        in_specs=(tokens, P("rows", "seq"), P("rows"), tokens) + (flat,) * 6 + (whole,) * 6,
        out_specs=(tokens, tokens) + (flat,) * 8 + (whole,) * 6,
        check_vma=False,
    )
```

```python
import functools

import jax
import jax.numpy as jnp
from jax import lax
from jax.experimental import pallas as pl
from jax.experimental.pallas import tpu as pltpu
from jax.sharding import PartitionSpec as P

HEAD_DIM = 64
FF = 3072
STEP = 10
NORM_EPSILON = 1e-05
GROUPS = 32
LANES = 128
TILE = 256
ROW_BLOCK = 64
GELU_C = 0.7978845608028654
GELU_A = 0.044715
LOG2E = 1.4426950408889634
BF = jnp.bfloat16
F32 = jnp.float32

NN = (((1,), (0,)), ((), ()))
NT = (((1,), (1,)), ((), ()))
TN = (((0,), (0,)), ((), ()))


def dot(a, b, dims=NN):
    return lax.dot_general(a, b, dims, preferred_element_type=F32)


def norm_stats(h):
    mean = jnp.mean(h, axis=-1, keepdims=True)
    centred = h - mean
    var = jnp.mean(centred * centred, axis=-1, keepdims=True)
    rs = lax.rsqrt(var + NORM_EPSILON)
    return centred * rs, rs


def fold(x):
    return jnp.sum(x.reshape(x.shape[0] // 8, 8, x.shape[1]), axis=0)


def add_small(small, which, x):
    small[which] = small[which] + fold(x)


class Layer:
    def __init__(self, **refs):
        self.__dict__.update(refs)
        self.T, self.D = self.h.shape
        self.L = self.mask.shape[0]
        self.S = self.T // self.L
        self.PAIRS = self.D // LANES
        self.NJ = FF // self.D

    def qkv_part(self, ref, j, c, n):
        rows = ref.shape[1] // 3
        used = self.D // rows
        return ref.at[pl.ds(0, used), pl.ds(pl.multiple_of(j * rows, rows), rows), pl.ds(pl.multiple_of(c, n), n)]

    def out_part(self, ref, c, n):
        rows = ref.shape[1]
        used = self.D // rows
        return ref.at[pl.ds(ref.shape[0] - used, used), :, pl.ds(pl.multiple_of(c, n), n)]

    def up_part(self, ref, j, c, n):
        rows = ref.shape[1] // self.NJ
        used = self.D // rows
        return ref.at[pl.ds(0, used), pl.ds(pl.multiple_of(j * rows, rows), rows), pl.ds(pl.multiple_of(c, n), n)]

    def down_part(self, ref, j, c, n):
        rows = ref.shape[1]
        used = self.D // rows
        return ref.at[pl.ds(ref.shape[0] // 2 + j * used, used), :, pl.ds(pl.multiple_of(c, n), n)]

    def mask_col(self, s, base, n):
        return self.mask[pl.ds(base, n), s : s + 1].astype(F32)

    def embed(self, s):
        def body(i, _):
            base = pl.multiple_of(i * ROW_BLOCK, ROW_BLOCK)
            rows = pl.ds(pl.multiple_of(s * self.L + base, ROW_BLOCK), ROW_BLOCK)
            m = self.mask_col(s, base, ROW_BLOCK)
            h = self.x[rows, :].astype(F32) + m * self.norm[4:5, :] + self.time[s : s + 1, :]
            self.h[rows, :] = h
            xhat, _ = norm_stats(h)
            self.n1[rows, :] = (xhat * self.norm[0:1, :] + self.norm[1:2, :]).astype(BF)
            return 0

        lax.fori_loop(0, self.L // ROW_BLOCK, body, 0)

    def project(self, s):
        per = self.D // TILE
        rows = pl.ds(s * self.L, self.L)

        def body(i, _):
            j, c = lax.div(i, per), lax.rem(i, per) * TILE
            w = self.qkv_part(self.wa, j, c, TILE)[...].reshape(self.D, TILE)
            y = dot(self.n1[rows, :], w)
            self.qkv[rows, pl.ds(pl.multiple_of(i * TILE, TILE), TILE)] = y.astype(BF)
            return 0

        lax.fori_loop(0, 3 * per, body, 0)

    def pair_slices(self, s, p):
        rows = pl.ds(pl.multiple_of(s * self.L, self.L), self.L)
        cols = [pl.ds(pl.multiple_of(k * self.D + p * LANES, LANES), LANES) for k in range(3)]
        return rows, cols

    def half(self, x, hh):
        first = lax.broadcasted_iota(jnp.int32, x.shape, 1) < HEAD_DIM
        zero = jnp.zeros_like(x)
        return jnp.where(first, zero, x) if hh else jnp.where(first, x, zero)

    def attend(self, s, p):
        rows, cols = self.pair_slices(s, p)
        q, k, v = (self.qkv[rows, c] for c in cols)
        total = None
        for hh in range(2):
            sc = dot(self.half(q, hh), k, NT)
            top = jnp.max(sc, axis=-1, keepdims=True)
            e = jnp.exp2((sc - top) * (HEAD_DIM**-0.5 * LOG2E))
            w = (e * (1.0 / jnp.sum(e, axis=-1, keepdims=True))).astype(BF)
            self.soft[s * 2 * self.PAIRS + p * 2 + hh] = w
            o = dot(w, self.half(v, hh))
            total = o if total is None else total + o
        self.att[rows, cols[0]] = total.astype(BF)

    def attend_sequence(self, s):
        def body(p, _):
            self.attend(s, p)
            return 0

        lax.fori_loop(0, self.PAIRS, body, 0)

    def outer(self, s):
        rows = pl.ds(s * self.L, self.L)

        def body(i, _):
            c = i * TILE
            cols = pl.ds(pl.multiple_of(c, TILE), TILE)
            w = self.out_part(self.wa, c, TILE)[...].reshape(self.D, TILE)
            self.mid[rows, cols] = self.h[rows, cols] + dot(self.att[rows, :], w)
            return 0

        lax.fori_loop(0, self.D // TILE, body, 0)

    def second_norm(self, s):
        def body(i, _):
            rows = pl.ds(pl.multiple_of(s * self.L + i * ROW_BLOCK, ROW_BLOCK), ROW_BLOCK)
            xhat, _ = norm_stats(self.mid[rows, :])
            self.n2[rows, :] = (xhat * self.norm[2:3, :] + self.norm[3:4, :]).astype(BF)
            return 0

        lax.fori_loop(0, self.L // ROW_BLOCK, body, 0)

    def up(self):
        per = self.D // TILE

        def body(i, _):
            j, c = lax.div(i, per), lax.rem(i, per) * TILE
            cols = pl.ds(pl.multiple_of(i * TILE, TILE), TILE)
            w = self.up_part(self.wm, j, c, TILE)[...].reshape(self.D, TILE)
            for s in range(self.S):
                rows = pl.ds(s * self.L, self.L)
                u = dot(self.n2[rows, :], w)
                uu = u * u
                t = jnp.tanh(GELU_C * (u * (1.0 + GELU_A * uu)))
                left = 0.5 * (1.0 + t)
                self.act[pl.ds(pl.multiple_of(j * self.T + s * self.L, self.L), self.L), pl.ds(pl.multiple_of(c, TILE), TILE)] = (u * left).astype(BF)
                slope = left + (0.5 * GELU_C) * u * (1.0 - t * t) * (1.0 + 3.0 * GELU_A * uu)
                self.du[rows, cols] = slope.astype(BF)
            return 0

        lax.fori_loop(0, self.NJ * per, body, 0)

    def down(self):
        per = self.D // TILE

        def body(i, _):
            c = i * TILE
            cols = pl.ds(pl.multiple_of(c, TILE), TILE)
            for s in range(self.S):
                rows = pl.ds(s * self.L, self.L)
                total = self.mid[rows, cols]
                for j in range(self.NJ):
                    w = self.down_part(self.wm, j, c, TILE)[...].reshape(self.D, TILE)
                    total = total + dot(self.act[pl.ds(j * self.T + s * self.L, self.L), :], w)
                self.out[rows, cols] = total.astype(BF)
            return 0

        lax.fori_loop(0, per, body, 0)

    def mask_cotangent(self):
        for s in range(self.S):
            def body(i, _, s=s):
                base = pl.multiple_of(i * ROW_BLOCK, ROW_BLOCK)
                rows = pl.ds(pl.multiple_of(s * self.L + base, ROW_BLOCK), ROW_BLOCK)
                m = self.mask_col(s, base, ROW_BLOCK)
                self.g[rows, :] = (self.g[rows, :].astype(F32) * m).astype(BF)
                return 0

            lax.fori_loop(0, self.L // ROW_BLOCK, body, 0)

    def grad_pre(self):
        per = self.D // TILE

        def body(i, _):
            cols = pl.ds(pl.multiple_of(i * (self.D // 2), self.D // 2), self.D // 2)
            rows_w = self.wm.shape[1]
            used = self.D // 2 // rows_w
            w = self.wm[pl.ds(self.wm.shape[0] // 2 + i * used, used)].reshape(self.D // 2, self.D)
            for s in range(self.S):
                rows = pl.ds(s * self.L, self.L)
                d = dot(self.g[rows, :], w, NT)
                self.du[rows, cols] = (d * self.du[rows, cols].astype(F32)).astype(BF)
            return 0

        lax.fori_loop(0, 2 * self.NJ, body, 0)

    def grad_down(self):
        per = self.D // TILE
        for j in range(self.NJ):
            self.turn[...] = self.act[pl.ds(j * self.T, self.T), :].T

            def body(i, _, j=j):
                c = pl.multiple_of(i * TILE, TILE)
                y = dot(self.turn[...], self.g[:, pl.ds(c, TILE)])
                ref = self.down_part(self.gm_down, j, c, TILE)
                ref[...] = y.astype(BF).reshape(ref.shape)
                return 0

            lax.fori_loop(0, per, body, 0)

    def grad_up(self):
        per = self.D // TILE
        self.turn[...] = self.n2[...].T

        def body(i, _):
            j, c = lax.div(i, per), lax.rem(i, per) * TILE
            y = dot(self.turn[...], self.du[:, pl.ds(pl.multiple_of(i * TILE, TILE), TILE)])
            ref = self.up_part(self.gm_up, j, c, TILE)
            ref[...] = y.astype(BF).reshape(ref.shape)
            return 0

        lax.fori_loop(0, self.NJ * per, body, 0)

    def grad_normed_two(self):
        rows_w = self.wm.shape[1] // self.NJ
        n = self.D // 2
        used = n // rows_w

        def body(i, _):
            cols = pl.ds(pl.multiple_of(i * n, n), n)
            for s in range(self.S):
                rows = pl.ds(s * self.L, self.L)
                total = None
                for j in range(self.NJ):
                    w = self.wm[pl.ds(i * used, used), pl.ds(j * rows_w, rows_w), :].reshape(n, self.D)
                    y = dot(self.du[rows, pl.ds(j * self.D, self.D)], w, NT)
                    total = y if total is None else total + y
                self.dn[rows, cols] = total
            return 0

        lax.fori_loop(0, 2, body, 0)

    def norm_two_back(self):
        def body(i, _):
            rows = pl.ds(pl.multiple_of(i * ROW_BLOCK, ROW_BLOCK), ROW_BLOCK)
            xhat, rs = norm_stats(self.mid[rows, :])
            dy = self.dn[rows, :]
            add_small(self.small, 5, dy * xhat)
            add_small(self.small, 6, dy)
            e = dy * self.norm[2:3, :]
            back = (e - jnp.mean(e, -1, keepdims=True) - xhat * jnp.mean(e * xhat, -1, keepdims=True)) * rs
            gm = self.g[rows, :].astype(F32) + back
            self.dn[rows, :] = gm
            self.gb[rows, :] = gm.astype(BF)
            return 0

        lax.fori_loop(0, self.T // ROW_BLOCK, body, 0)

    def grad_outer(self):
        self.turn[...] = self.att[...].T

        def body(i, _):
            c = pl.multiple_of(i * TILE, TILE)
            y = dot(self.turn[...], self.gb[:, pl.ds(c, TILE)])
            ref = self.out_part(self.ga, c, TILE)
            ref[...] = y.astype(BF).reshape(ref.shape)
            return 0

        lax.fori_loop(0, self.D // TILE, body, 0)

    def grad_attended(self):
        n = self.D // 2
        rows_w = self.wa.shape[1]
        used = n // rows_w
        first = self.wa.shape[0] - 2 * used

        def body(i, _):
            w = self.wa[pl.ds(first + i * used, used)].reshape(n, self.D)
            for s in range(self.S):
                rows = pl.ds(s * self.L, self.L)
                self.att[rows, pl.ds(pl.multiple_of(i * n, n), n)] = dot(self.gb[rows, :], w, NT).astype(BF)
            return 0

        lax.fori_loop(0, 2, body, 0)

    def attend_back(self, s, p):
        rows, cols = self.pair_slices(s, p)
        q, k, v = (self.qkv[rows, c] for c in cols)
        da = self.att[rows, cols[0]]
        dq = dk = dv = None
        for hh in range(2):
            w = self.soft[s * 2 * self.PAIRS + p * 2 + hh]
            da_h = self.half(da, hh)
            dp = dot(da_h, v, NT)
            wf = w.astype(F32)
            t = wf * dp
            ds = (t - wf * jnp.sum(t, axis=-1, keepdims=True)).astype(BF)
            parts = (dot(ds, self.half(k, hh)), dot(ds, self.half(q, hh), TN), dot(w, da_h, TN))
            dq, dk, dv = parts if dq is None else (dq + parts[0], dk + parts[1], dv + parts[2])
        scale = HEAD_DIM**-0.5
        self.qkv[rows, cols[0]] = (dq * scale).astype(BF)
        self.qkv[rows, cols[1]] = (dk * scale).astype(BF)
        self.qkv[rows, cols[2]] = dv.astype(BF)

    def attend_back_sequence(self, s):
        def body(p, _):
            self.attend_back(s, p)
            return 0

        lax.fori_loop(0, self.PAIRS, body, 0)

    def grad_normed_one(self, s):
        n = self.D // 3
        rows_w = self.wa.shape[1] // 3
        used = n // rows_w
        rows = pl.ds(s * self.L, self.L)

        def body(i, _):
            total = None
            for j in range(3):
                w = self.wa[pl.ds(i * used, used), pl.ds(j * rows_w, rows_w), :].reshape(n, self.D)
                y = dot(self.qkv[rows, pl.ds(j * self.D, self.D)], w, NT)
                total = y if total is None else total + y
            self.mid[rows, pl.ds(pl.multiple_of(i * n, n), n)] = total
            return 0

        lax.fori_loop(0, 3, body, 0)

    def norm_one_back(self, s):
        def body(i, _):
            base = pl.multiple_of(i * ROW_BLOCK, ROW_BLOCK)
            rows = pl.ds(pl.multiple_of(s * self.L + base, ROW_BLOCK), ROW_BLOCK)
            xhat, rs = norm_stats(self.h[rows, :])
            dy = self.mid[rows, :]
            add_small(self.small, 3, dy * xhat)
            add_small(self.small, 4, dy)
            e = dy * self.norm[0:1, :]
            back = (e - jnp.mean(e, -1, keepdims=True) - xhat * jnp.mean(e * xhat, -1, keepdims=True)) * rs
            gs = self.dn[rows, :] + back
            add_small(self.small, s, gs)
            add_small(self.small, 7, gs * self.mask_col(s, base, ROW_BLOCK))
            self.x[rows, :] = gs.astype(BF)
            return 0

        lax.fori_loop(0, self.L // ROW_BLOCK, body, 0)

    def grad_inner(self):
        per = self.D // TILE
        self.turn[...] = self.n1[...].T

        def body(i, _):
            j, c = lax.div(i, per), lax.rem(i, per) * TILE
            y = dot(self.turn[...], self.qkv[:, pl.ds(pl.multiple_of(i * TILE, TILE), TILE)])
            ref = self.qkv_part(self.ga, j, c, TILE)
            ref[...] = y.astype(BF).reshape(ref.shape)
            return 0

        lax.fori_loop(0, 3 * per, body, 0)


def run_all(k):
    for i in range(8):
        k.small[i] = jnp.zeros(k.small.shape[1:], F32)
    for s in range(k.S):
        k.embed(s)
        k.project(s)
        k.attend_sequence(s)
        k.outer(s)
        k.second_norm(s)
    k.up()
    k.down()
    k.mask_cotangent()
    k.grad_pre()
    k.grad_down()
    k.grad_up()
    k.grad_normed_two()
    k.norm_two_back()
    k.grad_outer()
    k.grad_attended()
    for s in range(k.S):
        k.attend_back_sequence(s)
        k.grad_normed_one(s)
        k.norm_one_back(s)
    k.grad_inner()


def flip(index, bit):
    return index + bit - 2 * bit * lax.rem(lax.div(index, bit), 2)


def pick(table, index):
    value = table[0]
    for i in range(1, len(table)):
        value = jnp.where(index == i, table[i], value)
    return value


class Links:
    def __init__(self, Z, S, part):
        self.Z, self.S, self.part = Z, S, part
        self.r, self.z = lax.axis_index("rows"), lax.axis_index("seq")
        r = self.r
        self.core, self.xn, self.yn = flip(r, 1), flip(r, 2), flip(r, 4)
        self.diag = flip(self.xn, 4)
        self.pending = []
        orders = [sorted(range(Z), key=lambda a: (abs(a - z), a)) for z in range(Z)]
        self.order = [pick([orders[z][i] for z in range(Z)], self.z) for i in range(Z)]
        self.has_right, self.has_left = self.z < Z - 1, self.z > 0

    def barrier(self):
        bar = pltpu.get_barrier_semaphore()
        peers = [(self.core, self.z), (self.xn, self.z), (self.yn, self.z)]
        peers += [(self.r, lax.rem(self.z + i, self.Z)) for i in range(1, self.Z)]
        for peer in peers:
            pl.semaphore_signal(bar, 1, device_id=peer, device_id_type=pl.DeviceIdType.MESH)
        pl.semaphore_wait(bar, len(peers))

    def send(self, src, dst, ss, rs, peer, cond=None):
        copy = pltpu.make_async_remote_copy(
            src, dst, ss, rs, device_id=peer, device_id_type=pl.DeviceIdType.MESH
        )
        if cond is None:
            copy.start()
        else:
            pl.when(cond)(copy.start)
        self.pending.append((cond, copy))

    def arrived(self, dst, rs, cond=None):
        copy = pltpu.make_async_remote_copy(
            dst, dst, rs, rs, device_id=(self.core, self.z), device_id_type=pl.DeviceIdType.MESH
        )
        if cond is None:
            copy.wait_recv()
        else:
            pl.when(cond)(copy.wait_recv)

    def flush(self, kept=0):
        for cond, copy in self.pending[kept:]:
            if cond is None:
                copy.wait_send()
            else:
                pl.when(cond)(copy.wait_send)
        del self.pending[kept:]

    def gather(self, w, ss, rs):
        Z, z = self.Z, self.z
        count = [0]

        def go(row, zz, peer, cond=None):
            i = row * Z + zz
            self.send(w.at[i], w.at[i], ss.at[count[0]], rs.at[i], peer, cond)
            count[0] += 1

        def got(row, zz):
            i = row * Z + zz
            self.arrived(w.at[i], rs.at[i])

        def own(i):
            zz = self.order[i]
            if i:
                got(self.r, zz)
            go(self.r, zz, (self.r, z + 1), jnp.logical_and(zz <= z, self.has_right))
            go(self.r, zz, (self.r, z - 1), jnp.logical_and(zz >= z, self.has_left))
            go(self.r, zz, (self.xn, z))
            go(self.r, zz, (self.yn, z))
            go(self.r, zz, (self.core, z))

        def side(i):
            zz = self.order[i]
            got(self.xn, zz)
            go(self.xn, zz, (self.yn, z), zz < Z // 2)
            got(self.yn, zz)
            go(self.yn, zz, (self.xn, z), zz >= Z // 2)
            go(self.xn, zz, (self.core, z))
            go(self.yn, zz, (self.core, z))

        def far(i):
            zz = self.order[i]
            got(self.diag, zz)
            go(self.diag, zz, (self.core, z))

        def last():
            for row in (self.r, self.xn, self.yn, self.diag):
                for i in range(Z):
                    got(flip(row, 1), self.order[i])

        steps = [functools.partial(own, 0), functools.partial(own, 1)]
        for i in range(Z):
            if i + 2 < Z:
                steps.append(functools.partial(own, i + 2))
            steps.append(functools.partial(side, i))
            if i:
                steps.append(functools.partial(far, i - 1))
        steps.append(functools.partial(far, Z - 1))
        steps.append(last)
        return steps

    def exchange_in(self, src, dst, ss, rs, local, seqs):
        L = self.part * self.Z
        for i in seqs:
            for step in range(1, self.Z):
                to = lax.rem(self.z + step, self.Z)
                rows = pl.ds(i * L + self.z * self.part, self.part)
                n = i * (self.Z - 1) + step - 1
                self.send(src.at[to * self.S + i], dst.at[rows], ss.at[n], rs.at[n], (self.r, to))
            rows = pl.ds(i * L + self.z * self.part, self.part)
            pltpu.make_async_copy(src.at[self.z * self.S + i], dst.at[rows], local.at[i]).start()

    def exchange_in_done(self, src, dst, rs, local, i):
        L = self.part * self.Z
        for step in range(1, self.Z):
            source = lax.rem(self.z + self.Z - step, self.Z)
            rows = pl.ds(i * L + source * self.part, self.part)
            self.arrived(dst.at[rows], rs.at[i * (self.Z - 1) + step - 1])
        rows = pl.ds(i * L + self.z * self.part, self.part)
        pltpu.make_async_copy(src.at[self.z * self.S + i], dst.at[rows], local.at[i]).wait()

    def exchange_out(self, src, dst, ss, rs, local, i):
        L = self.part * self.Z
        for step in range(1, self.Z):
            to = lax.rem(self.z + step, self.Z)
            rows = pl.ds(i * L + to * self.part, self.part)
            n = i * (self.Z - 1) + step - 1
            self.send(src.at[rows], dst.at[self.z * self.S + i], ss.at[n], rs.at[n], (self.r, to))
        rows = pl.ds(i * L + self.z * self.part, self.part)
        pltpu.make_async_copy(src.at[rows], dst.at[self.z * self.S + i], local.at[i]).start()

    def exchange_out_done(self, src, dst, rs, local, i):
        L = self.part * self.Z
        for step in range(1, self.Z):
            source = lax.rem(self.z + self.Z - step, self.Z)
            self.arrived(dst.at[source * self.S + i], rs.at[i * (self.Z - 1) + step - 1])
        rows = pl.ds(i * L + self.z * self.part, self.part)
        pltpu.make_async_copy(src.at[rows], dst.at[self.z * self.S + i], local.at[i]).wait()

    def scatter(self, g, base, inbox, ss, rs, total):
        Z, z = self.Z, self.z
        half = Z // 2
        chip = lax.div(self.r, 2)
        k = lax.rem(self.r, 2)
        cx, cy = flip(chip, 1), flip(chip, 2)
        cd = flip(cx, 2)
        rows = total.shape[0]

        def block(c, parity, lo, n):
            return g.at[pl.ds(base + (2 * c + parity) * Z + lo, n)]

        def inslot(i, n):
            return inbox.at[pl.ds(i, n), pl.ds(0, rows)]

        def add(dst, src, n):
            def body(i, _):
                dst[i] = (dst[i].astype(F32) + src[i].astype(F32)).astype(BF)
                return 0

            lax.fori_loop(0, n, body, 0)

        XY = 4 * Z
        ZB = XY + 6 * half

        def core_send(c):
            self.send(block(c, 1 - k, 0, Z), inslot(c * Z, Z), ss.at[c], rs.at[c], (self.core, z))

        def core_add(c):
            self.arrived(inslot(c * Z, Z), rs.at[c])
            add(block(c, k, 0, Z), inslot(c * Z, Z), Z)

        def xy_send(slot, c, lo, peer):
            i = XY + slot * half
            self.send(block(c, k, lo, half), inslot(i, half), ss.at[4 + slot], rs.at[4 + slot], (peer, z))

        def xy_add(slot, c, lo):
            i = XY + slot * half
            self.arrived(inslot(i, half), rs.at[4 + slot])
            add(block(c, k, lo, half), inslot(i, half), half)

        def first_send():
            xy_send(0, cd, 0, self.xn)
            xy_send(2, cd, half, self.yn)
            xy_send(1, cx, 0, self.xn)
            xy_send(3, cy, half, self.yn)

        def second():
            xy_add(0, cy, 0)
            xy_send(4, cy, 0, self.yn)
            xy_add(2, cx, half)
            xy_send(5, cx, half, self.xn)

        def second_own():
            xy_add(1, chip, 0)
            xy_add(3, chip, half)

        def third():
            xy_add(4, chip, 0)
            xy_add(5, chip, half)

        def line(zz_static):
            for target, going, back, step, slot in (
                (zz_static, self.has_right, self.has_left, 1, ZB + zz_static - 1),
                (Z - 1 - zz_static, self.has_left, self.has_right, -1, ZB + Z - 1 + zz_static - 1),
            ):
                sem = 10 + slot - ZB
                ahead = (target > z) if step == 1 else (target < z)
                own = block(chip, k, target, 1)
                box = inslot(slot, 1)

                @pl.when(jnp.logical_and(ahead, back))
                def _():
                    self.arrived(box, rs.at[sem])
                    own[0] = (own[0].astype(F32) + box[0].astype(F32)).astype(BF)

                self.send(own, box, ss.at[sem], rs.at[sem], (self.r, z + step), jnp.logical_and(ahead, going))

        def final():
            mine = block(chip, k, z, 1)
            total[...] = mine[0].astype(F32)
            left = inslot(ZB + z - 1, 1)
            right = inslot(ZB + Z - 1 + Z - 2 - z, 1)

            @pl.when(self.has_left)
            def _():
                self.arrived(left, rs.at[10 + z - 1])
                total[...] += left[0].astype(F32)

            @pl.when(self.has_right)
            def _():
                self.arrived(right, rs.at[10 + Z - 1 + Z - 2 - z])
                total[...] += right[0].astype(F32)

        return dict(
            core_send=core_send,
            core_add=core_add,
            first_send=first_send,
            second=second,
            second_own=second_own,
            third=third,
            line=line,
            final=final,
        )


def compute_kernel(x, mask, g_in, time, norm, wa, wm, out, gin, ga, gm, small, *scratch):
    names = ("g", "h", "n1", "qkv", "att", "mid", "n2", "act", "du", "soft", "dn", "gb", "turn", "sums")
    refs = dict(zip(names, scratch))
    sums = refs.pop("sums")
    pltpu.sync_copy(x, gin)
    pltpu.sync_copy(g_in, refs["g"])
    layer = Layer(
        x=gin, mask=mask, time=time, norm=norm, wa=wa, wm=wm, out=out, ga=ga, gm_down=gm, gm_up=gm, small=sums, **refs
    )
    run_all(layer)
    for i in range(8):
        small[i : i + 1, :] = jnp.sum(sums[i], axis=0, keepdims=True)


def layer_scratch(T, D, S, L):
    heads = D // HEAD_DIM
    return dict(
        h=pltpu.VMEM((T, D), F32),
        n1=pltpu.VMEM((T, D), BF),
        qkv=pltpu.VMEM((T, 3 * D), BF),
        att=pltpu.VMEM((T, D), BF),
        mid=pltpu.VMEM((T, D), F32),
        n2=pltpu.VMEM((T, D), BF),
        act=pltpu.VMEM((FF // D * T, D), BF),
        du=pltpu.VMEM((T, FF), BF),
        soft=pltpu.VMEM((S * heads, L, L), BF),
        dn=pltpu.VMEM((T, D), F32),
        gb=pltpu.VMEM((T, D), BF),
        turn=pltpu.VMEM((D, D), BF),
        sums=pltpu.VMEM((8, 8, D), F32),
    )


def pad_rows(x):
    return jnp.pad(x, ((0, 8 - x.shape[0]), (0, 0)))


def rows_split(flat, groups, parts, D):
    return flat.reshape(groups, -1, parts, D).transpose(0, 2, 1, 3).reshape(groups, -1, D)


def rows_join(block, parts, D):
    groups = block.shape[0]
    return block.reshape(groups, parts, -1, D).transpose(0, 2, 1, 3).reshape(-1)


def adamw(master, moment_one, moment_two, gradient, step_rate):
    first_new = 0.5 * moment_one + 0.5 * gradient
    second_new = 0.5 * moment_two + 0.5 * gradient * gradient
    correct = 1.0 - 0.5**STEP
    update = first_new / correct / (jnp.sqrt(second_new / correct) + 1e-08)
    return (master - step_rate * (update + 0.1 * master), first_new, second_new)


def general(
    resid_in,
    mask,
    steps_row,
    cotangent,
    attn_master,
    attn_first,
    attn_second,
    mlp_master,
    mlp_first,
    mlp_second,
    norm_master,
    norm_first,
    norm_second,
    time_master,
    time_first,
    time_second,
):
    D = resid_in.shape[2]
    axes = ("rows", "seq")
    seq_count = lax.axis_size("seq")
    S = resid_in.shape[0] // seq_count
    L = resid_in.shape[1] * seq_count
    T = S * L
    attn_full = lax.all_gather(attn_master.astype(BF), axes, axis=0, tiled=True)
    mlp_full = lax.all_gather(mlp_master.astype(BF), axes, axis=0, tiled=True)
    inner = 3 * D * D
    wide = D * FF
    wa = jnp.concatenate(
        (rows_split(attn_full[:inner], 24, 3, D), attn_full[inner:].reshape(8, -1, D))
    )
    wm = jnp.concatenate((rows_split(mlp_full[:wide], 16, FF // D, D), mlp_full[wide:].reshape(16, -1, D)))
    exchange = functools.partial(lax.all_to_all, axis_name="seq", split_axis=0, concat_axis=1, tiled=True)
    x = exchange(resid_in).reshape(T, D)
    g = exchange(cotangent).reshape(T, D)
    mask_t = jnp.pad(exchange(mask.astype(BF)).T, ((0, 0), (0, LANES - S)))
    steps_use = lax.dynamic_slice_in_dim(steps_row, lax.axis_index("seq") * S, S, 0)
    time_rows = pad_rows(jnp.take(time_master, steps_use, axis=0))
    V = pl.BlockSpec(memory_space=pltpu.VMEM)
    A = pl.BlockSpec(memory_space=pl.ANY)
    shape = jax.ShapeDtypeStruct
    scratch = layer_scratch(T, D, S, L)
    out, gin, ga, gm, small = pl.pallas_call(
        compute_kernel,
        out_shape=(shape((T, D), BF), shape((T, D), BF), shape(wa.shape, BF), shape(wm.shape, BF), shape((8, D), F32)),
        in_specs=[A, V, A, V, V, V, V],
        out_specs=(V,) * 5,
        scratch_shapes=[pltpu.VMEM((T, D), BF)] + list(scratch.values()),
        compiler_params=pltpu.CompilerParams(vmem_limit_bytes=62 << 20),
    )(x, mask_t, g, time_rows, pad_rows(norm_master), wa, wm)
    attn_flat = jnp.concatenate((rows_join(ga[:24], 3, D), ga[24:].reshape(-1))).astype(F32)
    mlp_flat = jnp.concatenate((rows_join(gm[:16], FF // D, D), gm[16:].reshape(-1))).astype(F32)
    attn_grad = lax.psum_scatter(attn_flat, axes, scatter_dimension=0, tiled=True)
    mlp_grad = lax.psum_scatter(mlp_flat, axes, scatter_dimension=0, tiled=True)
    every = lax.all_gather(small, axes, axis=0)
    spread = functools.partial(lax.all_to_all, axis_name="seq", split_axis=1, concat_axis=0, tiled=True)
    return finish(
        spread(out.reshape(S, L, D)),
        spread(gin.reshape(S, L, D)),
        lax.all_gather(steps_row, "rows", axis=0, tiled=True),
        every,
        adamw(attn_master, attn_first, attn_second, attn_grad, 0.05),
        adamw(mlp_master, mlp_first, mlp_second, mlp_grad, 0.03),
        (norm_master, norm_first, norm_second),
        (time_master, time_first, time_second),
        S,
    )


def finish(resid_out, grad_in, steps, every, attn, mlp, norm, time, S):
    D = every.shape[2]
    norm_grad = jnp.sum(every[:, 3:8], axis=0)
    chosen = (jnp.arange(time[0].shape[0], dtype=jnp.int32)[:, None] == steps[None, :]).astype(F32)
    time_grad = jnp.dot(chosen, every[:, :S].reshape(-1, D), precision=lax.Precision.HIGHEST)
    return (
        resid_out,
        grad_in,
        *attn,
        attn[0].astype(BF),
        *mlp,
        mlp[0].astype(BF),
        *adamw(*norm, norm_grad, 0.2),
        *adamw(*time, time_grad, 0.3),
    )


LAYER_REFS = ("h", "n1", "qkv", "att", "mid", "n2", "act", "du", "soft", "dn", "turn", "sums")


def whole_kernel(
    cfg, resid, cot, mask_in, time, norm, sa, sm, resid_out, grad_in, ta, tm, every_out, *scratch
):
    Z, S, part = cfg
    names = (
        "wa", "wm", "inbox", "x", "g", "mask", "h", "n1",
        "qkv", "att", "mid", "n2", "act", "du", "soft", "dn",
        "turn", "sums", "every", "sem_a", "sem_m", "sem_e", "sem_in", "sem_cot",
        "sem_out", "sem_gin", "sem_mask", "loc", "sem_ra", "sem_rm", "credit",
    )
    v = dict(zip(names, scratch))
    wm, ga = v["wm"], v["act"].reshape(GROUPS, v["wa"].shape[1], v["wa"].shape[2])
    half = GROUPS // 2
    grads = wm.at[pl.ds(half, GROUPS)]
    k = Layer(
        x=v["x"], out=v["x"], g=v["g"], mask=v["mask"], time=time, norm=norm, wa=v["wa"], wm=wm.at[pl.ds(0, GROUPS)],
        ga=ga, gm_up=grads, gm_down=grads, small=v["sums"], gb=v["n2"],
        **{n: v[n] for n in LAYER_REFS[:-1]},
    )
    net = Links(Z, S, part)
    me = net.r * Z + net.z
    loc = v["loc"]
    own_a = pltpu.make_async_copy(sa, v["wa"].at[me], loc.at[4, 0])
    own_m = pltpu.make_async_copy(sm, wm.at[me], loc.at[4, 1])
    own_a.start()
    own_m.start()
    for i in range(8):
        k.small[i] = jnp.zeros(k.small.shape[1:], F32)
    net.barrier()
    own_a.wait()
    own_m.wait()

    def pair(name):
        return v[name].at[0], v[name].at[1]

    ra = net.gather(v["wa"], *pair("sem_a"))
    rm = net.gather(wm, *pair("sem_m"))
    ra.pop(0)()
    for step in range(1, Z):
        to = lax.rem(net.z + step, Z)
        rows = pl.ds(net.z * part, part)
        net.send(mask_in.at[to], k.mask.at[rows], v["sem_mask"].at[0, step], v["sem_mask"].at[1, step], (net.r, to))
    own_mask = pltpu.make_async_copy(mask_in.at[net.z], k.mask.at[pl.ds(net.z * part, part)], loc.at[4, 2])
    own_mask.start()
    net.exchange_in(resid, k.x, *pair("sem_in"), loc.at[0], range(S))
    rm.pop(0)()
    while ra:
        ra.pop(0)()
        if rm and len(rm) > 3:
            rm.pop(0)()
    own_mask.wait()
    for step in range(1, Z):
        source = lax.rem(net.z + Z - step, Z)
        net.arrived(k.mask.at[pl.ds(source * part, part)], v["sem_mask"].at[1, step])

    def pump(events, n=1):
        for _ in range(n):
            if events:
                events.pop(0)()

    net.exchange_in(cot, k.g, *pair("sem_cot"), loc.at[1], range(S))
    for s in range(S):
        net.exchange_in_done(resid, k.x, v["sem_in"].at[1], loc.at[0], s)
        k.embed(s)
        k.project(s)
        pump(rm)
        k.attend_sequence(s)
        pump(rm)
        k.outer(s)
        k.second_norm(s)
    pump(rm, len(rm))
    k.up()
    k.down()
    net.flush()
    for s in range(S):
        net.exchange_out(k.out, resid_out, *pair("sem_out"), loc.at[2], s)
    for s in range(S):
        net.exchange_in_done(cot, k.g, v["sem_cot"].at[1], loc.at[1], s)
    k.mask_cotangent()
    k.grad_pre()
    k.grad_down()
    total_m, total_a = k.mid.at[pl.ds(0, sm.shape[0])], k.mid.at[pl.ds(sm.shape[0], sa.shape[0])]
    m = net.scatter(wm, half, v["inbox"], *pair("sem_rm"), total_m)
    m["core_send"](2)
    m["core_send"](3)
    k.grad_up()
    m["core_send"](0)
    m["core_send"](1)
    m["core_add"](2)
    m["core_add"](3)
    k.grad_normed_two()
    m["core_add"](0)
    m["core_add"](1)
    m["first_send"]()
    k.norm_two_back()
    k.grad_outer()
    k.grad_attended()
    net.flush()
    for s in range(S):
        net.exchange_out_done(k.out, resid_out, v["sem_out"].at[1], loc.at[2], s)
    k.attend_back_sequence(0)
    m["second"]()
    k.grad_normed_one(0)
    k.norm_one_back(0)
    net.exchange_out(k.x, grad_in, *pair("sem_gin"), loc.at[3], 0)
    m["second_own"]()
    k.attend_back_sequence(1)
    k.grad_normed_one(1)
    k.norm_one_back(1)
    net.exchange_out(k.x, grad_in, *pair("sem_gin"), loc.at[3], 1)
    m["third"]()
    m["line"](3)
    k.attend_back_sequence(2)
    k.grad_normed_one(2)
    m["line"](2)
    k.norm_one_back(2)
    net.exchange_out(k.x, grad_in, *pair("sem_gin"), loc.at[3], 2)
    m["line"](1)
    k.grad_inner()
    for i in range(8):
        v["every"][me, i : i + 1, :] = jnp.sum(k.small[i], axis=0, keepdims=True)
    re = net.gather(v["every"], *pair("sem_e"))
    m["final"]()
    credit = v["credit"]
    mesh_id = pl.DeviceIdType.MESH
    for peer in (net.core, net.xn, net.yn):
        pl.semaphore_signal(credit, 1, device_id=(peer, net.z), device_id_type=mesh_id)
    pl.when(net.has_right)(
        lambda: pl.semaphore_signal(credit, 1, device_id=(net.r, net.z + 1), device_id_type=mesh_id)
    )
    pl.when(net.has_left)(
        lambda: pl.semaphore_signal(credit, 1, device_id=(net.r, net.z - 1), device_id_type=mesh_id)
    )
    pl.semaphore_wait(credit, 3 + jnp.where(net.has_right, 1, 0) + jnp.where(net.has_left, 1, 0))
    a = net.scatter(ga, 0, v["inbox"], *pair("sem_ra"), total_a)
    for c in range(4):
        a["core_send"](c)
    pump(re, 2)
    for c in range(4):
        a["core_add"](c)
    a["first_send"]()
    pump(re, 4)
    a["second"]()
    a["second_own"]()
    pump(re, 2)
    a["third"]()
    for i in (3, 2, 1):
        a["line"](i)
        pump(re, 1)
    pump(re, len(re))
    a["final"]()
    for s in range(S):
        net.exchange_out_done(k.x, grad_in, v["sem_gin"].at[1], loc.at[3], s)
    outs = [
        pltpu.make_async_copy(total_m, tm, loc.at[4, 0]),
        pltpu.make_async_copy(total_a, ta, loc.at[4, 1]),
        pltpu.make_async_copy(v["every"], every_out, loc.at[4, 2]),
    ]
    for copy in outs:
        copy.start()
    for copy in outs:
        copy.wait()
    net.flush()


def fast(
    resid_in,
    mask,
    steps_row,
    cotangent,
    attn_master,
    attn_first,
    attn_second,
    mlp_master,
    mlp_first,
    mlp_second,
    norm_master,
    norm_first,
    norm_second,
    time_master,
    time_first,
    time_second,
):
    D = resid_in.shape[2]
    Z = lax.axis_size("seq")
    R = lax.axis_size("rows")
    S = resid_in.shape[0] // Z
    part = resid_in.shape[1]
    L = part * Z
    T = S * L
    device = lax.axis_index("rows") * Z + lax.axis_index("seq")
    attn_low, mlp_low = attn_master.astype(BF), mlp_master.astype(BF)
    inner_shards = R * Z * 3 // 4
    is_inner, is_up = device < inner_shards, device < R * Z // 2
    sa = jnp.where(is_inner, rows_split(attn_low, 1, 3, D)[0], attn_low.reshape(-1, D))
    sm = jnp.where(is_up, rows_split(mlp_low, 1, FF // D, D)[0], mlp_low.reshape(-1, D))
    mask_in = mask.astype(BF).reshape(Z, S, part).transpose(0, 2, 1)
    mask_in = jnp.pad(mask_in, ((0, 0), (0, 0), (0, LANES - S)))
    steps_use = lax.dynamic_slice_in_dim(steps_row, lax.axis_index("seq") * S, S, 0)
    time_rows = pad_rows(jnp.take(time_master, steps_use, axis=0))
    V = pl.BlockSpec(memory_space=pltpu.VMEM)
    A = pl.BlockSpec(memory_space=pl.ANY)
    shape = jax.ShapeDtypeStruct
    sc = layer_scratch(T, D, S, L)
    dma = pltpu.SemaphoreType.DMA
    scratch = [
        pltpu.VMEM((GROUPS, *sa.shape), BF),
        pltpu.VMEM((GROUPS * 3 // 2, *sm.shape), BF),
        pltpu.VMEM((4 * Z + 6 * (Z // 2) + 2 * (Z - 1), *sm.shape), BF),
        pltpu.VMEM((T, D), BF),
        pltpu.VMEM((T, D), BF),
        pltpu.VMEM((L, LANES), BF),
        *(sc[n] for n in LAYER_REFS),
        pltpu.VMEM((R * Z, 8, D), F32),
        *(dma((2, 40)) for _ in range(3)),
        *(dma((2, S * (Z - 1))) for _ in range(4)),
        dma((2, Z)),
        dma((5, S)),
        *(dma((2, 16)) for _ in range(2)),
        pltpu.SemaphoreType.REGULAR,
    ]
    resid_out, grad_in, ta, tm, every = pl.pallas_call(
        functools.partial(whole_kernel, (Z, S, part)),
        out_shape=(
            shape(resid_in.shape, BF),
            shape(resid_in.shape, BF),
            shape(sa.shape, F32),
            shape(sm.shape, F32),
            shape((R * Z, 8, D), F32),
        ),
        in_specs=[A, A, A, V, V, A, A],
        out_specs=(A,) * 5,
        scratch_shapes=scratch,
        compiler_params=pltpu.CompilerParams(
            collective_id=0, has_side_effects=True, vmem_limit_bytes=63 << 20
        ),
    )(resid_in, cotangent, mask_in, time_rows, pad_rows(norm_master), sa, sm)
    attn_grad = jnp.where(is_inner, rows_join(ta[None], 3, D), ta.reshape(-1))
    mlp_grad = jnp.where(is_up, rows_join(tm[None], FF // D, D), tm.reshape(-1))
    return finish(
        resid_out,
        grad_in,
        lax.all_gather(steps_row, "rows", axis=0, tiled=True),
        every,
        adamw(attn_master, attn_first, attn_second, attn_grad, 0.05),
        adamw(mlp_master, mlp_first, mlp_second, mlp_grad, 0.03),
        (norm_master, norm_first, norm_second),
        (time_master, time_first, time_second),
        S,
    )


def solution(mesh):
    flat, whole, tokens = P(("rows", "seq")), P(), P("rows", "seq", None)
    fits = mesh.shape["rows"] * mesh.shape["seq"] == GROUPS and mesh.shape["rows"] == 8
    return jax.shard_map(
        fast if fits else general,
        mesh=mesh,
        in_specs=(tokens, P("rows", "seq"), P("rows"), tokens) + (flat,) * 6 + (whole,) * 6,
        out_specs=(tokens, tokens) + (flat,) * 8 + (whole,) * 6,
        check_vma=False,
    )
```

```python
import functools

import jax
import jax.numpy as jnp
from jax import lax
from jax.experimental import pallas as pl
from jax.experimental.pallas import tpu as pltpu
from jax.sharding import PartitionSpec as P

HEAD_DIM = 64
FF = 3072
STEP = 10
NORM_EPSILON = 1e-05
GROUPS = 32
LANES = 128
TILE = 256
ROW_BLOCK = 64
GELU_C = 0.7978845608028654
GELU_A = 0.044715
LOG2E = 1.4426950408889634
BF = jnp.bfloat16
F32 = jnp.float32

NN = (((1,), (0,)), ((), ()))
NT = (((1,), (1,)), ((), ()))
TN = (((0,), (0,)), ((), ()))


def dot(a, b, dims=NN):
    return lax.dot_general(a, b, dims, preferred_element_type=F32)


def norm_stats(h):
    mean = jnp.mean(h, axis=-1, keepdims=True)
    centred = h - mean
    var = jnp.mean(centred * centred, axis=-1, keepdims=True)
    rs = lax.rsqrt(var + NORM_EPSILON)
    return centred * rs, rs


def fold(x):
    return jnp.sum(x.reshape(x.shape[0] // 8, 8, x.shape[1]), axis=0)


def add_small(small, which, x):
    small[which] = small[which] + fold(x)


class Layer:
    def __init__(self, **refs):
        self.__dict__.update(refs)
        self.T, self.D = self.h.shape
        self.L = self.mask.shape[0]
        self.S = self.T // self.L
        self.PAIRS = self.D // LANES
        self.NJ = FF // self.D

    def qkv_part(self, ref, j, c, n):
        rows = ref.shape[1] // 3
        used = self.D // rows
        return ref.at[pl.ds(0, used), pl.ds(pl.multiple_of(j * rows, rows), rows), pl.ds(pl.multiple_of(c, n), n)]

    def out_part(self, ref, c, n):
        rows = ref.shape[1]
        used = self.D // rows
        return ref.at[pl.ds(ref.shape[0] - used, used), :, pl.ds(pl.multiple_of(c, n), n)]

    def up_part(self, ref, j, c, n):
        rows = ref.shape[1] // self.NJ
        used = self.D // rows
        return ref.at[pl.ds(0, used), pl.ds(pl.multiple_of(j * rows, rows), rows), pl.ds(pl.multiple_of(c, n), n)]

    def down_part(self, ref, j, c, n):
        rows = ref.shape[1]
        used = self.D // rows
        return ref.at[pl.ds(ref.shape[0] // 2 + j * used, used), :, pl.ds(pl.multiple_of(c, n), n)]

    def mask_col(self, s, base, n):
        return self.mask[pl.ds(base, n), s : s + 1].astype(F32)

    def embed(self, s):
        def body(i, _):
            base = pl.multiple_of(i * ROW_BLOCK, ROW_BLOCK)
            rows = pl.ds(pl.multiple_of(s * self.L + base, ROW_BLOCK), ROW_BLOCK)
            m = self.mask_col(s, base, ROW_BLOCK)
            h = self.x[rows, :].astype(F32) + m * self.norm[4:5, :] + self.time[s : s + 1, :]
            self.h[rows, :] = h
            xhat, _ = norm_stats(h)
            self.n1[rows, :] = (xhat * self.norm[0:1, :] + self.norm[1:2, :]).astype(BF)
            return 0

        lax.fori_loop(0, self.L // ROW_BLOCK, body, 0)

    def project(self, s):
        per = self.D // TILE
        rows = pl.ds(s * self.L, self.L)

        def body(i, _):
            j, c = lax.div(i, per), lax.rem(i, per) * TILE
            w = self.qkv_part(self.wa, j, c, TILE)[...].reshape(self.D, TILE)
            y = dot(self.n1[rows, :], w)
            self.qkv[rows, pl.ds(pl.multiple_of(i * TILE, TILE), TILE)] = y.astype(BF)
            return 0

        lax.fori_loop(0, 3 * per, body, 0)

    def pair_slices(self, s, p):
        rows = pl.ds(pl.multiple_of(s * self.L, self.L), self.L)
        cols = [pl.ds(pl.multiple_of(k * self.D + p * LANES, LANES), LANES) for k in range(3)]
        return rows, cols

    def half(self, x, hh):
        first = lax.broadcasted_iota(jnp.int32, x.shape, 1) < HEAD_DIM
        zero = jnp.zeros_like(x)
        return jnp.where(first, zero, x) if hh else jnp.where(first, x, zero)

    def attend(self, s, p):
        rows, cols = self.pair_slices(s, p)
        q, k, v = (self.qkv[rows, c] for c in cols)
        total = None
        for hh in range(2):
            sc = dot(self.half(q, hh), k, NT)
            top = jnp.max(sc, axis=-1, keepdims=True)
            e = jnp.exp2((sc - top) * (HEAD_DIM**-0.5 * LOG2E))
            w = (e * (1.0 / jnp.sum(e, axis=-1, keepdims=True))).astype(BF)
            self.soft[s * 2 * self.PAIRS + p * 2 + hh] = w
            o = dot(w, self.half(v, hh))
            total = o if total is None else total + o
        self.att[rows, cols[0]] = total.astype(BF)

    def attend_sequence(self, s):
        def body(p, _):
            self.attend(s, p)
            return 0

        lax.fori_loop(0, self.PAIRS, body, 0)

    def outer(self, s):
        rows = pl.ds(s * self.L, self.L)

        def body(i, _):
            c = i * TILE
            cols = pl.ds(pl.multiple_of(c, TILE), TILE)
            w = self.out_part(self.wa, c, TILE)[...].reshape(self.D, TILE)
            self.mid[rows, cols] = self.h[rows, cols] + dot(self.att[rows, :], w)
            return 0

        lax.fori_loop(0, self.D // TILE, body, 0)

    def second_norm(self, s):
        def body(i, _):
            rows = pl.ds(pl.multiple_of(s * self.L + i * ROW_BLOCK, ROW_BLOCK), ROW_BLOCK)
            xhat, _ = norm_stats(self.mid[rows, :])
            self.n2[rows, :] = (xhat * self.norm[2:3, :] + self.norm[3:4, :]).astype(BF)
            return 0

        lax.fori_loop(0, self.L // ROW_BLOCK, body, 0)

    def up(self):
        per = self.D // TILE

        def body(i, _):
            j, c = lax.div(i, per), lax.rem(i, per) * TILE
            cols = pl.ds(pl.multiple_of(i * TILE, TILE), TILE)
            w = self.up_part(self.wm, j, c, TILE)[...].reshape(self.D, TILE)
            for s in range(self.S):
                rows = pl.ds(s * self.L, self.L)
                u = dot(self.n2[rows, :], w)
                uu = u * u
                t = jnp.tanh(GELU_C * (u * (1.0 + GELU_A * uu)))
                left = 0.5 * (1.0 + t)
                self.act[pl.ds(pl.multiple_of(j * self.T + s * self.L, self.L), self.L), pl.ds(pl.multiple_of(c, TILE), TILE)] = (u * left).astype(BF)
                slope = left + (0.5 * GELU_C) * u * (1.0 - t * t) * (1.0 + 3.0 * GELU_A * uu)
                self.du[rows, cols] = slope.astype(BF)
            return 0

        lax.fori_loop(0, self.NJ * per, body, 0)

    def down(self):
        per = self.D // TILE

        def body(i, _):
            c = i * TILE
            cols = pl.ds(pl.multiple_of(c, TILE), TILE)
            for s in range(self.S):
                rows = pl.ds(s * self.L, self.L)
                total = self.mid[rows, cols]
                for j in range(self.NJ):
                    w = self.down_part(self.wm, j, c, TILE)[...].reshape(self.D, TILE)
                    total = total + dot(self.act[pl.ds(j * self.T + s * self.L, self.L), :], w)
                self.out[rows, cols] = total.astype(BF)
            return 0

        lax.fori_loop(0, per, body, 0)

    def mask_cotangent(self):
        for s in range(self.S):
            def body(i, _, s=s):
                base = pl.multiple_of(i * ROW_BLOCK, ROW_BLOCK)
                rows = pl.ds(pl.multiple_of(s * self.L + base, ROW_BLOCK), ROW_BLOCK)
                m = self.mask_col(s, base, ROW_BLOCK)
                self.g[rows, :] = (self.g[rows, :].astype(F32) * m).astype(BF)
                return 0

            lax.fori_loop(0, self.L // ROW_BLOCK, body, 0)

    def grad_pre(self):
        per = self.D // TILE

        def body(i, _):
            cols = pl.ds(pl.multiple_of(i * (self.D // 2), self.D // 2), self.D // 2)
            rows_w = self.wm.shape[1]
            used = self.D // 2 // rows_w
            w = self.wm[pl.ds(self.wm.shape[0] // 2 + i * used, used)].reshape(self.D // 2, self.D)
            for s in range(self.S):
                rows = pl.ds(s * self.L, self.L)
                d = dot(self.g[rows, :], w, NT)
                self.du[rows, cols] = (d * self.du[rows, cols].astype(F32)).astype(BF)
            return 0

        lax.fori_loop(0, 2 * self.NJ, body, 0)

    def turn_activated(self):
        for j in range(self.NJ):
            rows = pl.ds(j * self.T, self.T)
            self.turn[...] = self.act[rows, :].T
            self.act[rows, :] = self.turn[...]
        self.turn[...] = self.n2[...].T

    def grad_down(self, part, parts):
        group = self.gm_down.shape[1]
        used = self.D // group
        n = group // parts
        per = self.D // TILE

        def body(i, _):
            j, c = lax.div(i, per), pl.multiple_of(lax.rem(i, per) * TILE, TILE)
            a = jnp.concatenate(
                [
                    self.act[pl.ds(pl.multiple_of(j * self.D + u * group + part * n, 16), n), :]
                    for u in range(used)
                ]
            )
            y = dot(a, self.g[:, pl.ds(c, TILE)]).astype(BF)
            ref = self.gm_down.at[pl.ds(self.gm_down.shape[0] // 2 + j * used, used), pl.ds(part * n, n), pl.ds(c, TILE)]
            ref[...] = y.reshape(used, n, TILE)
            return 0

        lax.fori_loop(0, self.NJ * per, body, 0)

    def grad_up(self, part, parts):
        per = self.D // TILE
        n = self.NJ * per // parts

        def body(i, _):
            j, c = lax.div(i, per), lax.rem(i, per) * TILE
            y = dot(self.turn[...], self.du[:, pl.ds(pl.multiple_of(i * TILE, TILE), TILE)])
            ref = self.up_part(self.gm_up, j, c, TILE)
            ref[...] = y.astype(BF).reshape(ref.shape)
            return 0

        lax.fori_loop(part * n, (part + 1) * n, body, 0)

    def grad_normed_two(self):
        rows_w = self.wm.shape[1] // self.NJ
        n = self.D // 2
        used = n // rows_w

        def body(i, _):
            cols = pl.ds(pl.multiple_of(i * n, n), n)
            for s in range(self.S):
                rows = pl.ds(s * self.L, self.L)
                total = None
                for j in range(self.NJ):
                    w = self.wm[pl.ds(i * used, used), pl.ds(j * rows_w, rows_w), :].reshape(n, self.D)
                    y = dot(self.du[rows, pl.ds(j * self.D, self.D)], w, NT)
                    total = y if total is None else total + y
                self.dn[rows, cols] = total
            return 0

        lax.fori_loop(0, 2, body, 0)

    def norm_two_back(self):
        def body(i, _):
            rows = pl.ds(pl.multiple_of(i * ROW_BLOCK, ROW_BLOCK), ROW_BLOCK)
            xhat, rs = norm_stats(self.mid[rows, :])
            dy = self.dn[rows, :]
            add_small(self.small, 5, dy * xhat)
            add_small(self.small, 6, dy)
            e = dy * self.norm[2:3, :]
            back = (e - jnp.mean(e, -1, keepdims=True) - xhat * jnp.mean(e * xhat, -1, keepdims=True)) * rs
            gm = self.g[rows, :].astype(F32) + back
            self.dn[rows, :] = gm
            self.gb[rows, :] = gm.astype(BF)
            return 0

        lax.fori_loop(0, self.T // ROW_BLOCK, body, 0)

    def grad_outer(self):
        self.turn[...] = self.att[...].T

        def body(i, _):
            c = pl.multiple_of(i * TILE, TILE)
            y = dot(self.turn[...], self.gb[:, pl.ds(c, TILE)])
            ref = self.out_part(self.ga, c, TILE)
            ref[...] = y.astype(BF).reshape(ref.shape)
            return 0

        lax.fori_loop(0, self.D // TILE, body, 0)

    def grad_attended(self):
        n = self.D // 2
        rows_w = self.wa.shape[1]
        used = n // rows_w
        first = self.wa.shape[0] - 2 * used

        def body(i, _):
            w = self.wa[pl.ds(first + i * used, used)].reshape(n, self.D)
            for s in range(self.S):
                rows = pl.ds(s * self.L, self.L)
                self.att[rows, pl.ds(pl.multiple_of(i * n, n), n)] = dot(self.gb[rows, :], w, NT).astype(BF)
            return 0

        lax.fori_loop(0, 2, body, 0)

    def attend_back(self, s, p):
        rows, cols = self.pair_slices(s, p)
        q, k, v = (self.qkv[rows, c] for c in cols)
        da = self.att[rows, cols[0]]
        dq = dk = dv = None
        for hh in range(2):
            w = self.soft[s * 2 * self.PAIRS + p * 2 + hh]
            da_h = self.half(da, hh)
            dp = dot(da_h, v, NT)
            wf = w.astype(F32)
            t = wf * dp
            ds = (t - wf * jnp.sum(t, axis=-1, keepdims=True)).astype(BF)
            parts = (dot(ds, self.half(k, hh)), dot(ds, self.half(q, hh), TN), dot(w, da_h, TN))
            dq, dk, dv = parts if dq is None else (dq + parts[0], dk + parts[1], dv + parts[2])
        scale = HEAD_DIM**-0.5
        self.qkv[rows, cols[0]] = (dq * scale).astype(BF)
        self.qkv[rows, cols[1]] = (dk * scale).astype(BF)
        self.qkv[rows, cols[2]] = dv.astype(BF)

    def attend_back_sequence(self, s):
        def body(p, _):
            self.attend_back(s, p)
            return 0

        lax.fori_loop(0, self.PAIRS, body, 0)

    def grad_normed_one(self, s):
        n = self.D // 3
        rows_w = self.wa.shape[1] // 3
        used = n // rows_w
        rows = pl.ds(s * self.L, self.L)

        def body(i, _):
            total = None
            for j in range(3):
                w = self.wa[pl.ds(i * used, used), pl.ds(j * rows_w, rows_w), :].reshape(n, self.D)
                y = dot(self.qkv[rows, pl.ds(j * self.D, self.D)], w, NT)
                total = y if total is None else total + y
            self.mid[rows, pl.ds(pl.multiple_of(i * n, n), n)] = total
            return 0

        lax.fori_loop(0, 3, body, 0)

    def norm_one_back(self, s):
        def body(i, _):
            base = pl.multiple_of(i * ROW_BLOCK, ROW_BLOCK)
            rows = pl.ds(pl.multiple_of(s * self.L + base, ROW_BLOCK), ROW_BLOCK)
            xhat, rs = norm_stats(self.h[rows, :])
            dy = self.mid[rows, :]
            add_small(self.small, 3, dy * xhat)
            add_small(self.small, 4, dy)
            e = dy * self.norm[0:1, :]
            back = (e - jnp.mean(e, -1, keepdims=True) - xhat * jnp.mean(e * xhat, -1, keepdims=True)) * rs
            gs = self.dn[rows, :] + back
            add_small(self.small, s, gs)
            add_small(self.small, 7, gs * self.mask_col(s, base, ROW_BLOCK))
            self.x[rows, :] = gs.astype(BF)
            return 0

        lax.fori_loop(0, self.L // ROW_BLOCK, body, 0)

    def grad_inner(self):
        per = self.D // TILE
        self.turn[...] = self.n1[...].T

        def body(i, _):
            j, c = lax.div(i, per), lax.rem(i, per) * TILE
            y = dot(self.turn[...], self.qkv[:, pl.ds(pl.multiple_of(i * TILE, TILE), TILE)])
            ref = self.qkv_part(self.ga, j, c, TILE)
            ref[...] = y.astype(BF).reshape(ref.shape)
            return 0

        lax.fori_loop(0, 3 * per, body, 0)


def run_all(k):
    for i in range(8):
        k.small[i] = jnp.zeros(k.small.shape[1:], F32)
    for s in range(k.S):
        k.embed(s)
        k.project(s)
        k.attend_sequence(s)
        k.outer(s)
        k.second_norm(s)
    k.up()
    k.down()
    k.mask_cotangent()
    k.grad_pre()
    k.turn_activated()
    k.grad_down(0, 1)
    k.grad_up(0, 1)
    k.grad_normed_two()
    k.norm_two_back()
    k.grad_outer()
    k.grad_attended()
    for s in range(k.S):
        k.attend_back_sequence(s)
        k.grad_normed_one(s)
        k.norm_one_back(s)
    k.grad_inner()


def flip(index, bit):
    return index + bit - 2 * bit * lax.rem(lax.div(index, bit), 2)


def pick(table, index):
    value = table[0]
    for i in range(1, len(table)):
        value = jnp.where(index == i, table[i], value)
    return value


class Links:
    def __init__(self, Z, S, part):
        self.Z, self.S, self.part = Z, S, part
        self.r, self.z = lax.axis_index("rows"), lax.axis_index("seq")
        r = self.r
        self.core, self.xn, self.yn = flip(r, 1), flip(r, 2), flip(r, 4)
        self.diag = flip(self.xn, 4)
        self.pending = []
        near, far = flip(self.z, 1), flip(self.z, 2)
        self.near, self.far = near, far
        self.order = [self.z, near, far, flip(near, 2)]

    def barrier(self):
        bar = pltpu.get_barrier_semaphore()
        peers = [(self.core, self.z), (self.xn, self.z), (self.yn, self.z)]
        peers += [(self.r, lax.rem(self.z + i, self.Z)) for i in range(1, self.Z)]
        for peer in peers:
            pl.semaphore_signal(bar, 1, device_id=peer, device_id_type=pl.DeviceIdType.MESH)
        pl.semaphore_wait(bar, len(peers))

    def send(self, src, dst, ss, rs, peer, cond=None, owner=None):
        copy = pltpu.make_async_remote_copy(
            src, dst, ss, rs, device_id=peer, device_id_type=pl.DeviceIdType.MESH
        )
        if cond is None:
            copy.start()
        else:
            pl.when(cond)(copy.start)
        self.pending.append((owner, cond, copy))

    def arrived(self, dst, rs, cond=None):
        copy = pltpu.make_async_remote_copy(
            dst, dst, rs, rs, device_id=(self.core, self.z), device_id_type=pl.DeviceIdType.MESH
        )
        if cond is None:
            copy.wait_recv()
        else:
            pl.when(cond)(copy.wait_recv)

    def flush(self, src=None):
        left = []
        for item in self.pending:
            owner, cond, copy = item
            if src is not None and owner is not src:
                left.append(item)
            elif cond is None:
                copy.wait_send()
            else:
                pl.when(cond)(copy.wait_send)
        self.pending = left

    def gather(self, w, ss, rs):
        Z, z = self.Z, self.z
        count = [0]

        def go(row, zz, peer, cond=None):
            i = row * Z + zz
            self.send(w.at[i], w.at[i], ss.at[count[0]], rs.at[i], peer, cond, w)
            count[0] += 1

        def got(row, zz):
            i = row * Z + zz
            self.arrived(w.at[i], rs.at[i])

        def own(i):
            zz = self.order[i]
            if i:
                got(self.r, zz)
            if i == 0:
                go(self.r, zz, (self.r, self.far))
            if i == 0 or i == 2:
                go(self.r, zz, (self.r, self.near))
            go(self.r, zz, (self.xn, z))
            go(self.r, zz, (self.yn, z))
            go(self.r, zz, (self.core, z))

        def side(i):
            zz = self.order[i]
            got(self.xn, zz)
            go(self.xn, zz, (self.yn, z), zz < Z // 2)
            got(self.yn, zz)
            go(self.yn, zz, (self.xn, z), zz >= Z // 2)
            go(self.xn, zz, (self.core, z))
            go(self.yn, zz, (self.core, z))

        def far(i):
            zz = self.order[i]
            got(self.diag, zz)
            go(self.diag, zz, (self.core, z))

        def last():
            for row in (self.r, self.xn, self.yn, self.diag):
                for i in range(Z):
                    got(flip(row, 1), self.order[i])

        return own, side, far, last

    def exchange_in(self, src, dst, ss, rs, local, seqs):
        L = self.part * self.Z
        for i in seqs:
            for step in range(1, self.Z):
                to = lax.rem(self.z + step, self.Z)
                rows = pl.ds(i * L + self.z * self.part, self.part)
                n = i * (self.Z - 1) + step - 1
                self.send(src.at[to * self.S + i], dst.at[rows], ss.at[n], rs.at[n], (self.r, to))
            rows = pl.ds(i * L + self.z * self.part, self.part)
            pltpu.make_async_copy(src.at[self.z * self.S + i], dst.at[rows], local.at[i]).start()

    def exchange_in_done(self, src, dst, rs, local, i):
        L = self.part * self.Z
        for step in range(1, self.Z):
            source = lax.rem(self.z + self.Z - step, self.Z)
            rows = pl.ds(i * L + source * self.part, self.part)
            self.arrived(dst.at[rows], rs.at[i * (self.Z - 1) + step - 1])
        rows = pl.ds(i * L + self.z * self.part, self.part)
        pltpu.make_async_copy(src.at[self.z * self.S + i], dst.at[rows], local.at[i]).wait()

    def exchange_out(self, src, dst, ss, rs, local, i):
        L = self.part * self.Z
        for step in range(1, self.Z):
            to = lax.rem(self.z + step, self.Z)
            rows = pl.ds(i * L + to * self.part, self.part)
            n = i * (self.Z - 1) + step - 1
            self.send(src.at[rows], dst.at[self.z * self.S + i], ss.at[n], rs.at[n], (self.r, to), None, dst)
        rows = pl.ds(i * L + self.z * self.part, self.part)
        pltpu.make_async_copy(src.at[rows], dst.at[self.z * self.S + i], local.at[i]).start()

    def exchange_out_done(self, src, dst, rs, local, i):
        L = self.part * self.Z
        for step in range(1, self.Z):
            source = lax.rem(self.z + self.Z - step, self.Z)
            self.arrived(dst.at[source * self.S + i], rs.at[i * (self.Z - 1) + step - 1])
        rows = pl.ds(i * L + self.z * self.part, self.part)
        pltpu.make_async_copy(src.at[rows], dst.at[self.z * self.S + i], local.at[i]).wait()

    def scatter(self, g, base, part, inbox, box0, ss, rs, total):
        Z, z = self.Z, self.z
        half = Z // 2
        chip = lax.div(self.r, 2)
        k = lax.rem(self.r, 2)
        cx, cy = flip(chip, 1), flip(chip, 2)
        cd = flip(cx, 2)
        rows = total.shape[0]

        def block(c, parity, lo, n):
            return g.at[pl.ds(base + (2 * c + parity) * Z + lo, n), pl.ds(part * rows, rows)]

        def inslot(i, n):
            return inbox.at[pl.ds(box0 + i, n)]

        def add(dst, src, n):
            def body(i, _):
                dst[i] = (dst[i].astype(F32) + src[i].astype(F32)).astype(BF)
                return 0

            lax.fori_loop(0, n, body, 0)

        XY = 4 * Z
        ZB = XY + 6 * half

        def core_send_all():
            for c in range(4):
                core_send(c)

        def core_send(c):
            self.send(block(c, 1 - k, 0, Z), inslot(c * Z, Z), ss.at[c], rs.at[c], (self.core, z))

        def core_add(c):
            self.arrived(inslot(c * Z, Z), rs.at[c])
            add(block(c, k, 0, Z), inslot(c * Z, Z), Z)

        def xy_send(slot, c, lo, peer):
            i = XY + slot * half
            self.send(block(c, k, lo, half), inslot(i, half), ss.at[4 + slot], rs.at[4 + slot], (peer, z))

        def xy_add(slot, c, lo):
            i = XY + slot * half
            self.arrived(inslot(i, half), rs.at[4 + slot])
            add(block(c, k, lo, half), inslot(i, half), half)

        def first():
            core_add(cd)
            xy_send(0, cd, 0, self.xn)
            xy_send(2, cd, half, self.yn)
            core_add(cx)
            xy_send(1, cx, 0, self.xn)
            core_add(cy)
            xy_send(3, cy, half, self.yn)
            core_add(chip)

        def second():
            xy_add(0, cy, 0)
            xy_send(4, cy, 0, self.yn)
            xy_add(2, cx, half)
            xy_send(5, cx, half, self.xn)

        def second_own():
            xy_add(1, chip, 0)
            xy_add(3, chip, half)

        def third():
            xy_add(4, chip, 0)
            xy_add(5, chip, half)

        def z_send(slot, target, peer):
            box = inslot(ZB + slot, 1)
            self.send(block(chip, k, target, 1), box, ss.at[10 + slot], rs.at[10 + slot], (self.r, peer))

        def z_first():
            z_send(1, self.order[3], self.near)
            z_send(0, self.near, self.near)

        def z_second():
            self.arrived(inslot(ZB + 1, 1), rs.at[11])
            add(block(chip, k, self.far, 1), inslot(ZB + 1, 1), 1)
            z_send(2, self.far, self.far)

        def final():
            self.arrived(inslot(ZB, 1), rs.at[10])
            total[...] = block(chip, k, z, 1)[0].astype(F32) + inbox[box0 + ZB].astype(F32)
            self.arrived(inslot(ZB + 2, 1), rs.at[12])
            total[...] += inbox[box0 + ZB + 2].astype(F32)

        return core_send_all, first, second, second_own, third, z_first, z_second, final


def compute_kernel(x, mask, g_in, time, norm, wa, wm, out, gin, ga, gm, small, *scratch):
    names = ("g", "h", "n1", "qkv", "att", "mid", "n2", "act", "du", "soft", "dn", "gb", "turn", "sums")
    refs = dict(zip(names, scratch))
    sums = refs.pop("sums")
    pltpu.sync_copy(x, gin)
    pltpu.sync_copy(g_in, refs["g"])
    layer = Layer(
        x=gin, mask=mask, time=time, norm=norm, wa=wa, wm=wm, out=out, ga=ga, gm_down=gm, gm_up=gm, small=sums, **refs
    )
    run_all(layer)
    for i in range(8):
        small[i : i + 1, :] = jnp.sum(sums[i], axis=0, keepdims=True)


def layer_scratch(T, D, S, L):
    heads = D // HEAD_DIM
    return dict(
        h=pltpu.VMEM((T, D), F32),
        n1=pltpu.VMEM((T, D), BF),
        qkv=pltpu.VMEM((T, 3 * D), BF),
        att=pltpu.VMEM((T, D), BF),
        mid=pltpu.VMEM((T, D), F32),
        n2=pltpu.VMEM((T, D), BF),
        act=pltpu.VMEM((FF // D * T, D), BF),
        du=pltpu.VMEM((T, FF), BF),
        soft=pltpu.VMEM((S * heads, L, L), BF),
        dn=pltpu.VMEM((T, D), F32),
        gb=pltpu.VMEM((T, D), BF),
        turn=pltpu.VMEM((D, D), BF),
        sums=pltpu.VMEM((8, 8, D), F32),
    )


def pad_rows(x):
    return jnp.pad(x, ((0, 8 - x.shape[0]), (0, 0)))


def rows_split(flat, groups, parts, D):
    return flat.reshape(groups, -1, parts, D).transpose(0, 2, 1, 3).reshape(groups, -1, D)


def rows_join(block, parts, D):
    groups = block.shape[0]
    return block.reshape(groups, parts, -1, D).transpose(0, 2, 1, 3).reshape(-1)


def adamw(master, moment_one, moment_two, gradient, step_rate):
    first_new = 0.5 * moment_one + 0.5 * gradient
    second_new = 0.5 * moment_two + 0.5 * gradient * gradient
    correct = 1.0 - 0.5**STEP
    update = first_new / correct / (jnp.sqrt(second_new / correct) + 1e-08)
    return (master - step_rate * (update + 0.1 * master), first_new, second_new)


def general(
    resid_in,
    mask,
    steps_row,
    cotangent,
    attn_master,
    attn_first,
    attn_second,
    mlp_master,
    mlp_first,
    mlp_second,
    norm_master,
    norm_first,
    norm_second,
    time_master,
    time_first,
    time_second,
):
    D = resid_in.shape[2]
    axes = ("rows", "seq")
    seq_count = lax.axis_size("seq")
    S = resid_in.shape[0] // seq_count
    L = resid_in.shape[1] * seq_count
    T = S * L
    attn_full = lax.all_gather(attn_master.astype(BF), axes, axis=0, tiled=True)
    mlp_full = lax.all_gather(mlp_master.astype(BF), axes, axis=0, tiled=True)
    inner = 3 * D * D
    wide = D * FF
    wa = jnp.concatenate(
        (rows_split(attn_full[:inner], 24, 3, D), attn_full[inner:].reshape(8, -1, D))
    )
    wm = jnp.concatenate((rows_split(mlp_full[:wide], 16, FF // D, D), mlp_full[wide:].reshape(16, -1, D)))
    exchange = functools.partial(lax.all_to_all, axis_name="seq", split_axis=0, concat_axis=1, tiled=True)
    x = exchange(resid_in).reshape(T, D)
    g = exchange(cotangent).reshape(T, D)
    mask_t = jnp.pad(exchange(mask.astype(BF)).T, ((0, 0), (0, LANES - S)))
    steps_use = lax.dynamic_slice_in_dim(steps_row, lax.axis_index("seq") * S, S, 0)
    time_rows = pad_rows(jnp.take(time_master, steps_use, axis=0))
    V = pl.BlockSpec(memory_space=pltpu.VMEM)
    A = pl.BlockSpec(memory_space=pl.ANY)
    shape = jax.ShapeDtypeStruct
    scratch = layer_scratch(T, D, S, L)
    out, gin, ga, gm, small = pl.pallas_call(
        compute_kernel,
        out_shape=(shape((T, D), BF), shape((T, D), BF), shape(wa.shape, BF), shape(wm.shape, BF), shape((8, D), F32)),
        in_specs=[A, V, A, V, V, V, V],
        out_specs=(V,) * 5,
        scratch_shapes=[pltpu.VMEM((T, D), BF)] + list(scratch.values()),
        compiler_params=pltpu.CompilerParams(vmem_limit_bytes=62 << 20),
    )(x, mask_t, g, time_rows, pad_rows(norm_master), wa, wm)
    attn_flat = jnp.concatenate((rows_join(ga[:24], 3, D), ga[24:].reshape(-1))).astype(F32)
    mlp_flat = jnp.concatenate((rows_join(gm[:16], FF // D, D), gm[16:].reshape(-1))).astype(F32)
    attn_grad = lax.psum_scatter(attn_flat, axes, scatter_dimension=0, tiled=True)
    mlp_grad = lax.psum_scatter(mlp_flat, axes, scatter_dimension=0, tiled=True)
    every = lax.all_gather(small, axes, axis=0)
    spread = functools.partial(lax.all_to_all, axis_name="seq", split_axis=1, concat_axis=0, tiled=True)
    return finish(
        spread(out.reshape(S, L, D)),
        spread(gin.reshape(S, L, D)),
        lax.all_gather(steps_row, "rows", axis=0, tiled=True),
        every,
        adamw(attn_master, attn_first, attn_second, attn_grad, 0.05),
        adamw(mlp_master, mlp_first, mlp_second, mlp_grad, 0.03),
        (norm_master, norm_first, norm_second),
        (time_master, time_first, time_second),
        S,
    )


def finish(resid_out, grad_in, steps, every, attn, mlp, norm, time, S):
    D = every.shape[2]
    norm_grad = jnp.sum(every[:, 3:8], axis=0)
    chosen = (jnp.arange(time[0].shape[0], dtype=jnp.int32)[:, None] == steps[None, :]).astype(F32)
    time_grad = jnp.dot(chosen, every[:, :S].reshape(-1, D), precision=lax.Precision.HIGHEST)
    return (
        resid_out,
        grad_in,
        *attn,
        attn[0].astype(BF),
        *mlp,
        mlp[0].astype(BF),
        *adamw(*norm, norm_grad, 0.2),
        *adamw(*time, time_grad, 0.3),
    )


LAYER_REFS = ("h", "n1", "qkv", "att", "mid", "n2", "act", "du", "soft", "dn", "turn", "sums")


def whole_kernel(
    cfg, resid, cot, mask_in, time, norm, sa, sm, resid_out, grad_in, ta, tm, every_out, *scratch
):
    Z, S, part = cfg
    names = (
        "wa", "wm", "inbox", "x", "g", "mask", "h", "n1",
        "qkv", "att", "mid", "n2", "act", "du", "soft", "dn",
        "turn", "sums", "every", "sem_a", "sem_m", "sem_e", "sem_in", "sem_cot",
        "sem_out", "sem_gin", "sem_mask", "loc", "sem_ra", "sem_rm", "credit", "total",
    )
    v = dict(zip(names, scratch))
    wm, ga = v["wm"], v["act"].reshape(GROUPS, v["wa"].shape[1], v["wa"].shape[2])
    half = GROUPS // 2
    grads = wm.at[pl.ds(half, GROUPS)]
    k = Layer(
        x=v["x"], out=v["x"], g=v["g"], mask=v["mask"], time=time, norm=norm, wa=v["wa"], wm=wm.at[pl.ds(0, GROUPS)],
        ga=ga, gm_up=grads, gm_down=grads, small=v["sums"], gb=v["n2"],
        **{n: v[n] for n in LAYER_REFS[:-1]},
    )
    net = Links(Z, S, part)
    me = net.r * Z + net.z
    loc = v["loc"]
    own_a = pltpu.make_async_copy(sa, v["wa"].at[me], loc.at[4, 0])
    own_m = pltpu.make_async_copy(sm, wm.at[me], loc.at[4, 1])
    own_a.start()
    own_m.start()
    for i in range(8):
        k.small[i] = jnp.zeros(k.small.shape[1:], F32)
    net.barrier()
    own_a.wait()
    own_m.wait()

    def pair(name):
        return v[name].at[0], v[name].at[1]

    def pump(events, n=1):
        for _ in range(n):
            if events:
                events.pop(0)()

    a_own, a_side, a_far, a_last = net.gather(v["wa"], *pair("sem_a"))
    m_own, m_side, m_far, m_last = net.gather(wm, *pair("sem_m"))

    def stream(s):
        net.exchange_in(resid, k.x, *pair("sem_in"), loc.at[0], [s])

    a_own(0)
    m_own(0)
    for step in range(1, Z):
        to = lax.rem(net.z + step, Z)
        rows = pl.ds(net.z * part, part)
        net.send(mask_in.at[to], k.mask.at[rows], v["sem_mask"].at[0, step], v["sem_mask"].at[1, step], (net.r, to))
    own_mask = pltpu.make_async_copy(mask_in.at[net.z], k.mask.at[pl.ds(net.z * part, part)], loc.at[4, 2])
    own_mask.start()
    a_own(1)
    a_side(0)
    m_own(1)
    stream(0)
    m_side(0)
    a_own(2)
    a_side(1)
    a_far(0)
    m_own(2)
    stream(1)
    m_side(1)
    m_far(0)
    a_own(3)
    a_side(2)
    a_far(1)
    m_own(3)
    stream(2)
    net.exchange_in(cot, k.g, *pair("sem_cot"), loc.at[1], range(S))
    a_side(3)
    a_far(2)
    a_far(3)
    a_last()
    rm = [functools.partial(m_side, 2), functools.partial(m_far, 1), functools.partial(m_side, 3), functools.partial(m_far, 2), functools.partial(m_far, 3), m_last]
    own_mask.wait()
    for step in range(1, Z):
        source = lax.rem(net.z + Z - step, Z)
        net.arrived(k.mask.at[pl.ds(source * part, part)], v["sem_mask"].at[1, step])

    for s in range(S):
        net.exchange_in_done(resid, k.x, v["sem_in"].at[1], loc.at[0], s)
        k.embed(s)
        k.project(s)
        pump(rm)
        k.attend_sequence(s)
        pump(rm)
        k.outer(s)
        k.second_norm(s)
    pump(rm, len(rm))
    k.up()
    k.down()
    for s in range(S):
        net.exchange_out(k.out, resid_out, *pair("sem_out"), loc.at[2], s)
    for s in range(S):
        net.exchange_in_done(cot, k.g, v["sem_cot"].at[1], loc.at[1], s)
    k.mask_cotangent()
    k.grad_pre()
    net.flush(wm)
    k.turn_activated()
    rows = sa.shape[0]
    parts = sm.shape[0] // rows
    boxes = v["inbox"].shape[0] // parts
    totals = [v["total"].at[pl.ds(p * rows, rows)] for p in range(parts + 1)]
    pieces = [
        net.scatter(wm, half, p, v["inbox"], p * boxes, v["sem_rm"].at[0, p], v["sem_rm"].at[1, p], totals[p])
        for p in range(parts)
    ]
    (p_core, p_first, p_second, p_own, p_third, p_z, p_zz, p_final) = pieces[0]
    (q_core, q_first, q_second, q_own, q_third, q_z, q_zz, q_final) = pieces[1]
    k.grad_down(0, parts)
    k.grad_up(0, parts)
    p_core()
    k.grad_down(1, parts)
    p_first()
    k.grad_up(1, parts)
    q_core()
    k.grad_normed_two()
    q_first()
    k.norm_two_back()
    k.grad_outer()
    k.grad_attended()
    net.flush(resid_out)
    for s in range(S):
        net.exchange_out_done(k.out, resid_out, v["sem_out"].at[1], loc.at[2], s)
    k.attend_back_sequence(0)
    p_second()
    k.attend_back_sequence(1)
    p_own()
    q_second()
    k.attend_back_sequence(2)
    p_third()
    p_z()
    k.grad_inner()
    q_own()
    q_third()
    q_z()
    p_zz()
    k.grad_normed_one(0)
    k.norm_one_back(0)
    net.exchange_out(k.x, grad_in, *pair("sem_gin"), loc.at[3], 0)
    q_zz()
    p_final()
    credit = v["credit"]
    mesh_id = pl.DeviceIdType.MESH
    peers = ((net.core, net.z), (net.xn, net.z), (net.yn, net.z), (net.r, net.near), (net.r, net.far))
    for peer in peers:
        pl.semaphore_signal(credit, 1, device_id=peer, device_id_type=mesh_id)
    k.grad_normed_one(1)
    pl.semaphore_wait(credit, len(peers))
    (a_core, a_first, a_second, a_own, a_third, a_z, a_zz, a_final) = net.scatter(
        ga, 0, 0, v["inbox"], 0, *pair("sem_ra"), totals[parts]
    )
    a_core()
    k.norm_one_back(1)
    net.exchange_out(k.x, grad_in, *pair("sem_gin"), loc.at[3], 1)
    a_first()
    k.grad_normed_one(2)
    k.norm_one_back(2)
    net.exchange_out(k.x, grad_in, *pair("sem_gin"), loc.at[3], 2)
    for i in range(8):
        v["every"][me, i : i + 1, :] = jnp.sum(k.small[i], axis=0, keepdims=True)
    e_own, e_side, e_far, e_last = net.gather(v["every"], *pair("sem_e"))
    re = [functools.partial(e_own, 0), functools.partial(e_own, 1)]
    for i in range(Z):
        if i + 2 < Z:
            re.append(functools.partial(e_own, i + 2))
        re.append(functools.partial(e_side, i))
        if i:
            re.append(functools.partial(e_far, i - 1))
    re += [functools.partial(e_far, Z - 1), e_last]
    pump(re, 4)
    q_final()
    a_second()
    a_own()
    pump(re, 3)
    a_third()
    a_z()
    pump(re, 1)
    a_zz()
    pump(re, len(re))
    a_final()
    for s in range(S):
        net.exchange_out_done(k.x, grad_in, v["sem_gin"].at[1], loc.at[3], s)
    outs = [pltpu.make_async_copy(totals[parts], ta, loc.at[4, 0])]
    outs += [pltpu.make_async_copy(totals[p], tm.at[pl.ds(p * rows, rows)], loc.at[0, p]) for p in range(parts)]
    outs.append(pltpu.make_async_copy(v["every"], every_out, loc.at[4, 2]))
    for copy in outs:
        copy.start()
    for copy in outs:
        copy.wait()
    net.flush()


def fast(
    resid_in,
    mask,
    steps_row,
    cotangent,
    attn_master,
    attn_first,
    attn_second,
    mlp_master,
    mlp_first,
    mlp_second,
    norm_master,
    norm_first,
    norm_second,
    time_master,
    time_first,
    time_second,
):
    D = resid_in.shape[2]
    Z = lax.axis_size("seq")
    R = lax.axis_size("rows")
    S = resid_in.shape[0] // Z
    part = resid_in.shape[1]
    L = part * Z
    T = S * L
    device = lax.axis_index("rows") * Z + lax.axis_index("seq")
    attn_low, mlp_low = attn_master.astype(BF), mlp_master.astype(BF)
    inner_shards = R * Z * 3 // 4
    is_inner, is_up = device < inner_shards, device < R * Z // 2
    sa = jnp.where(is_inner, rows_split(attn_low, 1, 3, D)[0], attn_low.reshape(-1, D))
    sm = jnp.where(is_up, rows_split(mlp_low, 1, FF // D, D)[0], mlp_low.reshape(-1, D))
    mask_in = mask.astype(BF).reshape(Z, S, part).transpose(0, 2, 1)
    mask_in = jnp.pad(mask_in, ((0, 0), (0, 0), (0, LANES - S)))
    steps_use = lax.dynamic_slice_in_dim(steps_row, lax.axis_index("seq") * S, S, 0)
    time_rows = pad_rows(jnp.take(time_master, steps_use, axis=0))
    V = pl.BlockSpec(memory_space=pltpu.VMEM)
    A = pl.BlockSpec(memory_space=pl.ANY)
    shape = jax.ShapeDtypeStruct
    sc = layer_scratch(T, D, S, L)
    dma = pltpu.SemaphoreType.DMA
    scratch = [
        pltpu.VMEM((GROUPS, *sa.shape), BF),
        pltpu.VMEM((GROUPS * 3 // 2, *sm.shape), BF),
        pltpu.VMEM((sm.shape[0] // sa.shape[0] * (4 * Z + 6 * (Z // 2) + Z - 1), *sa.shape), BF),
        pltpu.VMEM((T, D), BF),
        pltpu.VMEM((T, D), BF),
        pltpu.VMEM((L, LANES), BF),
        *(sc[n] for n in LAYER_REFS),
        pltpu.VMEM((R * Z, 8, D), F32),
        *(dma((2, 40)) for _ in range(3)),
        *(dma((2, S * (Z - 1))) for _ in range(4)),
        dma((2, Z)),
        dma((5, S)),
        dma((2, 16)),
        dma((2, sm.shape[0] // sa.shape[0], 16)),
        pltpu.SemaphoreType.REGULAR,
        pltpu.VMEM((sa.shape[0] + sm.shape[0], D), F32),
    ]
    resid_out, grad_in, ta, tm, every = pl.pallas_call(
        functools.partial(whole_kernel, (Z, S, part)),
        out_shape=(
            shape(resid_in.shape, BF),
            shape(resid_in.shape, BF),
            shape(sa.shape, F32),
            shape(sm.shape, F32),
            shape((R * Z, 8, D), F32),
        ),
        in_specs=[A, A, A, V, V, A, A],
        out_specs=(A,) * 5,
        scratch_shapes=scratch,
        compiler_params=pltpu.CompilerParams(
            collective_id=0, has_side_effects=True, vmem_limit_bytes=63 << 20
        ),
    )(resid_in, cotangent, mask_in, time_rows, pad_rows(norm_master), sa, sm)
    attn_grad = jnp.where(is_inner, rows_join(ta[None], 3, D), ta.reshape(-1))
    mlp_grad = jnp.where(is_up, rows_join(tm[None], FF // D, D), tm.reshape(-1))
    return finish(
        resid_out,
        grad_in,
        lax.all_gather(steps_row, "rows", axis=0, tiled=True),
        every,
        adamw(attn_master, attn_first, attn_second, attn_grad, 0.05),
        adamw(mlp_master, mlp_first, mlp_second, mlp_grad, 0.03),
        (norm_master, norm_first, norm_second),
        (time_master, time_first, time_second),
        S,
    )


def solution(mesh):
    flat, whole, tokens = P(("rows", "seq")), P(), P("rows", "seq", None)
    fits = mesh.shape["rows"] * mesh.shape["seq"] == GROUPS and mesh.shape["rows"] == 8
    return jax.shard_map(
        fast if fits else general,
        mesh=mesh,
        in_specs=(tokens, P("rows", "seq"), P("rows"), tokens) + (flat,) * 6 + (whole,) * 6,
        out_specs=(tokens, tokens) + (flat,) * 8 + (whole,) * 6,
        check_vma=False,
    )
```

```python
import functools

import jax
import jax.numpy as jnp
from jax import lax
from jax.experimental import pallas as pl
from jax.experimental.pallas import tpu as pltpu
from jax.sharding import PartitionSpec as P

HEAD_DIM = 64
FF = 3072
STEP = 10
NORM_EPSILON = 1e-05
GROUPS = 32
LANES = 128
TILE = 256
ROW_BLOCK = 64
GELU_C = 0.7978845608028654
GELU_A = 0.044715
LOG2E = 1.4426950408889634
BF = jnp.bfloat16
F32 = jnp.float32

NN = (((1,), (0,)), ((), ()))
NT = (((1,), (1,)), ((), ()))
TN = (((0,), (0,)), ((), ()))


def dot(a, b, dims=NN):
    return lax.dot_general(a, b, dims, preferred_element_type=F32)


def norm_stats(h):
    mean = jnp.mean(h, axis=-1, keepdims=True)
    centred = h - mean
    var = jnp.mean(centred * centred, axis=-1, keepdims=True)
    rs = lax.rsqrt(var + NORM_EPSILON)
    return centred * rs, rs


def fold(x):
    return jnp.sum(x.reshape(x.shape[0] // 8, 8, x.shape[1]), axis=0)


def add_small(small, which, x):
    small[which] = small[which] + fold(x)


class Layer:
    def __init__(self, **refs):
        self.__dict__.update(refs)
        self.T, self.D = self.h.shape
        self.L = self.mask.shape[0]
        self.S = self.T // self.L
        self.PAIRS = self.D // LANES
        self.NJ = FF // self.D

    def qkv_part(self, ref, j, c, n):
        rows = ref.shape[1] // 3
        used = self.D // rows
        return ref.at[pl.ds(0, used), pl.ds(pl.multiple_of(j * rows, rows), rows), pl.ds(pl.multiple_of(c, n), n)]

    def out_part(self, ref, c, n):
        rows = ref.shape[1]
        used = self.D // rows
        return ref.at[pl.ds(ref.shape[0] - used, used), :, pl.ds(pl.multiple_of(c, n), n)]

    def up_part(self, ref, j, c, n):
        rows = ref.shape[1] // self.NJ
        used = self.D // rows
        return ref.at[pl.ds(0, used), pl.ds(pl.multiple_of(j * rows, rows), rows), pl.ds(pl.multiple_of(c, n), n)]

    def down_part(self, ref, j, c, n):
        rows = ref.shape[1]
        used = self.D // rows
        return ref.at[pl.ds(ref.shape[0] // 2 + j * used, used), :, pl.ds(pl.multiple_of(c, n), n)]

    def mask_col(self, s, base, n):
        m = self.mask[pl.ds(base, n), :].astype(F32)
        lane = lax.broadcasted_iota(jnp.int32, m.shape, 1)
        return jnp.sum(jnp.where(lane == self.lane + s, m, 0.0), axis=-1, keepdims=True)

    def embed(self, s):
        def body(i, _):
            base = pl.multiple_of(i * ROW_BLOCK, ROW_BLOCK)
            rows = pl.ds(pl.multiple_of(s * self.L + base, ROW_BLOCK), ROW_BLOCK)
            m = self.mask_col(s, base, ROW_BLOCK)
            h = self.x[rows, :].astype(F32) + m * self.norm[4:5, :] + self.time[s : s + 1, :]
            self.h[rows, :] = h
            xhat, _ = norm_stats(h)
            self.n1[rows, :] = (xhat * self.norm[0:1, :] + self.norm[1:2, :]).astype(BF)
            return 0

        lax.fori_loop(0, self.L // ROW_BLOCK, body, 0)

    def project(self, s):
        per = self.D // TILE
        rows = pl.ds(s * self.L, self.L)

        def body(i, _):
            j, c = lax.div(i, per), lax.rem(i, per) * TILE
            w = self.qkv_part(self.wa, j, c, TILE)[...].reshape(self.D, TILE)
            y = dot(self.n1[rows, :], w)
            self.qkv[rows, pl.ds(pl.multiple_of(i * TILE, TILE), TILE)] = y.astype(BF)
            return 0

        lax.fori_loop(0, 3 * per, body, 0)

    def pair_slices(self, s, p):
        rows = pl.ds(pl.multiple_of(s * self.L, self.L), self.L)
        cols = [pl.ds(pl.multiple_of(k * self.D + p * LANES, LANES), LANES) for k in range(3)]
        return rows, cols

    def half(self, x, hh):
        first = lax.broadcasted_iota(jnp.int32, x.shape, 1) < HEAD_DIM
        zero = jnp.zeros_like(x)
        return jnp.where(first, zero, x) if hh else jnp.where(first, x, zero)

    def attend(self, s, p):
        rows, cols = self.pair_slices(s, p)
        q, k, v = (self.qkv[rows, c] for c in cols)
        total = None
        for hh in range(2):
            sc = dot(self.half(q, hh), k, NT)
            top = jnp.max(sc, axis=-1, keepdims=True)
            e = jnp.exp2((sc - top) * (HEAD_DIM**-0.5 * LOG2E))
            w = (e * (1.0 / jnp.sum(e, axis=-1, keepdims=True))).astype(BF)
            self.soft[s * 2 * self.PAIRS + p * 2 + hh] = w
            o = dot(w, self.half(v, hh))
            total = o if total is None else total + o
        self.att[rows, cols[0]] = total.astype(BF)

    def attend_sequence(self, s):
        def body(p, _):
            self.attend(s, p)
            return 0

        lax.fori_loop(0, self.PAIRS, body, 0)

    def outer(self, s):
        rows = pl.ds(s * self.L, self.L)

        def body(i, _):
            c = i * TILE
            cols = pl.ds(pl.multiple_of(c, TILE), TILE)
            w = self.out_part(self.wa, c, TILE)[...].reshape(self.D, TILE)
            self.mid[rows, cols] = self.h[rows, cols] + dot(self.att[rows, :], w)
            return 0

        lax.fori_loop(0, self.D // TILE, body, 0)

    def second_norm(self, s):
        def body(i, _):
            rows = pl.ds(pl.multiple_of(s * self.L + i * ROW_BLOCK, ROW_BLOCK), ROW_BLOCK)
            xhat, _ = norm_stats(self.mid[rows, :])
            self.n2[rows, :] = (xhat * self.norm[2:3, :] + self.norm[3:4, :]).astype(BF)
            return 0

        lax.fori_loop(0, self.L // ROW_BLOCK, body, 0)

    def up(self):
        per = self.D // TILE

        def body(i, _):
            j, c = lax.div(i, per), lax.rem(i, per) * TILE
            cols = pl.ds(pl.multiple_of(i * TILE, TILE), TILE)
            w = self.up_part(self.wm, j, c, TILE)[...].reshape(self.D, TILE)
            for s in range(self.S):
                rows = pl.ds(s * self.L, self.L)
                u = dot(self.n2[rows, :], w)
                uu = u * u
                t = jnp.tanh(GELU_C * (u * (1.0 + GELU_A * uu)))
                left = 0.5 * (1.0 + t)
                self.act[pl.ds(pl.multiple_of(j * self.T + s * self.L, self.L), self.L), pl.ds(pl.multiple_of(c, TILE), TILE)] = (u * left).astype(BF)
                slope = left + (0.5 * GELU_C) * u * (1.0 - t * t) * (1.0 + 3.0 * GELU_A * uu)
                self.du[rows, cols] = slope.astype(BF)
            return 0

        lax.fori_loop(0, self.NJ * per, body, 0)

    def down(self):
        per = self.D // TILE

        def body(i, _):
            c = i * TILE
            cols = pl.ds(pl.multiple_of(c, TILE), TILE)
            for s in range(self.S):
                rows = pl.ds(s * self.L, self.L)
                total = self.mid[rows, cols]
                for j in range(self.NJ):
                    w = self.down_part(self.wm, j, c, TILE)[...].reshape(self.D, TILE)
                    total = total + dot(self.act[pl.ds(j * self.T + s * self.L, self.L), :], w)
                self.out[rows, cols] = total.astype(BF)
            return 0

        lax.fori_loop(0, per, body, 0)

    def mask_cotangent(self):
        for s in range(self.S):
            def body(i, _, s=s):
                base = pl.multiple_of(i * ROW_BLOCK, ROW_BLOCK)
                rows = pl.ds(pl.multiple_of(s * self.L + base, ROW_BLOCK), ROW_BLOCK)
                m = self.mask_col(s, base, ROW_BLOCK)
                self.g[rows, :] = (self.g[rows, :].astype(F32) * m).astype(BF)
                return 0

            lax.fori_loop(0, self.L // ROW_BLOCK, body, 0)

    def grad_pre(self):
        per = self.D // TILE

        def body(i, _):
            cols = pl.ds(pl.multiple_of(i * (self.D // 2), self.D // 2), self.D // 2)
            rows_w = self.wm.shape[1]
            used = self.D // 2 // rows_w
            w = self.wm[pl.ds(self.wm.shape[0] // 2 + i * used, used)].reshape(self.D // 2, self.D)
            for s in range(self.S):
                rows = pl.ds(s * self.L, self.L)
                d = dot(self.g[rows, :], w, NT)
                self.du[rows, cols] = (d * self.du[rows, cols].astype(F32)).astype(BF)
            return 0

        lax.fori_loop(0, 2 * self.NJ, body, 0)

    def turn_activated(self):
        for j in range(self.NJ):
            rows = pl.ds(j * self.T, self.T)
            self.turn[...] = self.act[rows, :].T
            self.act[rows, :] = self.turn[...]
        self.turn[...] = self.n2[...].T

    def grad_down(self, part, parts):
        group = self.gm_down.shape[1]
        used = self.D // group
        n = group // parts
        per = self.D // TILE

        def body(i, _):
            j, c = lax.div(i, per), pl.multiple_of(lax.rem(i, per) * TILE, TILE)
            a = jnp.concatenate(
                [
                    self.act[pl.ds(pl.multiple_of(j * self.D + u * group + part * n, 16), n), :]
                    for u in range(used)
                ]
            )
            y = dot(a, self.g[:, pl.ds(c, TILE)]).astype(BF)
            ref = self.gm_down.at[pl.ds(self.gm_down.shape[0] // 2 + j * used, used), pl.ds(part * n, n), pl.ds(c, TILE)]
            ref[...] = y.reshape(used, n, TILE)
            return 0

        lax.fori_loop(0, self.NJ * per, body, 0)

    def grad_up(self, part, parts):
        per = self.D // TILE
        n = self.NJ * per // parts

        def body(i, _):
            j, c = lax.div(i, per), lax.rem(i, per) * TILE
            y = dot(self.turn[...], self.du[:, pl.ds(pl.multiple_of(i * TILE, TILE), TILE)])
            ref = self.up_part(self.gm_up, j, c, TILE)
            ref[...] = y.astype(BF).reshape(ref.shape)
            return 0

        lax.fori_loop(part * n, (part + 1) * n, body, 0)

    def grad_normed_two(self):
        rows_w = self.wm.shape[1] // self.NJ
        n = self.D // 2
        used = n // rows_w

        def body(i, _):
            cols = pl.ds(pl.multiple_of(i * n, n), n)
            for s in range(self.S):
                rows = pl.ds(s * self.L, self.L)
                total = None
                for j in range(self.NJ):
                    w = self.wm[pl.ds(i * used, used), pl.ds(j * rows_w, rows_w), :].reshape(n, self.D)
                    y = dot(self.du[rows, pl.ds(j * self.D, self.D)], w, NT)
                    total = y if total is None else total + y
                self.dn[rows, cols] = total
            return 0

        lax.fori_loop(0, 2, body, 0)

    def norm_two_back(self):
        def body(i, _):
            rows = pl.ds(pl.multiple_of(i * ROW_BLOCK, ROW_BLOCK), ROW_BLOCK)
            xhat, rs = norm_stats(self.mid[rows, :])
            dy = self.dn[rows, :]
            add_small(self.small, 2, dy * xhat)
            add_small(self.small, 3, dy)
            e = dy * self.norm[2:3, :]
            back = (e - jnp.mean(e, -1, keepdims=True) - xhat * jnp.mean(e * xhat, -1, keepdims=True)) * rs
            gm = self.g[rows, :].astype(F32) + back
            self.dn[rows, :] = gm
            self.gb[rows, :] = gm.astype(BF)
            return 0

        lax.fori_loop(0, self.T // ROW_BLOCK, body, 0)

    def grad_outer(self):
        self.turn[...] = self.att[...].T

        def body(i, _):
            c = pl.multiple_of(i * TILE, TILE)
            y = dot(self.turn[...], self.gb[:, pl.ds(c, TILE)])
            ref = self.out_part(self.ga, c, TILE)
            ref[...] = y.astype(BF).reshape(ref.shape)
            return 0

        lax.fori_loop(0, self.D // TILE, body, 0)

    def grad_attended(self):
        n = self.D // 2
        rows_w = self.wa.shape[1]
        used = n // rows_w
        first = self.wa.shape[0] - 2 * used

        def body(i, _):
            w = self.wa[pl.ds(first + i * used, used)].reshape(n, self.D)
            for s in range(self.S):
                rows = pl.ds(s * self.L, self.L)
                self.att[rows, pl.ds(pl.multiple_of(i * n, n), n)] = dot(self.gb[rows, :], w, NT).astype(BF)
            return 0

        lax.fori_loop(0, 2, body, 0)

    def attend_back(self, s, p):
        rows, cols = self.pair_slices(s, p)
        q, k, v = (self.qkv[rows, c] for c in cols)
        da = self.att[rows, cols[0]]
        dq = dk = dv = None
        for hh in range(2):
            w = self.soft[s * 2 * self.PAIRS + p * 2 + hh]
            da_h = self.half(da, hh)
            dp = dot(da_h, v, NT)
            wf = w.astype(F32)
            t = wf * dp
            ds = (t - wf * jnp.sum(t, axis=-1, keepdims=True)).astype(BF)
            parts = (dot(ds, self.half(k, hh)), dot(ds, self.half(q, hh), TN), dot(w, da_h, TN))
            dq, dk, dv = parts if dq is None else (dq + parts[0], dk + parts[1], dv + parts[2])
        scale = HEAD_DIM**-0.5
        self.qkv[rows, cols[0]] = (dq * scale).astype(BF)
        self.qkv[rows, cols[1]] = (dk * scale).astype(BF)
        self.qkv[rows, cols[2]] = dv.astype(BF)

    def attend_back_sequence(self, s):
        def body(p, _):
            self.attend_back(s, p)
            return 0

        lax.fori_loop(0, self.PAIRS, body, 0)

    def grad_normed_one(self, s):
        n = self.D // 3
        rows_w = self.wa.shape[1] // 3
        used = n // rows_w
        rows = pl.ds(s * self.L, self.L)

        def body(i, _):
            total = None
            for j in range(3):
                w = self.wa[pl.ds(i * used, used), pl.ds(j * rows_w, rows_w), :].reshape(n, self.D)
                y = dot(self.qkv[rows, pl.ds(j * self.D, self.D)], w, NT)
                total = y if total is None else total + y
            self.mid[rows, pl.ds(pl.multiple_of(i * n, n), n)] = total
            return 0

        lax.fori_loop(0, 3, body, 0)

    def norm_one_back(self, s):
        def body(i, _):
            base = pl.multiple_of(i * ROW_BLOCK, ROW_BLOCK)
            rows = pl.ds(pl.multiple_of(s * self.L + base, ROW_BLOCK), ROW_BLOCK)
            xhat, rs = norm_stats(self.h[rows, :])
            dy = self.mid[rows, :]
            add_small(self.small, 0, dy * xhat)
            add_small(self.small, 1, dy)
            e = dy * self.norm[0:1, :]
            back = (e - jnp.mean(e, -1, keepdims=True) - xhat * jnp.mean(e * xhat, -1, keepdims=True)) * rs
            gs = self.dn[rows, :] + back
            add_small(self.small, 5 + s, gs)
            add_small(self.small, 4, gs * self.mask_col(s, base, ROW_BLOCK))
            self.x[rows, :] = gs.astype(BF)
            return 0

        lax.fori_loop(0, self.L // ROW_BLOCK, body, 0)

    def grad_inner(self):
        per = self.D // TILE
        self.turn[...] = self.n1[...].T

        def body(i, _):
            j, c = lax.div(i, per), lax.rem(i, per) * TILE
            y = dot(self.turn[...], self.qkv[:, pl.ds(pl.multiple_of(i * TILE, TILE), TILE)])
            ref = self.qkv_part(self.ga, j, c, TILE)
            ref[...] = y.astype(BF).reshape(ref.shape)
            return 0

        lax.fori_loop(0, 3 * per, body, 0)


def run_all(k):
    for i in range(8):
        k.small[i] = jnp.zeros(k.small.shape[1:], F32)
    for s in range(k.S):
        k.embed(s)
        k.project(s)
        k.attend_sequence(s)
        k.outer(s)
        k.second_norm(s)
    k.up()
    k.down()
    k.mask_cotangent()
    k.grad_pre()
    k.turn_activated()
    k.grad_down(0, 1)
    k.grad_up(0, 1)
    k.grad_normed_two()
    k.norm_two_back()
    k.grad_outer()
    k.grad_attended()
    for s in range(k.S):
        k.attend_back_sequence(s)
        k.grad_normed_one(s)
        k.norm_one_back(s)
    k.grad_inner()


def flip(index, bit):
    return index + bit - 2 * bit * lax.rem(lax.div(index, bit), 2)


def pick(table, index):
    value = table[0]
    for i in range(1, len(table)):
        value = jnp.where(index == i, table[i], value)
    return value


class Links:
    def __init__(self, Z, S, part):
        self.Z, self.S, self.part = Z, S, part
        self.r, self.z = lax.axis_index("rows"), lax.axis_index("seq")
        r = self.r
        self.core, self.xn, self.yn = flip(r, 1), flip(r, 2), flip(r, 4)
        self.diag = flip(self.xn, 4)
        self.pending = []
        near, far = flip(self.z, 1), flip(self.z, 2)
        self.near, self.far = near, far
        self.order = [self.z, near, far, flip(near, 2)]

    def barrier(self):
        bar = pltpu.get_barrier_semaphore()
        peers = [(self.core, self.z), (self.xn, self.z), (self.yn, self.z)]
        peers += [(self.r, lax.rem(self.z + i, self.Z)) for i in range(1, self.Z)]
        for peer in peers:
            pl.semaphore_signal(bar, 1, device_id=peer, device_id_type=pl.DeviceIdType.MESH)
        pl.semaphore_wait(bar, len(peers))

    def send(self, src, dst, ss, rs, peer, cond=None, owner=None):
        copy = pltpu.make_async_remote_copy(
            src, dst, ss, rs, device_id=peer, device_id_type=pl.DeviceIdType.MESH
        )
        if cond is None:
            copy.start()
        else:
            pl.when(cond)(copy.start)
        self.pending.append((owner, cond, copy))

    def arrived(self, dst, rs, cond=None):
        copy = pltpu.make_async_remote_copy(
            dst, dst, rs, rs, device_id=(self.core, self.z), device_id_type=pl.DeviceIdType.MESH
        )
        if cond is None:
            copy.wait_recv()
        else:
            pl.when(cond)(copy.wait_recv)

    def flush(self, src=None):
        left = []
        for item in self.pending:
            owner, cond, copy = item
            if src is not None and owner is not src:
                left.append(item)
            elif cond is None:
                copy.wait_send()
            else:
                pl.when(cond)(copy.wait_send)
        self.pending = left

    def gather(self, w, ss, rs):
        Z, z = self.Z, self.z
        count = [0]

        def go(row, zz, peer, cond=None):
            i = row * Z + zz
            self.send(w.at[i], w.at[i], ss.at[count[0]], rs.at[i], peer, cond, w)
            count[0] += 1

        def got(row, zz):
            i = row * Z + zz
            self.arrived(w.at[i], rs.at[i])

        def own(i):
            zz = self.order[i]
            if i:
                got(self.r, zz)
            if i == 0:
                go(self.r, zz, (self.r, self.far))
            if i == 0 or i == 2:
                go(self.r, zz, (self.r, self.near))
            go(self.r, zz, (self.xn, z))
            go(self.r, zz, (self.yn, z))
            go(self.r, zz, (self.core, z))

        def side(i):
            zz = self.order[i]
            got(self.xn, zz)
            go(self.xn, zz, (self.yn, z), zz < Z // 2)
            got(self.yn, zz)
            go(self.yn, zz, (self.xn, z), zz >= Z // 2)
            go(self.xn, zz, (self.core, z))
            go(self.yn, zz, (self.core, z))

        def far(i):
            zz = self.order[i]
            got(self.diag, zz)
            go(self.diag, zz, (self.core, z))

        def last():
            for row in (self.r, self.xn, self.yn, self.diag):
                for i in range(Z):
                    got(flip(row, 1), self.order[i])

        return own, side, far, last

    def gather_small(self, w, ss, rs):
        Z, z = self.Z, self.z
        half = Z // 2

        def block(row, lo=0, n=Z):
            return w.at[pl.ds(row * Z + lo, n)]

        def go(ref, n, peer):
            self.send(ref, ref, ss.at[n], rs.at[n], peer)

        def along_z():
            for step in range(1, Z):
                go(block(self.r, z, 1), step, (self.r, lax.rem(z + step, Z)))

        def spread():
            for step in range(1, Z):
                self.arrived(block(self.r, lax.rem(z + Z - step, Z), 1), rs.at[step])
            go(block(self.r), 4, (self.xn, z))
            go(block(self.r), 5, (self.yn, z))
            go(block(self.r), 6, (self.core, z))

        def forward():
            self.arrived(block(self.xn), rs.at[4])
            go(block(self.xn, 0, half), 7, (self.yn, z))
            self.arrived(block(self.yn), rs.at[5])
            go(block(self.yn, half, half), 8, (self.xn, z))
            go(block(self.xn), 9, (self.core, z))
            go(block(self.yn), 10, (self.core, z))

        def corner():
            self.arrived(block(self.diag, 0, half), rs.at[7])
            self.arrived(block(self.diag, half, half), rs.at[8])
            go(block(self.diag), 11, (self.core, z))

        def last():
            self.arrived(block(self.core), rs.at[6])
            self.arrived(block(flip(self.xn, 1)), rs.at[9])
            self.arrived(block(flip(self.yn, 1)), rs.at[10])
            self.arrived(block(flip(self.diag, 1)), rs.at[11])

        return along_z, spread, forward, corner, last

    def exchange_in(self, src, dst, ss, rs, local, seqs):
        L = self.part * self.Z
        for i in seqs:
            for step in range(1, self.Z):
                to = lax.rem(self.z + step, self.Z)
                rows = pl.ds(i * L + self.z * self.part, self.part)
                n = i * (self.Z - 1) + step - 1
                self.send(src.at[to * self.S + i], dst.at[rows], ss.at[n], rs.at[n], (self.r, to))
            rows = pl.ds(i * L + self.z * self.part, self.part)
            pltpu.make_async_copy(src.at[self.z * self.S + i], dst.at[rows], local.at[i]).start()

    def exchange_in_done(self, src, dst, rs, local, i):
        L = self.part * self.Z
        for step in range(1, self.Z):
            source = lax.rem(self.z + self.Z - step, self.Z)
            rows = pl.ds(i * L + source * self.part, self.part)
            self.arrived(dst.at[rows], rs.at[i * (self.Z - 1) + step - 1])
        rows = pl.ds(i * L + self.z * self.part, self.part)
        pltpu.make_async_copy(src.at[self.z * self.S + i], dst.at[rows], local.at[i]).wait()

    def exchange_out(self, src, dst, ss, rs, local, i):
        L = self.part * self.Z
        for step in range(1, self.Z):
            to = lax.rem(self.z + step, self.Z)
            rows = pl.ds(i * L + to * self.part, self.part)
            n = i * (self.Z - 1) + step - 1
            self.send(src.at[rows], dst.at[self.z * self.S + i], ss.at[n], rs.at[n], (self.r, to), None, dst)
        rows = pl.ds(i * L + self.z * self.part, self.part)
        pltpu.make_async_copy(src.at[rows], dst.at[self.z * self.S + i], local.at[i]).start()

    def exchange_out_done(self, src, dst, rs, local, i):
        L = self.part * self.Z
        for step in range(1, self.Z):
            source = lax.rem(self.z + self.Z - step, self.Z)
            self.arrived(dst.at[source * self.S + i], rs.at[i * (self.Z - 1) + step - 1])
        rows = pl.ds(i * L + self.z * self.part, self.part)
        pltpu.make_async_copy(src.at[rows], dst.at[self.z * self.S + i], local.at[i]).wait()

    def scatter(self, g, base, part, inbox, box0, ss, rs, total):
        Z, z = self.Z, self.z
        half = Z // 2
        chip = lax.div(self.r, 2)
        k = lax.rem(self.r, 2)
        cx, cy = flip(chip, 1), flip(chip, 2)
        cd = flip(cx, 2)
        rows = total.shape[0]

        def block(c, parity, lo, n):
            return g.at[pl.ds(base + (2 * c + parity) * Z + lo, n), pl.ds(part * rows, rows)]

        def inslot(i, n):
            return inbox.at[pl.ds(box0 + i, n)]

        def add(dst, src, n):
            def body(i, _):
                dst[i] = (dst[i].astype(F32) + src[i].astype(F32)).astype(BF)
                return 0

            lax.fori_loop(0, n, body, 0)

        XY = 4 * Z
        ZB = XY + 6 * half

        def core_send_all():
            for c in range(4):
                core_send(c)

        def core_send(c):
            self.send(block(c, 1 - k, 0, Z), inslot(c * Z, Z), ss.at[c], rs.at[c], (self.core, z))

        def core_add(c):
            self.arrived(inslot(c * Z, Z), rs.at[c])
            add(block(c, k, 0, Z), inslot(c * Z, Z), Z)

        def xy_send(slot, c, lo, peer):
            i = XY + slot * half
            self.send(block(c, k, lo, half), inslot(i, half), ss.at[4 + slot], rs.at[4 + slot], (peer, z))

        def xy_add(slot, c, lo):
            i = XY + slot * half
            self.arrived(inslot(i, half), rs.at[4 + slot])
            add(block(c, k, lo, half), inslot(i, half), half)

        def first():
            core_add(cd)
            xy_send(0, cd, 0, self.xn)
            xy_send(2, cd, half, self.yn)
            core_add(cx)
            xy_send(1, cx, 0, self.xn)
            core_add(cy)
            xy_send(3, cy, half, self.yn)
            core_add(chip)

        def second():
            xy_add(0, cy, 0)
            xy_send(4, cy, 0, self.yn)
            xy_add(2, cx, half)
            xy_send(5, cx, half, self.xn)

        def second_own():
            xy_add(1, chip, 0)
            xy_add(3, chip, half)

        def third():
            xy_add(4, chip, 0)
            xy_add(5, chip, half)

        def z_send(slot, target, peer):
            box = inslot(ZB + slot, 1)
            self.send(block(chip, k, target, 1), box, ss.at[10 + slot], rs.at[10 + slot], (self.r, peer))

        def z_first():
            z_send(1, self.order[3], self.near)
            z_send(0, self.near, self.near)

        def z_second():
            self.arrived(inslot(ZB + 1, 1), rs.at[11])
            add(block(chip, k, self.far, 1), inslot(ZB + 1, 1), 1)
            z_send(2, self.far, self.far)

        def final():
            self.arrived(inslot(ZB, 1), rs.at[10])
            total[...] = block(chip, k, z, 1)[0].astype(F32) + inbox[box0 + ZB].astype(F32)
            self.arrived(inslot(ZB + 2, 1), rs.at[12])
            total[...] += inbox[box0 + ZB + 2].astype(F32)

        return core_send_all, first, second, second_own, third, z_first, z_second, final


def compute_kernel(x, mask, g_in, time, norm, wa, wm, out, gin, ga, gm, small, *scratch):
    names = ("g", "h", "n1", "qkv", "att", "mid", "n2", "act", "du", "soft", "dn", "gb", "turn", "sums")
    refs = dict(zip(names, scratch))
    sums = refs.pop("sums")
    pltpu.sync_copy(x, gin)
    pltpu.sync_copy(g_in, refs["g"])
    layer = Layer(
        x=gin, mask=mask, time=time, norm=norm, wa=wa, wm=wm, out=out, ga=ga, gm_down=gm, gm_up=gm, small=sums, lane=0, **refs
    )
    run_all(layer)
    for i in range(8):
        small[i : i + 1, :] = jnp.sum(sums[i], axis=0, keepdims=True)


def layer_scratch(T, D, S, L):
    heads = D // HEAD_DIM
    return dict(
        h=pltpu.VMEM((T, D), F32),
        n1=pltpu.VMEM((T, D), BF),
        qkv=pltpu.VMEM((T, 3 * D), BF),
        att=pltpu.VMEM((T, D), BF),
        mid=pltpu.VMEM((T, D), F32),
        n2=pltpu.VMEM((T, D), BF),
        act=pltpu.VMEM((FF // D * T, D), BF),
        du=pltpu.VMEM((T, FF), BF),
        soft=pltpu.VMEM((S * heads, L, L), BF),
        dn=pltpu.VMEM((T, D), F32),
        gb=pltpu.VMEM((T, D), BF),
        turn=pltpu.VMEM((D, D), BF),
        sums=pltpu.VMEM((8, 8, D), F32),
    )


def pad_rows(x):
    return jnp.pad(x, ((0, 8 - x.shape[0]), (0, 0)))


def rows_split(flat, groups, parts, D):
    return flat.reshape(groups, -1, parts, D).transpose(0, 2, 1, 3).reshape(groups, -1, D)


def rows_join(block, parts, D):
    groups = block.shape[0]
    return block.reshape(groups, parts, -1, D).transpose(0, 2, 1, 3).reshape(-1)


def adamw(master, moment_one, moment_two, gradient, step_rate):
    first_new = 0.5 * moment_one + 0.5 * gradient
    second_new = 0.5 * moment_two + 0.5 * gradient * gradient
    correct = 1.0 - 0.5**STEP
    update = first_new / correct / (jnp.sqrt(second_new / correct) + 1e-08)
    return (master - step_rate * (update + 0.1 * master), first_new, second_new)


def general(
    resid_in,
    mask,
    steps_row,
    cotangent,
    attn_master,
    attn_first,
    attn_second,
    mlp_master,
    mlp_first,
    mlp_second,
    norm_master,
    norm_first,
    norm_second,
    time_master,
    time_first,
    time_second,
):
    D = resid_in.shape[2]
    axes = ("rows", "seq")
    seq_count = lax.axis_size("seq")
    S = resid_in.shape[0] // seq_count
    L = resid_in.shape[1] * seq_count
    T = S * L
    attn_full = lax.all_gather(attn_master.astype(BF), axes, axis=0, tiled=True)
    mlp_full = lax.all_gather(mlp_master.astype(BF), axes, axis=0, tiled=True)
    inner = 3 * D * D
    wide = D * FF
    wa = jnp.concatenate(
        (rows_split(attn_full[:inner], 24, 3, D), attn_full[inner:].reshape(8, -1, D))
    )
    wm = jnp.concatenate((rows_split(mlp_full[:wide], 16, FF // D, D), mlp_full[wide:].reshape(16, -1, D)))
    exchange = functools.partial(lax.all_to_all, axis_name="seq", split_axis=0, concat_axis=1, tiled=True)
    x = exchange(resid_in).reshape(T, D)
    g = exchange(cotangent).reshape(T, D)
    mask_t = jnp.pad(exchange(mask.astype(BF)).T, ((0, 0), (0, LANES - S)))
    steps_use = lax.dynamic_slice_in_dim(steps_row, lax.axis_index("seq") * S, S, 0)
    time_rows = pad_rows(jnp.take(time_master, steps_use, axis=0))
    V = pl.BlockSpec(memory_space=pltpu.VMEM)
    A = pl.BlockSpec(memory_space=pl.ANY)
    shape = jax.ShapeDtypeStruct
    scratch = layer_scratch(T, D, S, L)
    out, gin, ga, gm, small = pl.pallas_call(
        compute_kernel,
        out_shape=(shape((T, D), BF), shape((T, D), BF), shape(wa.shape, BF), shape(wm.shape, BF), shape((8, D), F32)),
        in_specs=[A, V, A, V, V, V, V],
        out_specs=(V,) * 5,
        scratch_shapes=[pltpu.VMEM((T, D), BF)] + list(scratch.values()),
        compiler_params=pltpu.CompilerParams(vmem_limit_bytes=62 << 20),
    )(x, mask_t, g, time_rows, pad_rows(norm_master), wa, wm)
    attn_flat = jnp.concatenate((rows_join(ga[:24], 3, D), ga[24:].reshape(-1))).astype(F32)
    mlp_flat = jnp.concatenate((rows_join(gm[:16], FF // D, D), gm[16:].reshape(-1))).astype(F32)
    attn_grad = lax.psum_scatter(attn_flat, axes, scatter_dimension=0, tiled=True)
    mlp_grad = lax.psum_scatter(mlp_flat, axes, scatter_dimension=0, tiled=True)
    every = lax.all_gather(small, axes, axis=0)
    spread = functools.partial(lax.all_to_all, axis_name="seq", split_axis=1, concat_axis=0, tiled=True)
    return finish(
        spread(out.reshape(S, L, D)),
        spread(gin.reshape(S, L, D)),
        lax.all_gather(steps_row, "rows", axis=0, tiled=True),
        every,
        adamw(attn_master, attn_first, attn_second, attn_grad, 0.05),
        adamw(mlp_master, mlp_first, mlp_second, mlp_grad, 0.03),
        (norm_master, norm_first, norm_second),
        (time_master, time_first, time_second),
        S,
    )


def finish(resid_out, grad_in, steps, every, attn, mlp, norm, time, S):
    D = every.shape[2]
    norm_grad = jnp.sum(every[:, :5], axis=0)
    chosen = (jnp.arange(time[0].shape[0], dtype=jnp.int32)[:, None] == steps[None, :]).astype(F32)
    time_grad = jnp.dot(chosen, every[:, 5 : 5 + S].reshape(-1, D), precision=lax.Precision.HIGHEST)
    return (
        resid_out,
        grad_in,
        *attn,
        attn[0].astype(BF),
        *mlp,
        mlp[0].astype(BF),
        *adamw(*norm, norm_grad, 0.2),
        *adamw(*time, time_grad, 0.3),
    )


LAYER_REFS = ("h", "n1", "qkv", "att", "mid", "n2", "act", "du", "soft", "dn", "turn", "sums")


def whole_kernel(
    cfg, resid, cot, mask_in, time, tags, norm, sa, sm, resid_out, grad_in, ta, tm, every_out, *scratch
):
    Z, S, part = cfg
    names = (
        "wa", "wm", "inbox", "x", "g", "mask", "h", "n1",
        "qkv", "att", "mid", "n2", "act", "du", "soft", "dn",
        "turn", "sums", "every", "sem_a", "sem_m", "sem_e", "sem_in", "sem_cot",
        "sem_out", "sem_gin", "sem_mask", "loc", "sem_ra", "sem_rm", "credit", "total",
    )
    v = dict(zip(names, scratch))
    wm, ga = v["wm"], v["act"].reshape(GROUPS, v["wa"].shape[1], v["wa"].shape[2])
    half = GROUPS // 2
    grads = wm.at[pl.ds(half, GROUPS)]
    k = Layer(
        x=v["x"], out=v["x"], g=v["g"], mask=v["mask"], time=time, norm=norm, wa=v["wa"], wm=wm.at[pl.ds(0, GROUPS)],
        ga=ga, gm_up=grads, gm_down=grads, small=v["sums"], gb=v["n2"], lane=lax.axis_index("seq") * S,
        **{n: v[n] for n in LAYER_REFS[:-1]},
    )
    net = Links(Z, S, part)
    me = net.r * Z + net.z
    loc = v["loc"]
    own_a = pltpu.make_async_copy(sa, v["wa"].at[me], loc.at[4, 0])
    own_m = pltpu.make_async_copy(sm, wm.at[me], loc.at[4, 1])
    own_a.start()
    own_m.start()
    for i in range(8):
        k.small[i] = jnp.zeros(k.small.shape[1:], F32)
    net.barrier()
    own_a.wait()
    own_m.wait()

    def pair(name):
        return v[name].at[0], v[name].at[1]

    def pump(events, n=1):
        for _ in range(n):
            if events:
                events.pop(0)()

    a_own, a_side, a_far, a_last = net.gather(v["wa"], *pair("sem_a"))
    m_own, m_side, m_far, m_last = net.gather(wm, *pair("sem_m"))

    def stream(s):
        net.exchange_in(resid, k.x, *pair("sem_in"), loc.at[0], [s])

    a_own(0)
    m_own(0)
    for step in range(1, Z):
        to = lax.rem(net.z + step, Z)
        rows = pl.ds(net.z * part, part)
        net.send(mask_in, k.mask.at[rows], v["sem_mask"].at[0, step], v["sem_mask"].at[1, step], (net.r, to))
    own_mask = pltpu.make_async_copy(mask_in, k.mask.at[pl.ds(net.z * part, part)], loc.at[4, 2])
    own_mask.start()
    a_own(1)
    a_side(0)
    m_own(1)
    stream(0)
    m_side(0)
    a_own(2)
    a_side(1)
    a_far(0)
    m_own(2)
    stream(1)
    m_side(1)
    m_far(0)
    a_own(3)
    a_side(2)
    a_far(1)
    m_own(3)
    stream(2)
    net.exchange_in(cot, k.g, *pair("sem_cot"), loc.at[1], range(S))
    a_side(3)
    a_far(2)
    a_far(3)
    a_last()
    rm = [functools.partial(m_side, 2), functools.partial(m_far, 1), functools.partial(m_side, 3), functools.partial(m_far, 2), functools.partial(m_far, 3), m_last]
    own_mask.wait()
    for step in range(1, Z):
        source = lax.rem(net.z + Z - step, Z)
        net.arrived(k.mask.at[pl.ds(source * part, part)], v["sem_mask"].at[1, step])

    for s in range(S):
        net.exchange_in_done(resid, k.x, v["sem_in"].at[1], loc.at[0], s)
        k.embed(s)
        pump(rm)
        k.project(s)
        pump(rm)
        k.attend_sequence(s)
        pump(rm)
        k.outer(s)
        k.second_norm(s)
    pump(rm, len(rm))
    k.up()
    k.down()
    for s in range(S):
        net.exchange_out(k.out, resid_out, *pair("sem_out"), loc.at[2], s)
    for s in range(S):
        net.exchange_in_done(cot, k.g, v["sem_cot"].at[1], loc.at[1], s)
    k.mask_cotangent()
    k.grad_pre()
    net.flush(wm)
    k.turn_activated()
    rows = sa.shape[0]
    parts = sm.shape[0] // rows
    boxes = v["inbox"].shape[0] // parts
    totals = [v["total"].at[pl.ds(p * rows, rows)] for p in range(parts + 1)]
    pieces = [
        net.scatter(wm, half, p, v["inbox"], p * boxes, v["sem_rm"].at[0, p], v["sem_rm"].at[1, p], totals[p])
        for p in range(parts)
    ]
    (p_core, p_first, p_second, p_own, p_third, p_z, p_zz, p_final) = pieces[0]
    (q_core, q_first, q_second, q_own, q_third, q_z, q_zz, q_final) = pieces[1]
    k.grad_down(0, parts)
    k.grad_up(0, parts)
    p_core()
    k.grad_down(1, parts)
    p_first()
    k.grad_up(1, parts)
    q_core()
    k.grad_normed_two()
    credit = v["credit"]
    peers = ((net.core, net.z), (net.xn, net.z), (net.yn, net.z), (net.r, net.near), (net.r, net.far))
    for peer in peers:
        pl.semaphore_signal(credit, 1, device_id=peer, device_id_type=pl.DeviceIdType.MESH)
    q_first()
    k.norm_two_back()
    k.grad_outer()
    k.grad_attended()
    net.flush(resid_out)
    for s in range(S):
        net.exchange_out_done(k.out, resid_out, v["sem_out"].at[1], loc.at[2], s)
    k.attend_back_sequence(0)
    p_second()
    k.grad_normed_one(0)
    k.norm_one_back(0)
    net.exchange_out(k.x, grad_in, *pair("sem_gin"), loc.at[3], 0)
    k.attend_back_sequence(1)
    p_own()
    q_second()
    k.grad_normed_one(1)
    k.norm_one_back(1)
    net.exchange_out(k.x, grad_in, *pair("sem_gin"), loc.at[3], 1)
    k.attend_back_sequence(2)
    p_third()
    p_z()
    k.grad_inner()
    pl.semaphore_wait(credit, len(peers))
    (a_core, a_first, a_second, a_own, a_third, a_z, a_zz, a_final) = net.scatter(
        ga, 0, 0, wm.reshape(wm.shape[0] * parts, rows, wm.shape[2]), 0, *pair("sem_ra"), totals[parts]
    )
    a_core()
    k.grad_normed_one(2)
    a_first()
    k.norm_one_back(2)
    net.exchange_out(k.x, grad_in, *pair("sem_gin"), loc.at[3], 2)
    for i in range(8):
        v["every"][me, i : i + 1, 0 : k.D] = jnp.sum(k.small[i], axis=0, keepdims=True)
    v["every"][me, :, k.D : k.D + LANES] = tags[...]
    e_z, e_spread, e_forward, e_corner, e_last = net.gather_small(v["every"], *pair("sem_e"))
    e_z()
    q_own()
    q_third()
    q_z()
    p_zz()
    e_spread()
    a_second()
    q_zz()
    e_forward()
    a_own()
    p_final()
    e_corner()
    a_third()
    a_z()
    q_final()
    a_zz()
    e_last()
    a_final()
    for s in range(S):
        net.exchange_out_done(k.x, grad_in, v["sem_gin"].at[1], loc.at[3], s)
    outs = [pltpu.make_async_copy(totals[parts], ta, loc.at[4, 0])]
    outs += [pltpu.make_async_copy(totals[p], tm.at[pl.ds(p * rows, rows)], loc.at[0, p]) for p in range(parts)]
    outs.append(pltpu.make_async_copy(v["every"], every_out, loc.at[4, 2]))
    for copy in outs:
        copy.start()
    for copy in outs:
        copy.wait()
    net.flush()


def walk(is_split, parts, rows, D, visit):
    per = D // LANES

    def split():
        n = rows // parts
        for j in range(parts):
            for c in range(per):
                visit(pl.ds(j * n, n), pl.ds(c * LANES, LANES), pl.ds(j * per + c, n, stride=parts * per))

    def plain():
        for c in range(per):
            visit(pl.ds(0, rows), pl.ds(c * LANES, LANES), pl.ds(c, rows, stride=per))

    pl.when(is_split)(split)
    pl.when(jnp.logical_not(is_split))(plain)


def device_kinds():
    Z, R = lax.axis_size("seq"), lax.axis_size("rows")
    device = lax.axis_index("rows") * Z + lax.axis_index("seq")
    return device < R * Z * 3 // 4, device < R * Z // 2


def before_kernel(S, steps, mask, time_master, attn, mlp, sa, sm, mask_out, time_rows, tags, board, sems):
    D = sa.shape[1]
    first = lax.axis_index("seq") * S
    time_rows[...] = jnp.zeros(time_rows.shape, F32)
    copies = [
        pltpu.make_async_copy(time_master.at[pl.ds(steps[first + s], 1)], time_rows.at[pl.ds(s, 1)], sems.at[s])
        for s in range(S)
    ]
    for copy in copies:
        copy.start()
    row = lax.broadcasted_iota(jnp.int32, tags.shape, 0)
    value = jnp.full(tags.shape, -1, jnp.int32)
    for s in range(S):
        value = jnp.where(row == 5 + s, steps[first + s], value)
    tags[...] = value.astype(F32)
    board[...] = jnp.zeros(board.shape, F32)
    board[0 : mask.shape[0], 0 : mask.shape[1]] = mask[...].astype(F32)
    mask_out[...] = board[...].T[0 : mask.shape[1], :].astype(BF)
    is_inner, is_up = device_kinds()

    def cast(src, dst):
        def visit(rows, cols, lines):
            dst[rows, cols] = src[lines, :].astype(BF)

        return visit

    walk(is_inner, 3, sa.shape[0], D, cast(attn, sa))
    walk(is_up, FF // D, sm.shape[0], D, cast(mlp, sm))
    for copy in copies:
        copy.wait()


def adamw_low(master, moment_one, moment_two, gradient, step_rate):
    first_new = 0.5 * moment_one + 0.5 * gradient
    second_new = 0.5 * moment_two + 0.5 * gradient * gradient
    scale = 1.0 / (1.0 - 0.5**STEP)
    update = (first_new * scale) / (jnp.sqrt(second_new * scale) + 1e-08)
    return master - step_rate * (update + 0.1 * master), first_new, second_new


def after_kernel(ta, tm, every, *refs):
    D = ta.shape[1]
    attn, mlp, norm, time = refs[0:3], refs[3:6], refs[6:9], refs[9:12]
    attn_out, mlp_out, norm_out, time_out = refs[12:16], refs[16:20], refs[20:23], refs[23:26]
    step = pl.program_id(0)
    is_inner, is_up = device_kinds()

    def update(olds, news, grad, rate):
        def visit(rows, cols, lines):
            values = adamw_low(*(old[lines, :] for old in olds), grad[rows, cols], rate)
            for new, value in zip(news, values):
                new[lines, :] = value

        return visit

    @pl.when(step == 0)
    def _():
        walk(is_inner, 3, ta.shape[0], D, update(attn, attn_out[:3], ta, 0.05))
        attn_out[3][...] = attn_out[0][...].astype(BF)
        total = every[0, :, 0:D]
        for i in range(1, every.shape[0]):
            total = total + every[i, :, 0:D]
        values = adamw_low(*(old[...] for old in norm), total[0:5], 0.2)
        for new, value in zip(norm_out, values):
            new[...] = value

    @pl.when(step == 1)
    def _():
        walk(is_up, FF // D, tm.shape[0], D, update(mlp, mlp_out[:3], tm, 0.03))
        mlp_out[3][...] = mlp_out[0][...].astype(BF)

    n = time[0].shape[0]
    rows = every.shape[0] * every.shape[1]
    tag = every[:, :, D : D + LANES].reshape(rows, LANES)[:, 0:1]
    at = (lax.broadcasted_iota(jnp.int32, (rows, n), 1) + step * n).astype(F32)
    chosen = jnp.where(tag == at, 1.0, 0.0).astype(BF)
    rest = every[:, :, 0:D].reshape(rows, D)
    grad = None
    for _ in range(3):
        low = rest.astype(BF)
        rest = rest - low.astype(F32)
        y = dot(chosen, low, TN)
        grad = y if grad is None else grad + y
    values = adamw_low(*(old[...] for old in time), grad, 0.3)
    for new, value in zip(time_out, values):
        new[...] = value


def fast(
    resid_in,
    mask,
    steps_row,
    cotangent,
    attn_master,
    attn_first,
    attn_second,
    mlp_master,
    mlp_first,
    mlp_second,
    norm_master,
    norm_first,
    norm_second,
    time_master,
    time_first,
    time_second,
):
    D = resid_in.shape[2]
    Z = lax.axis_size("seq")
    R = lax.axis_size("rows")
    S = resid_in.shape[0] // Z
    part = resid_in.shape[1]
    L = part * Z
    T = S * L
    V = pl.BlockSpec(memory_space=pltpu.VMEM)
    A = pl.BlockSpec(memory_space=pl.ANY)
    shape = jax.ShapeDtypeStruct
    dma = pltpu.SemaphoreType.DMA
    attn = [a.reshape(-1, LANES) for a in (attn_master, attn_first, attn_second)]
    mlp = [a.reshape(-1, LANES) for a in (mlp_master, mlp_first, mlp_second)]
    sa_shape = (attn_master.shape[0] // D, D)
    sm_shape = (mlp_master.shape[0] // D, D)
    sa, sm, mask_in, time_rows, tags = pl.pallas_call(
        functools.partial(before_kernel, S),
        out_shape=(
            shape(sa_shape, BF),
            shape(sm_shape, BF),
            shape((part, LANES), BF),
            shape((8, D), F32),
            shape((8, LANES), F32),
        ),
        in_specs=[pl.BlockSpec(memory_space=pltpu.SMEM), V, A, V, V],
        out_specs=(V,) * 5,
        scratch_shapes=[pltpu.VMEM((LANES, LANES), F32), dma((S,))],
        compiler_params=pltpu.CompilerParams(vmem_limit_bytes=63 << 20),
    )(steps_row, mask, time_master, attn[0], mlp[0])
    sc = layer_scratch(T, D, S, L)
    scratch = [
        pltpu.VMEM((GROUPS, *sa.shape), BF),
        pltpu.VMEM((GROUPS * 3 // 2, *sm.shape), BF),
        pltpu.VMEM((sm.shape[0] // sa.shape[0] * (4 * Z + 6 * (Z // 2) + Z - 1), *sa.shape), BF),
        pltpu.VMEM((T, D), BF),
        pltpu.VMEM((T, D), BF),
        pltpu.VMEM((L, LANES), BF),
        *(sc[n] for n in LAYER_REFS),
        pltpu.VMEM((R * Z, 8, D + LANES), F32),
        *(dma((2, n)) for n in (40, 40, 12)),
        *(dma((2, S * (Z - 1))) for _ in range(4)),
        dma((2, Z)),
        dma((5, S)),
        dma((2, 16)),
        dma((2, sm.shape[0] // sa.shape[0], 16)),
        pltpu.SemaphoreType.REGULAR,
        pltpu.VMEM((sa.shape[0] + sm.shape[0], D), F32),
    ]
    resid_out, grad_in, ta, tm, every = pl.pallas_call(
        functools.partial(whole_kernel, (Z, S, part)),
        out_shape=(
            shape(resid_in.shape, BF),
            shape(resid_in.shape, BF),
            shape(sa.shape, F32),
            shape(sm.shape, F32),
            shape((R * Z, 8, D + LANES), F32),
        ),
        in_specs=[A, A, A, V, V, V, A, A],
        out_specs=(A,) * 5,
        scratch_shapes=scratch,
        compiler_params=pltpu.CompilerParams(
            collective_id=0, has_side_effects=True, vmem_limit_bytes=63 << 20
        ),
    )(resid_in, cotangent, mask_in, time_rows, tags, norm_master, sa, sm)
    steps = 5
    norm = (norm_master, norm_first, norm_second)
    time = (time_master, time_first, time_second)
    rows = time_master.shape[0] // steps
    moving = pl.BlockSpec((rows, D), lambda i: (i, 0))

    def fixed(a):
        return pl.BlockSpec(a.shape, lambda i: (0,) * len(a.shape))

    outs = [shape(a.shape, F32) for a in attn] + [shape(attn[0].shape, BF)]
    outs += [shape(a.shape, F32) for a in mlp] + [shape(mlp[0].shape, BF)]
    outs += [shape(a.shape, F32) for a in norm]
    news = pl.pallas_call(
        after_kernel,
        grid=(steps,),
        out_shape=(*outs, *(shape(a.shape, F32) for a in time)),
        in_specs=[fixed(a) for a in (ta, tm, every, *attn, *mlp, *norm)] + [moving] * 3,
        out_specs=(*(fixed(a) for a in outs), *(moving,) * 3),
        compiler_params=pltpu.CompilerParams(vmem_limit_bytes=63 << 20),
    )(ta, tm, every, *attn, *mlp, *norm, *time)
    return (resid_out, grad_in, *(a.reshape(-1) for a in news[:8]), *news[8:])


def solution(mesh):
    flat, whole, tokens = P(("rows", "seq")), P(), P("rows", "seq", None)
    fits = mesh.shape["rows"] * mesh.shape["seq"] == GROUPS and mesh.shape["rows"] == 8
    return jax.shard_map(
        fast if fits else general,
        mesh=mesh,
        in_specs=(tokens, P("rows", "seq"), P("rows"), tokens) + (flat,) * 6 + (whole,) * 6,
        out_specs=(tokens, tokens) + (flat,) * 8 + (whole,) * 6,
        check_vma=False,
    )
```

```python
import functools

import jax
import jax.numpy as jnp
from jax import lax
from jax.experimental import pallas as pl
from jax.experimental.pallas import tpu as pltpu
from jax.sharding import PartitionSpec as P

HEAD_DIM = 64
FF = 3072
STEP = 10
NORM_EPSILON = 1e-05
GROUPS = 32
LANES = 128
TILE = 256
ROW_BLOCK = 64
GELU_C = 0.7978845608028654
GELU_A = 0.044715
LOG2E = 1.4426950408889634
BF = jnp.bfloat16
F32 = jnp.float32

NN = (((1,), (0,)), ((), ()))
NT = (((1,), (1,)), ((), ()))
TN = (((0,), (0,)), ((), ()))


def dot(a, b, dims=NN):
    return lax.dot_general(a, b, dims, preferred_element_type=F32)


def norm_stats(h):
    mean = jnp.mean(h, axis=-1, keepdims=True)
    centred = h - mean
    var = jnp.mean(centred * centred, axis=-1, keepdims=True)
    rs = lax.rsqrt(var + NORM_EPSILON)
    return centred * rs, rs


def fold(x):
    return jnp.sum(x.reshape(x.shape[0] // 8, 8, x.shape[1]), axis=0)


def add_small(small, which, x):
    small[which] = small[which] + fold(x)


class Layer:
    def __init__(self, **refs):
        self.__dict__.update(refs)
        self.T, self.D = self.h.shape
        self.L = self.mask.shape[0]
        self.S = self.T // self.L
        self.PAIRS = self.D // LANES
        self.NJ = FF // self.D

    def qkv_part(self, ref, j, c, n):
        rows = ref.shape[1] // 3
        used = self.D // rows
        return ref.at[pl.ds(0, used), pl.ds(pl.multiple_of(j * rows, rows), rows), pl.ds(pl.multiple_of(c, n), n)]

    def out_part(self, ref, c, n):
        rows = ref.shape[1]
        used = self.D // rows
        return ref.at[pl.ds(ref.shape[0] - used, used), :, pl.ds(pl.multiple_of(c, n), n)]

    def up_part(self, ref, j, c, n):
        rows = ref.shape[1] // self.NJ
        used = self.D // rows
        return ref.at[pl.ds(0, used), pl.ds(pl.multiple_of(j * rows, rows), rows), pl.ds(pl.multiple_of(c, n), n)]

    def down_part(self, ref, j, c, n):
        rows = ref.shape[1]
        used = self.D // rows
        return ref.at[pl.ds(ref.shape[0] // 2 + j * used, used), :, pl.ds(pl.multiple_of(c, n), n)]

    def mask_col(self, s, base, n):
        m = self.mask[pl.ds(base, n), :].astype(F32)
        lane = lax.broadcasted_iota(jnp.int32, m.shape, 1)
        return jnp.sum(jnp.where(lane == self.lane + s, m, 0.0), axis=-1, keepdims=True)

    def embed(self, s):
        def body(i, _):
            base = pl.multiple_of(i * ROW_BLOCK, ROW_BLOCK)
            rows = pl.ds(pl.multiple_of(s * self.L + base, ROW_BLOCK), ROW_BLOCK)
            m = self.mask_col(s, base, ROW_BLOCK)
            h = self.x[rows, :].astype(F32) + m * self.norm[4:5, :] + self.time[s : s + 1, :]
            self.h[rows, :] = h
            xhat, _ = norm_stats(h)
            self.n1[rows, :] = (xhat * self.norm[0:1, :] + self.norm[1:2, :]).astype(BF)
            return 0

        lax.fori_loop(0, self.L // ROW_BLOCK, body, 0)

    def project(self, s):
        per = self.D // TILE
        rows = pl.ds(s * self.L, self.L)

        def body(i, _):
            j, c = lax.div(i, per), lax.rem(i, per) * TILE
            w = self.qkv_part(self.wa, j, c, TILE)[...].reshape(self.D, TILE)
            y = dot(self.n1[rows, :], w)
            self.qkv[rows, pl.ds(pl.multiple_of(i * TILE, TILE), TILE)] = y.astype(BF)
            return 0

        lax.fori_loop(0, 3 * per, body, 0)

    def pair_slices(self, s, p):
        rows = pl.ds(pl.multiple_of(s * self.L, self.L), self.L)
        cols = [pl.ds(pl.multiple_of(k * self.D + p * LANES, LANES), LANES) for k in range(3)]
        return rows, cols

    def half(self, x, hh):
        first = lax.broadcasted_iota(jnp.int32, x.shape, 1) < HEAD_DIM
        zero = jnp.zeros_like(x)
        return jnp.where(first, zero, x) if hh else jnp.where(first, x, zero)

    def attend(self, s, p):
        rows, cols = self.pair_slices(s, p)
        q, k, v = (self.qkv[rows, c] for c in cols)
        total = None
        for hh in range(2):
            sc = dot(self.half(q, hh), k, NT)
            top = jnp.max(sc, axis=-1, keepdims=True)
            e = jnp.exp2((sc - top) * (HEAD_DIM**-0.5 * LOG2E))
            w = (e * (1.0 / jnp.sum(e, axis=-1, keepdims=True))).astype(BF)
            self.soft[s * 2 * self.PAIRS + p * 2 + hh] = w
            o = dot(w, self.half(v, hh))
            total = o if total is None else total + o
        self.att[rows, cols[0]] = total.astype(BF)

    def attend_sequence(self, s):
        def body(p, _):
            self.attend(s, p)
            return 0

        lax.fori_loop(0, self.PAIRS, body, 0)

    def outer(self, s):
        rows = pl.ds(s * self.L, self.L)

        def body(i, _):
            c = i * TILE
            cols = pl.ds(pl.multiple_of(c, TILE), TILE)
            w = self.out_part(self.wa, c, TILE)[...].reshape(self.D, TILE)
            self.mid[rows, cols] = self.h[rows, cols] + dot(self.att[rows, :], w)
            return 0

        lax.fori_loop(0, self.D // TILE, body, 0)

    def second_norm(self, s):
        def body(i, _):
            rows = pl.ds(pl.multiple_of(s * self.L + i * ROW_BLOCK, ROW_BLOCK), ROW_BLOCK)
            xhat, _ = norm_stats(self.mid[rows, :])
            self.n2[rows, :] = (xhat * self.norm[2:3, :] + self.norm[3:4, :]).astype(BF)
            return 0

        lax.fori_loop(0, self.L // ROW_BLOCK, body, 0)

    def up(self):
        per = self.D // TILE

        def body(i, _):
            j, c = lax.div(i, per), lax.rem(i, per) * TILE
            cols = pl.ds(pl.multiple_of(i * TILE, TILE), TILE)
            w = self.up_part(self.wm, j, c, TILE)[...].reshape(self.D, TILE)
            for s in range(self.S):
                rows = pl.ds(s * self.L, self.L)
                u = dot(self.n2[rows, :], w)
                uu = u * u
                t = jnp.tanh(GELU_C * (u * (1.0 + GELU_A * uu)))
                left = 0.5 * (1.0 + t)
                self.act[pl.ds(pl.multiple_of(j * self.T + s * self.L, self.L), self.L), pl.ds(pl.multiple_of(c, TILE), TILE)] = (u * left).astype(BF)
                slope = left + (0.5 * GELU_C) * u * (1.0 - t * t) * (1.0 + 3.0 * GELU_A * uu)
                self.du[rows, cols] = slope.astype(BF)
            return 0

        lax.fori_loop(0, self.NJ * per, body, 0)

    def down(self):
        per = self.D // TILE

        def body(i, _):
            c = i * TILE
            cols = pl.ds(pl.multiple_of(c, TILE), TILE)
            for s in range(self.S):
                rows = pl.ds(s * self.L, self.L)
                total = self.mid[rows, cols]
                for j in range(self.NJ):
                    w = self.down_part(self.wm, j, c, TILE)[...].reshape(self.D, TILE)
                    total = total + dot(self.act[pl.ds(j * self.T + s * self.L, self.L), :], w)
                self.out[rows, cols] = total.astype(BF)
            return 0

        lax.fori_loop(0, per, body, 0)

    def mask_cotangent(self):
        for s in range(self.S):
            def body(i, _, s=s):
                base = pl.multiple_of(i * ROW_BLOCK, ROW_BLOCK)
                rows = pl.ds(pl.multiple_of(s * self.L + base, ROW_BLOCK), ROW_BLOCK)
                m = self.mask_col(s, base, ROW_BLOCK)
                self.g[rows, :] = (self.g[rows, :].astype(F32) * m).astype(BF)
                return 0

            lax.fori_loop(0, self.L // ROW_BLOCK, body, 0)

    def grad_pre(self):
        per = self.D // TILE

        def body(i, _):
            cols = pl.ds(pl.multiple_of(i * (self.D // 2), self.D // 2), self.D // 2)
            rows_w = self.wm.shape[1]
            used = self.D // 2 // rows_w
            w = self.wm[pl.ds(self.wm.shape[0] // 2 + i * used, used)].reshape(self.D // 2, self.D)
            for s in range(self.S):
                rows = pl.ds(s * self.L, self.L)
                d = dot(self.g[rows, :], w, NT)
                self.du[rows, cols] = (d * self.du[rows, cols].astype(F32)).astype(BF)
            return 0

        lax.fori_loop(0, 2 * self.NJ, body, 0)

    def turn_activated(self):
        for j in range(self.NJ):
            rows = pl.ds(j * self.T, self.T)
            self.turn[...] = self.act[rows, :].T
            self.act[rows, :] = self.turn[...]
        self.turn[...] = self.n2[...].T

    def grad_down(self, part, parts):
        group = self.gm_down.shape[1]
        used = self.D // group
        n = group // parts
        per = self.D // TILE

        def body(i, _):
            j, c = lax.div(i, per), pl.multiple_of(lax.rem(i, per) * TILE, TILE)
            a = jnp.concatenate(
                [
                    self.act[pl.ds(pl.multiple_of(j * self.D + u * group + part * n, 16), n), :]
                    for u in range(used)
                ]
            )
            y = dot(a, self.g[:, pl.ds(c, TILE)]).astype(BF)
            ref = self.gm_down.at[pl.ds(self.gm_down.shape[0] // 2 + j * used, used), pl.ds(part * n, n), pl.ds(c, TILE)]
            ref[...] = y.reshape(used, n, TILE)
            return 0

        lax.fori_loop(0, self.NJ * per, body, 0)

    def grad_up(self, part, parts):
        per = self.D // TILE
        n = self.NJ * per // parts

        def body(i, _):
            j, c = lax.div(i, per), lax.rem(i, per) * TILE
            y = dot(self.turn[...], self.du[:, pl.ds(pl.multiple_of(i * TILE, TILE), TILE)])
            ref = self.up_part(self.gm_up, j, c, TILE)
            ref[...] = y.astype(BF).reshape(ref.shape)
            return 0

        lax.fori_loop(part * n, (part + 1) * n, body, 0)

    def grad_normed_two(self):
        rows_w = self.wm.shape[1] // self.NJ
        n = self.D // 2
        used = n // rows_w

        def body(i, _):
            cols = pl.ds(pl.multiple_of(i * n, n), n)
            for s in range(self.S):
                rows = pl.ds(s * self.L, self.L)
                total = None
                for j in range(self.NJ):
                    w = self.wm[pl.ds(i * used, used), pl.ds(j * rows_w, rows_w), :].reshape(n, self.D)
                    y = dot(self.du[rows, pl.ds(j * self.D, self.D)], w, NT)
                    total = y if total is None else total + y
                self.dn[rows, cols] = total
            return 0

        lax.fori_loop(0, 2, body, 0)

    def norm_two_back(self):
        def body(i, _):
            rows = pl.ds(pl.multiple_of(i * ROW_BLOCK, ROW_BLOCK), ROW_BLOCK)
            xhat, rs = norm_stats(self.mid[rows, :])
            dy = self.dn[rows, :]
            add_small(self.small, 2, dy * xhat)
            add_small(self.small, 3, dy)
            e = dy * self.norm[2:3, :]
            back = (e - jnp.mean(e, -1, keepdims=True) - xhat * jnp.mean(e * xhat, -1, keepdims=True)) * rs
            gm = self.g[rows, :].astype(F32) + back
            self.dn[rows, :] = gm
            self.gb[rows, :] = gm.astype(BF)
            return 0

        lax.fori_loop(0, self.T // ROW_BLOCK, body, 0)

    def grad_outer(self):
        self.turn[...] = self.att[...].T

        def body(i, _):
            c = pl.multiple_of(i * TILE, TILE)
            y = dot(self.turn[...], self.gb[:, pl.ds(c, TILE)])
            ref = self.out_part(self.ga, c, TILE)
            ref[...] = y.astype(BF).reshape(ref.shape)
            return 0

        lax.fori_loop(0, self.D // TILE, body, 0)

    def grad_attended(self):
        n = self.D // 2
        rows_w = self.wa.shape[1]
        used = n // rows_w
        first = self.wa.shape[0] - 2 * used

        def body(i, _):
            w = self.wa[pl.ds(first + i * used, used)].reshape(n, self.D)
            for s in range(self.S):
                rows = pl.ds(s * self.L, self.L)
                self.att[rows, pl.ds(pl.multiple_of(i * n, n), n)] = dot(self.gb[rows, :], w, NT).astype(BF)
            return 0

        lax.fori_loop(0, 2, body, 0)

    def attend_back(self, s, p):
        rows, cols = self.pair_slices(s, p)
        q, k, v = (self.qkv[rows, c] for c in cols)
        da = self.att[rows, cols[0]]
        dq = dk = dv = None
        for hh in range(2):
            w = self.soft[s * 2 * self.PAIRS + p * 2 + hh]
            da_h = self.half(da, hh)
            dp = dot(da_h, v, NT)
            wf = w.astype(F32)
            t = wf * dp
            ds = (t - wf * jnp.sum(t, axis=-1, keepdims=True)).astype(BF)
            parts = (dot(ds, self.half(k, hh)), dot(ds, self.half(q, hh), TN), dot(w, da_h, TN))
            dq, dk, dv = parts if dq is None else (dq + parts[0], dk + parts[1], dv + parts[2])
        scale = HEAD_DIM**-0.5
        self.qkv[rows, cols[0]] = (dq * scale).astype(BF)
        self.qkv[rows, cols[1]] = (dk * scale).astype(BF)
        self.qkv[rows, cols[2]] = dv.astype(BF)

    def attend_back_sequence(self, s):
        def body(p, _):
            self.attend_back(s, p)
            return 0

        lax.fori_loop(0, self.PAIRS, body, 0)

    def grad_normed_one(self, s):
        n = self.D // 3
        rows_w = self.wa.shape[1] // 3
        used = n // rows_w
        rows = pl.ds(s * self.L, self.L)

        def body(i, _):
            total = None
            for j in range(3):
                w = self.wa[pl.ds(i * used, used), pl.ds(j * rows_w, rows_w), :].reshape(n, self.D)
                y = dot(self.qkv[rows, pl.ds(j * self.D, self.D)], w, NT)
                total = y if total is None else total + y
            self.mid[rows, pl.ds(pl.multiple_of(i * n, n), n)] = total
            return 0

        lax.fori_loop(0, 3, body, 0)

    def norm_one_back(self, s):
        def body(i, _):
            base = pl.multiple_of(i * ROW_BLOCK, ROW_BLOCK)
            rows = pl.ds(pl.multiple_of(s * self.L + base, ROW_BLOCK), ROW_BLOCK)
            xhat, rs = norm_stats(self.h[rows, :])
            dy = self.mid[rows, :]
            add_small(self.small, 0, dy * xhat)
            add_small(self.small, 1, dy)
            e = dy * self.norm[0:1, :]
            back = (e - jnp.mean(e, -1, keepdims=True) - xhat * jnp.mean(e * xhat, -1, keepdims=True)) * rs
            gs = self.dn[rows, :] + back
            add_small(self.small, 5 + s, gs)
            add_small(self.small, 4, gs * self.mask_col(s, base, ROW_BLOCK))
            self.x[rows, :] = gs.astype(BF)
            return 0

        lax.fori_loop(0, self.L // ROW_BLOCK, body, 0)

    def grad_inner(self):
        per = self.D // TILE
        self.turn[...] = self.n1[...].T

        def body(i, _):
            j, c = lax.div(i, per), lax.rem(i, per) * TILE
            y = dot(self.turn[...], self.qkv[:, pl.ds(pl.multiple_of(i * TILE, TILE), TILE)])
            ref = self.qkv_part(self.ga, j, c, TILE)
            ref[...] = y.astype(BF).reshape(ref.shape)
            return 0

        lax.fori_loop(0, 3 * per, body, 0)


def run_all(k):
    for i in range(8):
        k.small[i] = jnp.zeros(k.small.shape[1:], F32)
    for s in range(k.S):
        k.embed(s)
        k.project(s)
        k.attend_sequence(s)
        k.outer(s)
        k.second_norm(s)
    k.up()
    k.down()
    k.mask_cotangent()
    k.grad_pre()
    k.turn_activated()
    k.grad_down(0, 1)
    k.grad_up(0, 1)
    k.grad_normed_two()
    k.norm_two_back()
    k.grad_outer()
    k.grad_attended()
    for s in range(k.S):
        k.attend_back_sequence(s)
        k.grad_normed_one(s)
        k.norm_one_back(s)
    k.grad_inner()


def flip(index, bit):
    return index + bit - 2 * bit * lax.rem(lax.div(index, bit), 2)


def pick(table, index):
    value = table[0]
    for i in range(1, len(table)):
        value = jnp.where(index == i, table[i], value)
    return value


class Links:
    def __init__(self, Z, S, part):
        self.Z, self.S, self.part = Z, S, part
        self.r, self.z = lax.axis_index("rows"), lax.axis_index("seq")
        r = self.r
        self.core, self.xn, self.yn = flip(r, 1), flip(r, 2), flip(r, 4)
        self.diag = flip(self.xn, 4)
        self.pending = []
        near, far = flip(self.z, 1), flip(self.z, 2)
        self.near, self.far = near, far
        self.order = [self.z, near, far, flip(near, 2)]

    def barrier(self):
        bar = pltpu.get_barrier_semaphore()
        peers = [(self.core, self.z), (self.xn, self.z), (self.yn, self.z)]
        peers += [(self.r, lax.rem(self.z + i, self.Z)) for i in range(1, self.Z)]
        for peer in peers:
            pl.semaphore_signal(bar, 1, device_id=peer, device_id_type=pl.DeviceIdType.MESH)
        pl.semaphore_wait(bar, len(peers))

    def send(self, src, dst, ss, rs, peer, cond=None, owner=None):
        copy = pltpu.make_async_remote_copy(
            src, dst, ss, rs, device_id=peer, device_id_type=pl.DeviceIdType.MESH
        )
        if cond is None:
            copy.start()
        else:
            pl.when(cond)(copy.start)
        self.pending.append((owner, cond, copy))

    def arrived(self, dst, rs, cond=None):
        copy = pltpu.make_async_remote_copy(
            dst, dst, rs, rs, device_id=(self.core, self.z), device_id_type=pl.DeviceIdType.MESH
        )
        if cond is None:
            copy.wait_recv()
        else:
            pl.when(cond)(copy.wait_recv)

    def flush(self, src=None):
        left = []
        for item in self.pending:
            owner, cond, copy = item
            if src is not None and owner is not src:
                left.append(item)
            elif cond is None:
                copy.wait_send()
            else:
                pl.when(cond)(copy.wait_send)
        self.pending = left

    def gather(self, w, ss, rs):
        Z, z = self.Z, self.z
        count = [0]

        def go(row, zz, peer, cond=None):
            i = row * Z + zz
            self.send(w.at[i], w.at[i], ss.at[count[0]], rs.at[i], peer, cond, w)
            count[0] += 1

        def got(row, zz):
            i = row * Z + zz
            self.arrived(w.at[i], rs.at[i])

        def own(i):
            zz = self.order[i]
            if i:
                got(self.r, zz)
            if i == 0:
                go(self.r, zz, (self.r, self.far))
            if i == 0 or i == 2:
                go(self.r, zz, (self.r, self.near))
            go(self.r, zz, (self.xn, z))
            go(self.r, zz, (self.yn, z))
            go(self.r, zz, (self.core, z))

        def side(i):
            zz = self.order[i]
            got(self.xn, zz)
            if i % 2 == 0:
                go(self.xn, zz, (self.yn, z))
            go(self.xn, zz, (self.core, z))
            got(self.yn, zz)
            if i % 2 == 1:
                go(self.yn, zz, (self.xn, z))
            go(self.yn, zz, (self.core, z))

        def far(i):
            zz = self.order[i]
            got(self.diag, zz)
            go(self.diag, zz, (self.core, z))

        def last():
            for row in (self.r, self.xn, self.yn, self.diag):
                for i in range(Z):
                    got(flip(row, 1), self.order[i])

        return own, side, far, last

    def gather_small(self, w, ss, rs):
        Z, z = self.Z, self.z
        half = Z // 2

        def block(row, lo=0, n=Z):
            return w.at[pl.ds(row * Z + lo, n)]

        def go(ref, n, peer):
            self.send(ref, ref, ss.at[n], rs.at[n], peer)

        def along_z():
            for step in range(1, Z):
                go(block(self.r, z, 1), step, (self.r, lax.rem(z + step, Z)))

        def spread():
            for step in range(1, Z):
                self.arrived(block(self.r, lax.rem(z + Z - step, Z), 1), rs.at[step])
            go(block(self.r), 4, (self.xn, z))
            go(block(self.r), 5, (self.yn, z))
            go(block(self.r), 6, (self.core, z))

        def forward():
            self.arrived(block(self.xn), rs.at[4])
            go(block(self.xn, 0, half), 7, (self.yn, z))
            self.arrived(block(self.yn), rs.at[5])
            go(block(self.yn, half, half), 8, (self.xn, z))
            go(block(self.xn), 9, (self.core, z))
            go(block(self.yn), 10, (self.core, z))

        def corner():
            self.arrived(block(self.diag, 0, half), rs.at[7])
            self.arrived(block(self.diag, half, half), rs.at[8])
            go(block(self.diag), 11, (self.core, z))

        def last():
            self.arrived(block(self.core), rs.at[6])
            self.arrived(block(flip(self.xn, 1)), rs.at[9])
            self.arrived(block(flip(self.yn, 1)), rs.at[10])
            self.arrived(block(flip(self.diag, 1)), rs.at[11])

        return along_z, spread, forward, corner, last

    def exchange_in(self, src, dst, ss, rs, local, seqs):
        L = self.part * self.Z
        for i in seqs:
            for step in range(1, self.Z):
                to = lax.rem(self.z + step, self.Z)
                rows = pl.ds(i * L + self.z * self.part, self.part)
                n = i * (self.Z - 1) + step - 1
                self.send(src.at[to * self.S + i], dst.at[rows], ss.at[n], rs.at[n], (self.r, to))
            rows = pl.ds(i * L + self.z * self.part, self.part)
            pltpu.make_async_copy(src.at[self.z * self.S + i], dst.at[rows], local.at[i]).start()

    def exchange_in_done(self, src, dst, rs, local, i):
        L = self.part * self.Z
        for step in range(1, self.Z):
            source = lax.rem(self.z + self.Z - step, self.Z)
            rows = pl.ds(i * L + source * self.part, self.part)
            self.arrived(dst.at[rows], rs.at[i * (self.Z - 1) + step - 1])
        rows = pl.ds(i * L + self.z * self.part, self.part)
        pltpu.make_async_copy(src.at[self.z * self.S + i], dst.at[rows], local.at[i]).wait()

    def exchange_out(self, src, dst, ss, rs, local, i):
        L = self.part * self.Z
        for step in range(1, self.Z):
            to = lax.rem(self.z + step, self.Z)
            rows = pl.ds(i * L + to * self.part, self.part)
            n = i * (self.Z - 1) + step - 1
            self.send(src.at[rows], dst.at[self.z * self.S + i], ss.at[n], rs.at[n], (self.r, to), None, dst)
        rows = pl.ds(i * L + self.z * self.part, self.part)
        pltpu.make_async_copy(src.at[rows], dst.at[self.z * self.S + i], local.at[i]).start()

    def exchange_out_done(self, src, dst, rs, local, i):
        L = self.part * self.Z
        for step in range(1, self.Z):
            source = lax.rem(self.z + self.Z - step, self.Z)
            self.arrived(dst.at[source * self.S + i], rs.at[i * (self.Z - 1) + step - 1])
        rows = pl.ds(i * L + self.z * self.part, self.part)
        pltpu.make_async_copy(src.at[rows], dst.at[self.z * self.S + i], local.at[i]).wait()

    def scatter(self, g, base, part, inbox, box0, ss, rs, total):
        Z, z = self.Z, self.z
        half = Z // 2
        chip = lax.div(self.r, 2)
        k = lax.rem(self.r, 2)
        cx, cy = flip(chip, 1), flip(chip, 2)
        cd = flip(cx, 2)
        rows = total.shape[0]

        def block(c, parity, lo, n):
            return g.at[pl.ds(base + (2 * c + parity) * Z + lo, n), pl.ds(part * rows, rows)]

        def inslot(i, n):
            return inbox.at[pl.ds(box0 + i, n)]

        def add(dst, src, n):
            def body(i, _):
                dst[i] = (dst[i].astype(F32) + src[i].astype(F32)).astype(BF)
                return 0

            lax.fori_loop(0, n, body, 0)

        XY = 4 * Z
        ZB = XY + 6 * half

        def core_send_all():
            for c in range(4):
                core_send(c)

        def core_send(c):
            self.send(block(c, 1 - k, 0, Z), inslot(c * Z, Z), ss.at[c], rs.at[c], (self.core, z))

        def core_add(c):
            self.arrived(inslot(c * Z, Z), rs.at[c])
            add(block(c, k, 0, Z), inslot(c * Z, Z), Z)

        def xy_send(slot, c, lo, peer):
            i = XY + slot * half
            self.send(block(c, k, lo, half), inslot(i, half), ss.at[4 + slot], rs.at[4 + slot], (peer, z))

        def xy_add(slot, c, lo):
            i = XY + slot * half
            self.arrived(inslot(i, half), rs.at[4 + slot])
            add(block(c, k, lo, half), inslot(i, half), half)

        def first():
            core_add(cd)
            xy_send(0, cd, 0, self.xn)
            xy_send(2, cd, half, self.yn)
            core_add(cx)
            xy_send(1, cx, 0, self.xn)
            core_add(cy)
            xy_send(3, cy, half, self.yn)
            core_add(chip)

        def second():
            xy_add(0, cy, 0)
            xy_send(4, cy, 0, self.yn)
            xy_add(2, cx, half)
            xy_send(5, cx, half, self.xn)

        def second_own():
            xy_add(1, chip, 0)
            xy_add(3, chip, half)

        def third():
            xy_add(4, chip, 0)
            xy_add(5, chip, half)

        def z_send(slot, target, peer):
            box = inslot(ZB + slot, 1)
            self.send(block(chip, k, target, 1), box, ss.at[10 + slot], rs.at[10 + slot], (self.r, peer))

        def z_first():
            z_send(1, self.order[3], self.near)
            z_send(0, self.near, self.near)

        def z_second():
            self.arrived(inslot(ZB + 1, 1), rs.at[11])
            add(block(chip, k, self.far, 1), inslot(ZB + 1, 1), 1)
            z_send(2, self.far, self.far)

        def final():
            self.arrived(inslot(ZB, 1), rs.at[10])
            total[...] = block(chip, k, z, 1)[0].astype(F32) + inbox[box0 + ZB].astype(F32)
            self.arrived(inslot(ZB + 2, 1), rs.at[12])
            total[...] += inbox[box0 + ZB + 2].astype(F32)

        return core_send_all, first, second, second_own, third, z_first, z_second, final


def compute_kernel(x, mask, g_in, time, norm, wa, wm, out, gin, ga, gm, small, *scratch):
    names = ("g", "h", "n1", "qkv", "att", "mid", "n2", "act", "du", "soft", "dn", "gb", "turn", "sums")
    refs = dict(zip(names, scratch))
    sums = refs.pop("sums")
    pltpu.sync_copy(x, gin)
    pltpu.sync_copy(g_in, refs["g"])
    layer = Layer(
        x=gin, mask=mask, time=time, norm=norm, wa=wa, wm=wm, out=out, ga=ga, gm_down=gm, gm_up=gm, small=sums, lane=0, **refs
    )
    run_all(layer)
    for i in range(8):
        small[i : i + 1, :] = jnp.sum(sums[i], axis=0, keepdims=True)


def layer_scratch(T, D, S, L):
    heads = D // HEAD_DIM
    return dict(
        h=pltpu.VMEM((T, D), F32),
        n1=pltpu.VMEM((T, D), BF),
        qkv=pltpu.VMEM((T, 3 * D), BF),
        att=pltpu.VMEM((T, D), BF),
        mid=pltpu.VMEM((T, D), F32),
        n2=pltpu.VMEM((T, D), BF),
        act=pltpu.VMEM((FF // D * T, D), BF),
        du=pltpu.VMEM((T, FF), BF),
        soft=pltpu.VMEM((S * heads, L, L), BF),
        dn=pltpu.VMEM((T, D), F32),
        gb=pltpu.VMEM((T, D), BF),
        turn=pltpu.VMEM((D, D), BF),
        sums=pltpu.VMEM((8, 8, D), F32),
    )


def pad_rows(x):
    return jnp.pad(x, ((0, 8 - x.shape[0]), (0, 0)))


def rows_split(flat, groups, parts, D):
    return flat.reshape(groups, -1, parts, D).transpose(0, 2, 1, 3).reshape(groups, -1, D)


def rows_join(block, parts, D):
    groups = block.shape[0]
    return block.reshape(groups, parts, -1, D).transpose(0, 2, 1, 3).reshape(-1)


def adamw(master, moment_one, moment_two, gradient, step_rate):
    first_new = 0.5 * moment_one + 0.5 * gradient
    second_new = 0.5 * moment_two + 0.5 * gradient * gradient
    correct = 1.0 - 0.5**STEP
    update = first_new / correct / (jnp.sqrt(second_new / correct) + 1e-08)
    return (master - step_rate * (update + 0.1 * master), first_new, second_new)


def general(
    resid_in,
    mask,
    steps_row,
    cotangent,
    attn_master,
    attn_first,
    attn_second,
    mlp_master,
    mlp_first,
    mlp_second,
    norm_master,
    norm_first,
    norm_second,
    time_master,
    time_first,
    time_second,
):
    D = resid_in.shape[2]
    axes = ("rows", "seq")
    seq_count = lax.axis_size("seq")
    S = resid_in.shape[0] // seq_count
    L = resid_in.shape[1] * seq_count
    T = S * L
    attn_full = lax.all_gather(attn_master.astype(BF), axes, axis=0, tiled=True)
    mlp_full = lax.all_gather(mlp_master.astype(BF), axes, axis=0, tiled=True)
    inner = 3 * D * D
    wide = D * FF
    wa = jnp.concatenate(
        (rows_split(attn_full[:inner], 24, 3, D), attn_full[inner:].reshape(8, -1, D))
    )
    wm = jnp.concatenate((rows_split(mlp_full[:wide], 16, FF // D, D), mlp_full[wide:].reshape(16, -1, D)))
    exchange = functools.partial(lax.all_to_all, axis_name="seq", split_axis=0, concat_axis=1, tiled=True)
    x = exchange(resid_in).reshape(T, D)
    g = exchange(cotangent).reshape(T, D)
    mask_t = jnp.pad(exchange(mask.astype(BF)).T, ((0, 0), (0, LANES - S)))
    steps_use = lax.dynamic_slice_in_dim(steps_row, lax.axis_index("seq") * S, S, 0)
    time_rows = pad_rows(jnp.take(time_master, steps_use, axis=0))
    V = pl.BlockSpec(memory_space=pltpu.VMEM)
    A = pl.BlockSpec(memory_space=pl.ANY)
    shape = jax.ShapeDtypeStruct
    scratch = layer_scratch(T, D, S, L)
    out, gin, ga, gm, small = pl.pallas_call(
        compute_kernel,
        out_shape=(shape((T, D), BF), shape((T, D), BF), shape(wa.shape, BF), shape(wm.shape, BF), shape((8, D), F32)),
        in_specs=[A, V, A, V, V, V, V],
        out_specs=(V,) * 5,
        scratch_shapes=[pltpu.VMEM((T, D), BF)] + list(scratch.values()),
        compiler_params=pltpu.CompilerParams(vmem_limit_bytes=62 << 20),
    )(x, mask_t, g, time_rows, pad_rows(norm_master), wa, wm)
    attn_flat = jnp.concatenate((rows_join(ga[:24], 3, D), ga[24:].reshape(-1))).astype(F32)
    mlp_flat = jnp.concatenate((rows_join(gm[:16], FF // D, D), gm[16:].reshape(-1))).astype(F32)
    attn_grad = lax.psum_scatter(attn_flat, axes, scatter_dimension=0, tiled=True)
    mlp_grad = lax.psum_scatter(mlp_flat, axes, scatter_dimension=0, tiled=True)
    every = lax.all_gather(small, axes, axis=0)
    spread = functools.partial(lax.all_to_all, axis_name="seq", split_axis=1, concat_axis=0, tiled=True)
    return finish(
        spread(out.reshape(S, L, D)),
        spread(gin.reshape(S, L, D)),
        lax.all_gather(steps_row, "rows", axis=0, tiled=True),
        every,
        adamw(attn_master, attn_first, attn_second, attn_grad, 0.05),
        adamw(mlp_master, mlp_first, mlp_second, mlp_grad, 0.03),
        (norm_master, norm_first, norm_second),
        (time_master, time_first, time_second),
        S,
    )


def finish(resid_out, grad_in, steps, every, attn, mlp, norm, time, S):
    D = every.shape[2]
    norm_grad = jnp.sum(every[:, :5], axis=0)
    chosen = (jnp.arange(time[0].shape[0], dtype=jnp.int32)[:, None] == steps[None, :]).astype(F32)
    time_grad = jnp.dot(chosen, every[:, 5 : 5 + S].reshape(-1, D), precision=lax.Precision.HIGHEST)
    return (
        resid_out,
        grad_in,
        *attn,
        attn[0].astype(BF),
        *mlp,
        mlp[0].astype(BF),
        *adamw(*norm, norm_grad, 0.2),
        *adamw(*time, time_grad, 0.3),
    )


LAYER_REFS = ("h", "n1", "qkv", "att", "mid", "n2", "act", "du", "soft", "dn", "turn", "sums")


def whole_kernel(
    cfg, resid, cot, mask_in, time, tags, norm, sa, sm, resid_out, grad_in, ta, tm, every_out, *scratch
):
    Z, S, part = cfg
    names = (
        "wa", "wm", "inbox", "x", "g", "mask", "h", "n1",
        "qkv", "att", "mid", "n2", "act", "du", "soft", "dn",
        "turn", "sums", "every", "sem_a", "sem_m", "sem_e", "sem_in", "sem_cot",
        "sem_out", "sem_gin", "sem_mask", "loc", "sem_ra", "sem_rm", "credit", "total",
    )
    v = dict(zip(names, scratch))
    wm, ga = v["wm"], v["act"].reshape(GROUPS, v["wa"].shape[1], v["wa"].shape[2])
    half = GROUPS // 2
    grads = wm.at[pl.ds(half, GROUPS)]
    k = Layer(
        x=v["x"], out=v["x"], g=v["g"], mask=v["mask"], time=time, norm=norm, wa=v["wa"], wm=wm.at[pl.ds(0, GROUPS)],
        ga=ga, gm_up=grads, gm_down=grads, small=v["sums"], gb=v["n2"], lane=lax.axis_index("seq") * S,
        **{n: v[n] for n in LAYER_REFS[:-1]},
    )
    net = Links(Z, S, part)
    me = net.r * Z + net.z
    loc = v["loc"]
    own_a = pltpu.make_async_copy(sa, v["wa"].at[me], loc.at[4, 0])
    own_m = pltpu.make_async_copy(sm, wm.at[me], loc.at[4, 1])
    own_a.start()
    own_m.start()
    for i in range(8):
        k.small[i] = jnp.zeros(k.small.shape[1:], F32)
    net.barrier()
    own_a.wait()
    own_m.wait()

    def pair(name):
        return v[name].at[0], v[name].at[1]

    def pump(events, n=1):
        for _ in range(n):
            if events:
                events.pop(0)()

    a_own, a_side, a_far, a_last = net.gather(v["wa"], *pair("sem_a"))
    m_own, m_side, m_far, m_last = net.gather(wm, *pair("sem_m"))

    def stream(s):
        net.exchange_in(resid, k.x, *pair("sem_in"), loc.at[0], [s])

    a_own(0)
    m_own(0)
    for step in range(1, Z):
        to = lax.rem(net.z + step, Z)
        rows = pl.ds(net.z * part, part)
        net.send(mask_in, k.mask.at[rows], v["sem_mask"].at[0, step], v["sem_mask"].at[1, step], (net.r, to))
    own_mask = pltpu.make_async_copy(mask_in, k.mask.at[pl.ds(net.z * part, part)], loc.at[4, 2])
    own_mask.start()
    a_own(1)
    a_side(0)
    a_own(2)
    stream(0)
    a_side(1)
    a_far(0)
    m_own(1)
    a_own(3)
    a_side(2)
    a_far(1)
    m_side(0)
    m_own(2)
    stream(1)
    a_side(3)
    a_far(2)
    stream(2)
    a_far(3)
    a_last()
    net.exchange_in(cot, k.g, *pair("sem_cot"), loc.at[1], range(S))
    rm = [
        functools.partial(m_side, 1),
        functools.partial(m_own, 3),
        functools.partial(m_far, 0),
        functools.partial(m_side, 2),
        functools.partial(m_far, 1),
        functools.partial(m_side, 3),
        functools.partial(m_far, 2),
        functools.partial(m_far, 3),
        m_last,
    ]
    own_mask.wait()
    for step in range(1, Z):
        source = lax.rem(net.z + Z - step, Z)
        net.arrived(k.mask.at[pl.ds(source * part, part)], v["sem_mask"].at[1, step])

    for s in range(S):
        net.exchange_in_done(resid, k.x, v["sem_in"].at[1], loc.at[0], s)
        k.embed(s)
        pump(rm)
        k.project(s)
        pump(rm)
        k.attend_sequence(s)
        pump(rm)
        k.outer(s)
        k.second_norm(s)
    pump(rm, len(rm))
    k.up()
    k.down()
    for s in range(S):
        net.exchange_out(k.out, resid_out, *pair("sem_out"), loc.at[2], s)
    for s in range(S):
        net.exchange_in_done(cot, k.g, v["sem_cot"].at[1], loc.at[1], s)
    k.mask_cotangent()
    k.grad_pre()
    net.flush(wm)
    k.turn_activated()
    rows = sa.shape[0]
    parts = sm.shape[0] // rows
    boxes = v["inbox"].shape[0] // parts
    totals = [v["total"].at[pl.ds(p * rows, rows)] for p in range(parts + 1)]
    pieces = [
        net.scatter(wm, half, p, v["inbox"], p * boxes, v["sem_rm"].at[0, p], v["sem_rm"].at[1, p], totals[p])
        for p in range(parts)
    ]
    (p_core, p_first, p_second, p_own, p_third, p_z, p_zz, p_final) = pieces[0]
    (q_core, q_first, q_second, q_own, q_third, q_z, q_zz, q_final) = pieces[1]
    k.grad_down(0, parts)
    k.grad_up(0, parts)
    p_core()
    k.grad_down(1, parts)
    p_first()
    k.grad_up(1, parts)
    q_core()
    k.grad_normed_two()
    credit = v["credit"]
    peers = ((net.core, net.z), (net.xn, net.z), (net.yn, net.z), (net.r, net.near), (net.r, net.far))
    for peer in peers:
        pl.semaphore_signal(credit, 1, device_id=peer, device_id_type=pl.DeviceIdType.MESH)
    q_first()
    k.norm_two_back()
    k.grad_outer()
    k.grad_attended()
    net.flush(resid_out)
    for s in range(S):
        net.exchange_out_done(k.out, resid_out, v["sem_out"].at[1], loc.at[2], s)
    k.attend_back_sequence(0)
    p_second()
    k.grad_normed_one(0)
    k.norm_one_back(0)
    net.exchange_out(k.x, grad_in, *pair("sem_gin"), loc.at[3], 0)
    k.attend_back_sequence(1)
    p_own()
    q_second()
    k.grad_normed_one(1)
    k.norm_one_back(1)
    net.exchange_out(k.x, grad_in, *pair("sem_gin"), loc.at[3], 1)
    k.attend_back_sequence(2)
    p_third()
    p_z()
    k.grad_inner()
    pl.semaphore_wait(credit, len(peers))
    (a_core, a_first, a_second, a_own, a_third, a_z, a_zz, a_final) = net.scatter(
        ga, 0, 0, wm.reshape(wm.shape[0] * parts, rows, wm.shape[2]), 0, *pair("sem_ra"), totals[parts]
    )
    a_core()
    k.grad_normed_one(2)
    a_first()
    k.norm_one_back(2)
    net.exchange_out(k.x, grad_in, *pair("sem_gin"), loc.at[3], 2)
    for i in range(8):
        v["every"][me, i : i + 1, 0 : k.D] = jnp.sum(k.small[i], axis=0, keepdims=True)
    v["every"][me, :, k.D : k.D + LANES] = tags[...]
    e_z, e_spread, e_forward, e_corner, e_last = net.gather_small(v["every"], *pair("sem_e"))
    e_z()
    q_own()
    q_third()
    q_z()
    p_zz()
    e_spread()
    a_second()
    q_zz()
    e_forward()
    a_own()
    p_final()
    e_corner()
    a_third()
    a_z()
    q_final()
    a_zz()
    e_last()
    a_final()
    for s in range(S):
        net.exchange_out_done(k.x, grad_in, v["sem_gin"].at[1], loc.at[3], s)
    outs = [pltpu.make_async_copy(totals[parts], ta, loc.at[4, 0])]
    outs += [pltpu.make_async_copy(totals[p], tm.at[pl.ds(p * rows, rows)], loc.at[0, p]) for p in range(parts)]
    outs.append(pltpu.make_async_copy(v["every"], every_out, loc.at[4, 2]))
    for copy in outs:
        copy.start()
    for copy in outs:
        copy.wait()
    net.flush()


def walk(is_split, parts, rows, D, visit):
    per = D // LANES

    def split():
        n = rows // parts
        for j in range(parts):
            for c in range(per):
                visit(pl.ds(j * n, n), pl.ds(c * LANES, LANES), pl.ds(j * per + c, n, stride=parts * per))

    def plain():
        for c in range(per):
            visit(pl.ds(0, rows), pl.ds(c * LANES, LANES), pl.ds(c, rows, stride=per))

    pl.when(is_split)(split)
    pl.when(jnp.logical_not(is_split))(plain)


def device_kinds():
    Z, R = lax.axis_size("seq"), lax.axis_size("rows")
    device = lax.axis_index("rows") * Z + lax.axis_index("seq")
    return device < R * Z * 3 // 4, device < R * Z // 2


def before_kernel(S, steps, mask, time_master, attn, mlp, sa, sm, mask_out, time_rows, tags, board, sems):
    D = sa.shape[1]
    first = lax.axis_index("seq") * S
    time_rows[...] = jnp.zeros(time_rows.shape, F32)
    copies = [
        pltpu.make_async_copy(time_master.at[pl.ds(steps[first + s], 1)], time_rows.at[pl.ds(s, 1)], sems.at[s])
        for s in range(S)
    ]
    for copy in copies:
        copy.start()
    row = lax.broadcasted_iota(jnp.int32, tags.shape, 0)
    value = jnp.full(tags.shape, -1, jnp.int32)
    for s in range(S):
        value = jnp.where(row == 5 + s, steps[first + s], value)
    tags[...] = value.astype(F32)
    board[...] = jnp.zeros(board.shape, F32)
    board[0 : mask.shape[0], 0 : mask.shape[1]] = mask[...].astype(F32)
    mask_out[...] = board[...].T[0 : mask.shape[1], :].astype(BF)
    is_inner, is_up = device_kinds()

    def cast(src, dst):
        def visit(rows, cols, lines):
            dst[rows, cols] = src[lines, :].astype(BF)

        return visit

    walk(is_inner, 3, sa.shape[0], D, cast(attn, sa))
    walk(is_up, FF // D, sm.shape[0], D, cast(mlp, sm))
    for copy in copies:
        copy.wait()


def adamw_low(master, moment_one, moment_two, gradient, step_rate):
    first_new = 0.5 * moment_one + 0.5 * gradient
    second_new = 0.5 * moment_two + 0.5 * gradient * gradient
    scale = 1.0 / (1.0 - 0.5**STEP)
    update = (first_new * scale) / (jnp.sqrt(second_new * scale) + 1e-08)
    return master - step_rate * (update + 0.1 * master), first_new, second_new


def after_kernel(ta, tm, every, *refs):
    D = ta.shape[1]
    attn, mlp, norm, time = refs[0:3], refs[3:6], refs[6:9], refs[9:12]
    attn_out, mlp_out, norm_out, time_out = refs[12:16], refs[16:20], refs[20:23], refs[23:26]
    step = pl.program_id(0)
    is_inner, is_up = device_kinds()

    def update(olds, news, grad, rate):
        def visit(rows, cols, lines):
            values = adamw_low(*(old[lines, :] for old in olds), grad[rows, cols], rate)
            for new, value in zip(news, values):
                new[lines, :] = value

        return visit

    @pl.when(step == 0)
    def _():
        walk(is_inner, 3, ta.shape[0], D, update(attn, attn_out[:3], ta, 0.05))
        attn_out[3][...] = attn_out[0][...].astype(BF)
        total = every[0, :, 0:D]
        for i in range(1, every.shape[0]):
            total = total + every[i, :, 0:D]
        values = adamw_low(*(old[...] for old in norm), total[0:5], 0.2)
        for new, value in zip(norm_out, values):
            new[...] = value

    @pl.when(step == 1)
    def _():
        walk(is_up, FF // D, tm.shape[0], D, update(mlp, mlp_out[:3], tm, 0.03))
        mlp_out[3][...] = mlp_out[0][...].astype(BF)

    n = time[0].shape[0]
    rows = every.shape[0] * every.shape[1]
    tag = every[:, :, D : D + LANES].reshape(rows, LANES)[:, 0:1]
    at = (lax.broadcasted_iota(jnp.int32, (rows, n), 1) + step * n).astype(F32)
    chosen = jnp.where(tag == at, 1.0, 0.0).astype(BF)
    rest = every[:, :, 0:D].reshape(rows, D)
    grad = None
    for _ in range(3):
        low = rest.astype(BF)
        rest = rest - low.astype(F32)
        y = dot(chosen, low, TN)
        grad = y if grad is None else grad + y
    values = adamw_low(*(old[...] for old in time), grad, 0.3)
    for new, value in zip(time_out, values):
        new[...] = value


def fast(
    resid_in,
    mask,
    steps_row,
    cotangent,
    attn_master,
    attn_first,
    attn_second,
    mlp_master,
    mlp_first,
    mlp_second,
    norm_master,
    norm_first,
    norm_second,
    time_master,
    time_first,
    time_second,
):
    D = resid_in.shape[2]
    Z = lax.axis_size("seq")
    R = lax.axis_size("rows")
    S = resid_in.shape[0] // Z
    part = resid_in.shape[1]
    L = part * Z
    T = S * L
    V = pl.BlockSpec(memory_space=pltpu.VMEM)
    A = pl.BlockSpec(memory_space=pl.ANY)
    shape = jax.ShapeDtypeStruct
    dma = pltpu.SemaphoreType.DMA
    attn = [a.reshape(-1, LANES) for a in (attn_master, attn_first, attn_second)]
    mlp = [a.reshape(-1, LANES) for a in (mlp_master, mlp_first, mlp_second)]
    sa_shape = (attn_master.shape[0] // D, D)
    sm_shape = (mlp_master.shape[0] // D, D)
    sa, sm, mask_in, time_rows, tags = pl.pallas_call(
        functools.partial(before_kernel, S),
        out_shape=(
            shape(sa_shape, BF),
            shape(sm_shape, BF),
            shape((part, LANES), BF),
            shape((8, D), F32),
            shape((8, LANES), F32),
        ),
        in_specs=[pl.BlockSpec(memory_space=pltpu.SMEM), V, A, V, V],
        out_specs=(V,) * 5,
        scratch_shapes=[pltpu.VMEM((LANES, LANES), F32), dma((S,))],
        compiler_params=pltpu.CompilerParams(vmem_limit_bytes=63 << 20),
    )(steps_row, mask, time_master, attn[0], mlp[0])
    sc = layer_scratch(T, D, S, L)
    scratch = [
        pltpu.VMEM((GROUPS, *sa.shape), BF),
        pltpu.VMEM((GROUPS * 3 // 2, *sm.shape), BF),
        pltpu.VMEM((sm.shape[0] // sa.shape[0] * (4 * Z + 6 * (Z // 2) + Z - 1), *sa.shape), BF),
        pltpu.VMEM((T, D), BF),
        pltpu.VMEM((T, D), BF),
        pltpu.VMEM((L, LANES), BF),
        *(sc[n] for n in LAYER_REFS),
        pltpu.VMEM((R * Z, 8, D + LANES), F32),
        *(dma((2, n)) for n in (40, 40, 12)),
        *(dma((2, S * (Z - 1))) for _ in range(4)),
        dma((2, Z)),
        dma((5, S)),
        dma((2, 16)),
        dma((2, sm.shape[0] // sa.shape[0], 16)),
        pltpu.SemaphoreType.REGULAR,
        pltpu.VMEM((sa.shape[0] + sm.shape[0], D), F32),
    ]
    resid_out, grad_in, ta, tm, every = pl.pallas_call(
        functools.partial(whole_kernel, (Z, S, part)),
        out_shape=(
            shape(resid_in.shape, BF),
            shape(resid_in.shape, BF),
            shape(sa.shape, F32),
            shape(sm.shape, F32),
            shape((R * Z, 8, D + LANES), F32),
        ),
        in_specs=[A, A, A, V, V, V, A, A],
        out_specs=(A,) * 5,
        scratch_shapes=scratch,
        compiler_params=pltpu.CompilerParams(
            collective_id=0, has_side_effects=True, vmem_limit_bytes=63 << 20
        ),
    )(resid_in, cotangent, mask_in, time_rows, tags, norm_master, sa, sm)
    steps = 5
    norm = (norm_master, norm_first, norm_second)
    time = (time_master, time_first, time_second)
    rows = time_master.shape[0] // steps
    moving = pl.BlockSpec((rows, D), lambda i: (i, 0))

    def fixed(a):
        return pl.BlockSpec(a.shape, lambda i: (0,) * len(a.shape))

    outs = [shape(a.shape, F32) for a in attn] + [shape(attn[0].shape, BF)]
    outs += [shape(a.shape, F32) for a in mlp] + [shape(mlp[0].shape, BF)]
    outs += [shape(a.shape, F32) for a in norm]
    news = pl.pallas_call(
        after_kernel,
        grid=(steps,),
        out_shape=(*outs, *(shape(a.shape, F32) for a in time)),
        in_specs=[fixed(a) for a in (ta, tm, every, *attn, *mlp, *norm)] + [moving] * 3,
        out_specs=(*(fixed(a) for a in outs), *(moving,) * 3),
        compiler_params=pltpu.CompilerParams(vmem_limit_bytes=63 << 20),
    )(ta, tm, every, *attn, *mlp, *norm, *time)
    return (resid_out, grad_in, *(a.reshape(-1) for a in news[:8]), *news[8:])


def solution(mesh):
    flat, whole, tokens = P(("rows", "seq")), P(), P("rows", "seq", None)
    fits = mesh.shape["rows"] * mesh.shape["seq"] == GROUPS and mesh.shape["rows"] == 8
    return jax.shard_map(
        fast if fits else general,
        mesh=mesh,
        in_specs=(tokens, P("rows", "seq"), P("rows"), tokens) + (flat,) * 6 + (whole,) * 6,
        out_specs=(tokens, tokens) + (flat,) * 8 + (whole,) * 6,
        check_vma=False,
    )
```

```python
import functools

import jax
import jax.numpy as jnp
from jax import lax
from jax.experimental import pallas as pl
from jax.experimental.pallas import tpu as pltpu
from jax.sharding import PartitionSpec as P

HEAD_DIM = 64
FF = 3072
STEP = 10
NORM_EPSILON = 1e-05
GROUPS = 32
LANES = 128
TILE = 256
ROW_BLOCK = 64
GELU_C = 0.7978845608028654
GELU_A = 0.044715
LOG2E = 1.4426950408889634
BF = jnp.bfloat16
F32 = jnp.float32

NN = (((1,), (0,)), ((), ()))
NT = (((1,), (1,)), ((), ()))
TN = (((0,), (0,)), ((), ()))


def dot(a, b, dims=NN):
    return lax.dot_general(a, b, dims, preferred_element_type=F32)


def norm_stats(h):
    mean = jnp.mean(h, axis=-1, keepdims=True)
    centred = h - mean
    var = jnp.mean(centred * centred, axis=-1, keepdims=True)
    rs = lax.rsqrt(var + NORM_EPSILON)
    return centred * rs, rs


def fold(x):
    return jnp.sum(x.reshape(x.shape[0] // 8, 8, x.shape[1]), axis=0)


def add_small(small, which, x):
    small[which] = small[which] + fold(x)


class Layer:
    def __init__(self, **refs):
        self.__dict__.update(refs)
        self.T, self.D = self.h.shape
        self.L = self.mask.shape[0]
        self.S = self.T // self.L
        self.PAIRS = self.D // LANES
        self.NJ = FF // self.D

    def qkv_part(self, ref, j, c, n):
        rows = ref.shape[1] // 3
        used = self.D // rows
        return ref.at[pl.ds(0, used), pl.ds(pl.multiple_of(j * rows, rows), rows), pl.ds(pl.multiple_of(c, n), n)]

    def out_part(self, ref, c, n):
        rows = ref.shape[1]
        used = self.D // rows
        return ref.at[pl.ds(ref.shape[0] - used, used), :, pl.ds(pl.multiple_of(c, n), n)]

    def up_part(self, ref, j, c, n):
        rows = ref.shape[1] // self.NJ
        used = self.D // rows
        return ref.at[pl.ds(0, used), pl.ds(pl.multiple_of(j * rows, rows), rows), pl.ds(pl.multiple_of(c, n), n)]

    def down_part(self, ref, j, c, n):
        rows = ref.shape[1]
        used = self.D // rows
        return ref.at[pl.ds(ref.shape[0] // 2 + j * used, used), :, pl.ds(pl.multiple_of(c, n), n)]

    def mask_col(self, s, base, n):
        m = self.mask[pl.ds(base, n), :].astype(F32)
        lane = lax.broadcasted_iota(jnp.int32, m.shape, 1)
        return jnp.sum(jnp.where(lane == self.lane + s, m, 0.0), axis=-1, keepdims=True)

    def embed(self, s):
        def body(i, _):
            base = pl.multiple_of(i * ROW_BLOCK, ROW_BLOCK)
            rows = pl.ds(pl.multiple_of(s * self.L + base, ROW_BLOCK), ROW_BLOCK)
            m = self.mask_col(s, base, ROW_BLOCK)
            h = self.x[rows, :].astype(F32) + m * self.norm[4:5, :] + self.time[s : s + 1, :]
            self.h[rows, :] = h
            xhat, _ = norm_stats(h)
            self.n1[rows, :] = (xhat * self.norm[0:1, :] + self.norm[1:2, :]).astype(BF)
            return 0

        lax.fori_loop(0, self.L // ROW_BLOCK, body, 0)

    def project(self, s):
        per = self.D // TILE
        rows = pl.ds(s * self.L, self.L)

        def body(i, _):
            j, c = lax.div(i, per), lax.rem(i, per) * TILE
            w = self.qkv_part(self.wa, j, c, TILE)[...].reshape(self.D, TILE)
            y = dot(self.n1[rows, :], w)
            self.qkv[rows, pl.ds(pl.multiple_of(i * TILE, TILE), TILE)] = y.astype(BF)
            return 0

        lax.fori_loop(0, 3 * per, body, 0)

    def pair_slices(self, s, p):
        rows = pl.ds(pl.multiple_of(s * self.L, self.L), self.L)
        cols = [pl.ds(pl.multiple_of(k * self.D + p * LANES, LANES), LANES) for k in range(3)]
        return rows, cols

    def half(self, x, hh):
        first = lax.broadcasted_iota(jnp.int32, x.shape, 1) < HEAD_DIM
        zero = jnp.zeros_like(x)
        return jnp.where(first, zero, x) if hh else jnp.where(first, x, zero)

    def attend(self, s, p):
        rows, cols = self.pair_slices(s, p)
        q, k, v = (self.qkv[rows, c] for c in cols)
        total = None
        for hh in range(2):
            sc = dot(self.half(q, hh), k, NT)
            top = jnp.max(sc, axis=-1, keepdims=True)
            e = jnp.exp2((sc - top) * (HEAD_DIM**-0.5 * LOG2E))
            w = (e * (1.0 / jnp.sum(e, axis=-1, keepdims=True))).astype(BF)
            self.soft[s * 2 * self.PAIRS + p * 2 + hh] = w
            o = dot(w, self.half(v, hh))
            total = o if total is None else total + o
        self.att[rows, cols[0]] = total.astype(BF)

    def attend_sequence(self, s):
        def body(p, _):
            self.attend(s, p)
            return 0

        lax.fori_loop(0, self.PAIRS, body, 0)

    def outer(self, s):
        rows = pl.ds(s * self.L, self.L)

        def body(i, _):
            c = i * TILE
            cols = pl.ds(pl.multiple_of(c, TILE), TILE)
            w = self.out_part(self.wa, c, TILE)[...].reshape(self.D, TILE)
            self.mid[rows, cols] = self.h[rows, cols] + dot(self.att[rows, :], w)
            return 0

        lax.fori_loop(0, self.D // TILE, body, 0)

    def second_norm(self, s):
        def body(i, _):
            rows = pl.ds(pl.multiple_of(s * self.L + i * ROW_BLOCK, ROW_BLOCK), ROW_BLOCK)
            xhat, _ = norm_stats(self.mid[rows, :])
            self.n2[rows, :] = (xhat * self.norm[2:3, :] + self.norm[3:4, :]).astype(BF)
            return 0

        lax.fori_loop(0, self.L // ROW_BLOCK, body, 0)

    def up(self):
        per = self.D // TILE

        def body(i, _):
            j, c = lax.div(i, per), lax.rem(i, per) * TILE
            cols = pl.ds(pl.multiple_of(i * TILE, TILE), TILE)
            w = self.up_part(self.wm, j, c, TILE)[...].reshape(self.D, TILE)
            for s in range(self.S):
                rows = pl.ds(s * self.L, self.L)
                u = dot(self.n2[rows, :], w)
                uu = u * u
                t = jnp.tanh(GELU_C * (u * (1.0 + GELU_A * uu)))
                left = 0.5 * (1.0 + t)
                self.act[pl.ds(pl.multiple_of(j * self.T + s * self.L, self.L), self.L), pl.ds(pl.multiple_of(c, TILE), TILE)] = (u * left).astype(BF)
                slope = left + (0.5 * GELU_C) * u * (1.0 - t * t) * (1.0 + 3.0 * GELU_A * uu)
                self.du[rows, cols] = slope.astype(BF)
            return 0

        lax.fori_loop(0, self.NJ * per, body, 0)

    def down(self):
        per = self.D // TILE

        def body(i, _):
            c = i * TILE
            cols = pl.ds(pl.multiple_of(c, TILE), TILE)
            for s in range(self.S):
                rows = pl.ds(s * self.L, self.L)
                total = self.mid[rows, cols]
                for j in range(self.NJ):
                    w = self.down_part(self.wm, j, c, TILE)[...].reshape(self.D, TILE)
                    total = total + dot(self.act[pl.ds(j * self.T + s * self.L, self.L), :], w)
                self.out[rows, cols] = total.astype(BF)
            return 0

        lax.fori_loop(0, per, body, 0)

    def mask_cotangent(self):
        for s in range(self.S):
            def body(i, _, s=s):
                base = pl.multiple_of(i * ROW_BLOCK, ROW_BLOCK)
                rows = pl.ds(pl.multiple_of(s * self.L + base, ROW_BLOCK), ROW_BLOCK)
                m = self.mask_col(s, base, ROW_BLOCK)
                self.g[rows, :] = (self.g[rows, :].astype(F32) * m).astype(BF)
                return 0

            lax.fori_loop(0, self.L // ROW_BLOCK, body, 0)

    def grad_pre(self):
        per = self.D // TILE

        def body(i, _):
            cols = pl.ds(pl.multiple_of(i * (self.D // 2), self.D // 2), self.D // 2)
            rows_w = self.wm.shape[1]
            used = self.D // 2 // rows_w
            w = self.wm[pl.ds(self.wm.shape[0] // 2 + i * used, used)].reshape(self.D // 2, self.D)
            for s in range(self.S):
                rows = pl.ds(s * self.L, self.L)
                d = dot(self.g[rows, :], w, NT)
                self.du[rows, cols] = (d * self.du[rows, cols].astype(F32)).astype(BF)
            return 0

        lax.fori_loop(0, 2 * self.NJ, body, 0)

    def turn_activated(self):
        for j in range(self.NJ):
            rows = pl.ds(j * self.T, self.T)
            self.turn[...] = self.act[rows, :].T
            self.act[rows, :] = self.turn[...]
        self.turn[...] = self.n2[...].T

    def grad_down(self, part, parts):
        group = self.gm_down.shape[1]
        used = self.D // group
        n = group // parts
        per = self.D // TILE

        def body(i, _):
            j, c = lax.div(i, per), pl.multiple_of(lax.rem(i, per) * TILE, TILE)
            a = jnp.concatenate(
                [
                    self.act[pl.ds(pl.multiple_of(j * self.D + u * group + part * n, 16), n), :]
                    for u in range(used)
                ]
            )
            y = dot(a, self.g[:, pl.ds(c, TILE)]).astype(BF)
            ref = self.gm_down.at[pl.ds(self.gm_down.shape[0] // 2 + j * used, used), pl.ds(part * n, n), pl.ds(c, TILE)]
            ref[...] = y.reshape(used, n, TILE)
            return 0

        lax.fori_loop(0, self.NJ * per, body, 0)

    def grad_up(self, part, parts):
        per = self.D // TILE
        n = self.NJ * per // parts

        def body(i, _):
            j, c = lax.div(i, per), lax.rem(i, per) * TILE
            y = dot(self.turn[...], self.du[:, pl.ds(pl.multiple_of(i * TILE, TILE), TILE)])
            ref = self.up_part(self.gm_up, j, c, TILE)
            ref[...] = y.astype(BF).reshape(ref.shape)
            return 0

        lax.fori_loop(part * n, (part + 1) * n, body, 0)

    def grad_normed_two(self):
        rows_w = self.wm.shape[1] // self.NJ
        n = self.D // 2
        used = n // rows_w

        def body(i, _):
            cols = pl.ds(pl.multiple_of(i * n, n), n)
            for s in range(self.S):
                rows = pl.ds(s * self.L, self.L)
                total = None
                for j in range(self.NJ):
                    w = self.wm[pl.ds(i * used, used), pl.ds(j * rows_w, rows_w), :].reshape(n, self.D)
                    y = dot(self.du[rows, pl.ds(j * self.D, self.D)], w, NT)
                    total = y if total is None else total + y
                self.dn[rows, cols] = total
            return 0

        lax.fori_loop(0, 2, body, 0)

    def norm_two_back(self):
        def body(i, _):
            rows = pl.ds(pl.multiple_of(i * ROW_BLOCK, ROW_BLOCK), ROW_BLOCK)
            xhat, rs = norm_stats(self.mid[rows, :])
            dy = self.dn[rows, :]
            add_small(self.small, 2, dy * xhat)
            add_small(self.small, 3, dy)
            e = dy * self.norm[2:3, :]
            back = (e - jnp.mean(e, -1, keepdims=True) - xhat * jnp.mean(e * xhat, -1, keepdims=True)) * rs
            gm = self.g[rows, :].astype(F32) + back
            self.dn[rows, :] = gm
            self.gb[rows, :] = gm.astype(BF)
            return 0

        lax.fori_loop(0, self.T // ROW_BLOCK, body, 0)

    def grad_outer(self):
        self.turn[...] = self.att[...].T

        def body(i, _):
            c = pl.multiple_of(i * TILE, TILE)
            y = dot(self.turn[...], self.gb[:, pl.ds(c, TILE)])
            ref = self.out_part(self.ga, c, TILE)
            ref[...] = y.astype(BF).reshape(ref.shape)
            return 0

        lax.fori_loop(0, self.D // TILE, body, 0)

    def grad_attended(self):
        n = self.D // 2
        rows_w = self.wa.shape[1]
        used = n // rows_w
        first = self.wa.shape[0] - 2 * used

        def body(i, _):
            w = self.wa[pl.ds(first + i * used, used)].reshape(n, self.D)
            for s in range(self.S):
                rows = pl.ds(s * self.L, self.L)
                self.att[rows, pl.ds(pl.multiple_of(i * n, n), n)] = dot(self.gb[rows, :], w, NT).astype(BF)
            return 0

        lax.fori_loop(0, 2, body, 0)

    def attend_back(self, s, p):
        rows, cols = self.pair_slices(s, p)
        q, k, v = (self.qkv[rows, c] for c in cols)
        da = self.att[rows, cols[0]]
        dq = dk = dv = None
        for hh in range(2):
            w = self.soft[s * 2 * self.PAIRS + p * 2 + hh]
            da_h = self.half(da, hh)
            dp = dot(da_h, v, NT)
            wf = w.astype(F32)
            t = wf * dp
            ds = (t - wf * jnp.sum(t, axis=-1, keepdims=True)).astype(BF)
            parts = (dot(ds, self.half(k, hh)), dot(ds, self.half(q, hh), TN), dot(w, da_h, TN))
            dq, dk, dv = parts if dq is None else (dq + parts[0], dk + parts[1], dv + parts[2])
        scale = HEAD_DIM**-0.5
        self.qkv[rows, cols[0]] = (dq * scale).astype(BF)
        self.qkv[rows, cols[1]] = (dk * scale).astype(BF)
        self.qkv[rows, cols[2]] = dv.astype(BF)

    def attend_back_sequence(self, s):
        def body(p, _):
            self.attend_back(s, p)
            return 0

        lax.fori_loop(0, self.PAIRS, body, 0)

    def grad_normed_one(self, s):
        n = self.D // 3
        rows_w = self.wa.shape[1] // 3
        used = n // rows_w
        rows = pl.ds(s * self.L, self.L)

        def body(i, _):
            total = None
            for j in range(3):
                w = self.wa[pl.ds(i * used, used), pl.ds(j * rows_w, rows_w), :].reshape(n, self.D)
                y = dot(self.qkv[rows, pl.ds(j * self.D, self.D)], w, NT)
                total = y if total is None else total + y
            self.mid[rows, pl.ds(pl.multiple_of(i * n, n), n)] = total
            return 0

        lax.fori_loop(0, 3, body, 0)

    def norm_one_back(self, s):
        def body(i, _):
            base = pl.multiple_of(i * ROW_BLOCK, ROW_BLOCK)
            rows = pl.ds(pl.multiple_of(s * self.L + base, ROW_BLOCK), ROW_BLOCK)
            xhat, rs = norm_stats(self.h[rows, :])
            dy = self.mid[rows, :]
            add_small(self.small, 0, dy * xhat)
            add_small(self.small, 1, dy)
            e = dy * self.norm[0:1, :]
            back = (e - jnp.mean(e, -1, keepdims=True) - xhat * jnp.mean(e * xhat, -1, keepdims=True)) * rs
            gs = self.dn[rows, :] + back
            add_small(self.small, 5 + s, gs)
            add_small(self.small, 4, gs * self.mask_col(s, base, ROW_BLOCK))
            self.x[rows, :] = gs.astype(BF)
            return 0

        lax.fori_loop(0, self.L // ROW_BLOCK, body, 0)

    def grad_inner(self):
        per = self.D // TILE
        self.turn[...] = self.n1[...].T

        def body(i, _):
            j, c = lax.div(i, per), lax.rem(i, per) * TILE
            y = dot(self.turn[...], self.qkv[:, pl.ds(pl.multiple_of(i * TILE, TILE), TILE)])
            ref = self.qkv_part(self.ga, j, c, TILE)
            ref[...] = y.astype(BF).reshape(ref.shape)
            return 0

        lax.fori_loop(0, 3 * per, body, 0)


def run_all(k):
    for i in range(8):
        k.small[i] = jnp.zeros(k.small.shape[1:], F32)
    for s in range(k.S):
        k.embed(s)
        k.project(s)
        k.attend_sequence(s)
        k.outer(s)
        k.second_norm(s)
    k.up()
    k.down()
    k.mask_cotangent()
    k.grad_pre()
    k.turn_activated()
    k.grad_down(0, 1)
    k.grad_up(0, 1)
    k.grad_normed_two()
    k.norm_two_back()
    k.grad_outer()
    k.grad_attended()
    for s in range(k.S):
        k.attend_back_sequence(s)
        k.grad_normed_one(s)
        k.norm_one_back(s)
    k.grad_inner()


def flip(index, bit):
    return index + bit - 2 * bit * lax.rem(lax.div(index, bit), 2)


def pick(table, index):
    value = table[0]
    for i in range(1, len(table)):
        value = jnp.where(index == i, table[i], value)
    return value


class Links:
    def __init__(self, Z, S, part):
        self.Z, self.S, self.part = Z, S, part
        self.r, self.z = lax.axis_index("rows"), lax.axis_index("seq")
        r = self.r
        self.core, self.xn, self.yn = flip(r, 1), flip(r, 2), flip(r, 4)
        self.diag = flip(self.xn, 4)
        self.pending = []
        near, far = flip(self.z, 1), flip(self.z, 2)
        self.near, self.far = near, far
        self.order = [self.z, near, far, flip(near, 2)]

    def barrier(self):
        bar = pltpu.get_barrier_semaphore()
        peers = [(self.core, self.z), (self.xn, self.z), (self.yn, self.z)]
        peers += [(self.r, lax.rem(self.z + i, self.Z)) for i in range(1, self.Z)]
        for peer in peers:
            pl.semaphore_signal(bar, 1, device_id=peer, device_id_type=pl.DeviceIdType.MESH)
        pl.semaphore_wait(bar, len(peers))

    def send(self, src, dst, ss, rs, peer, cond=None, owner=None):
        copy = pltpu.make_async_remote_copy(
            src, dst, ss, rs, device_id=peer, device_id_type=pl.DeviceIdType.MESH
        )
        if cond is None:
            copy.start()
        else:
            pl.when(cond)(copy.start)
        self.pending.append((owner, cond, copy))

    def arrived(self, dst, rs, cond=None):
        copy = pltpu.make_async_remote_copy(
            dst, dst, rs, rs, device_id=(self.core, self.z), device_id_type=pl.DeviceIdType.MESH
        )
        if cond is None:
            copy.wait_recv()
        else:
            pl.when(cond)(copy.wait_recv)

    def flush(self, src=None):
        left = []
        for item in self.pending:
            owner, cond, copy = item
            if src is not None and owner is not src:
                left.append(item)
            elif cond is None:
                copy.wait_send()
            else:
                pl.when(cond)(copy.wait_send)
        self.pending = left

    def gather(self, w, ss, rs):
        Z, z = self.Z, self.z
        count = [0]

        def go(row, zz, peer, cond=None):
            i = row * Z + zz
            self.send(w.at[i], w.at[i], ss.at[count[0]], rs.at[i], peer, cond, w)
            count[0] += 1

        def got(row, zz):
            i = row * Z + zz
            self.arrived(w.at[i], rs.at[i])

        def own(i):
            zz = self.order[i]
            if i:
                got(self.r, zz)
            if i == 0:
                go(self.r, zz, (self.r, self.far))
            if i == 0 or i == 2:
                go(self.r, zz, (self.r, self.near))
            go(self.r, zz, (self.xn, z))
            go(self.r, zz, (self.yn, z))
            go(self.r, zz, (self.core, z))

        def side(i):
            zz = self.order[i]
            got(self.xn, zz)
            if i % 2 == 0:
                go(self.xn, zz, (self.yn, z))
            go(self.xn, zz, (self.core, z))
            got(self.yn, zz)
            if i % 2 == 1:
                go(self.yn, zz, (self.xn, z))
            go(self.yn, zz, (self.core, z))

        def far(i):
            zz = self.order[i]
            got(self.diag, zz)
            go(self.diag, zz, (self.core, z))

        def last():
            for row in (self.r, self.xn, self.yn, self.diag):
                for i in range(Z):
                    got(flip(row, 1), self.order[i])

        return own, side, far, last

    def gather_small(self, w, ss, rs):
        Z, z = self.Z, self.z
        half = Z // 2

        def block(row, lo=0, n=Z):
            return w.at[pl.ds(row * Z + lo, n)]

        def go(ref, n, peer):
            self.send(ref, ref, ss.at[n], rs.at[n], peer)

        def along_z():
            for step in range(1, Z):
                go(block(self.r, z, 1), step, (self.r, lax.rem(z + step, Z)))

        def spread():
            for step in range(1, Z):
                self.arrived(block(self.r, lax.rem(z + Z - step, Z), 1), rs.at[step])
            go(block(self.r), 4, (self.xn, z))
            go(block(self.r), 5, (self.yn, z))
            go(block(self.r), 6, (self.core, z))

        def forward():
            self.arrived(block(self.xn), rs.at[4])
            go(block(self.xn, 0, half), 7, (self.yn, z))
            self.arrived(block(self.yn), rs.at[5])
            go(block(self.yn, half, half), 8, (self.xn, z))
            go(block(self.xn), 9, (self.core, z))
            go(block(self.yn), 10, (self.core, z))

        def corner():
            self.arrived(block(self.diag, 0, half), rs.at[7])
            self.arrived(block(self.diag, half, half), rs.at[8])
            go(block(self.diag), 11, (self.core, z))

        def last():
            self.arrived(block(self.core), rs.at[6])
            self.arrived(block(flip(self.xn, 1)), rs.at[9])
            self.arrived(block(flip(self.yn, 1)), rs.at[10])
            self.arrived(block(flip(self.diag, 1)), rs.at[11])

        return along_z, spread, forward, corner, last

    def exchange_in(self, src, dst, ss, rs, local, seqs):
        L = self.part * self.Z
        for i in seqs:
            for step in range(1, self.Z):
                to = lax.rem(self.z + step, self.Z)
                rows = pl.ds(i * L + self.z * self.part, self.part)
                n = i * (self.Z - 1) + step - 1
                self.send(src.at[to * self.S + i], dst.at[rows], ss.at[n], rs.at[n], (self.r, to))
            rows = pl.ds(i * L + self.z * self.part, self.part)
            pltpu.make_async_copy(src.at[self.z * self.S + i], dst.at[rows], local.at[i]).start()

    def exchange_in_done(self, src, dst, rs, local, i):
        L = self.part * self.Z
        for step in range(1, self.Z):
            source = lax.rem(self.z + self.Z - step, self.Z)
            rows = pl.ds(i * L + source * self.part, self.part)
            self.arrived(dst.at[rows], rs.at[i * (self.Z - 1) + step - 1])
        rows = pl.ds(i * L + self.z * self.part, self.part)
        pltpu.make_async_copy(src.at[self.z * self.S + i], dst.at[rows], local.at[i]).wait()

    def exchange_out(self, src, dst, ss, rs, local, i):
        L = self.part * self.Z
        for step in range(1, self.Z):
            to = lax.rem(self.z + step, self.Z)
            rows = pl.ds(i * L + to * self.part, self.part)
            n = i * (self.Z - 1) + step - 1
            self.send(src.at[rows], dst.at[self.z * self.S + i], ss.at[n], rs.at[n], (self.r, to), None, dst)
        rows = pl.ds(i * L + self.z * self.part, self.part)
        pltpu.make_async_copy(src.at[rows], dst.at[self.z * self.S + i], local.at[i]).start()

    def exchange_out_done(self, src, dst, rs, local, i):
        L = self.part * self.Z
        for step in range(1, self.Z):
            source = lax.rem(self.z + self.Z - step, self.Z)
            self.arrived(dst.at[source * self.S + i], rs.at[i * (self.Z - 1) + step - 1])
        rows = pl.ds(i * L + self.z * self.part, self.part)
        pltpu.make_async_copy(src.at[rows], dst.at[self.z * self.S + i], local.at[i]).wait()

    def scatter(self, g, base, part, inbox, box0, ss, rs, total):
        Z, z = self.Z, self.z
        half = Z // 2
        chip = lax.div(self.r, 2)
        k = lax.rem(self.r, 2)
        cx, cy = flip(chip, 1), flip(chip, 2)
        cd = flip(cx, 2)
        rows = total.shape[0]

        def block(c, parity, lo, n):
            return g.at[pl.ds(base + (2 * c + parity) * Z + lo, n), pl.ds(part * rows, rows)]

        def inslot(i, n):
            return inbox.at[pl.ds(box0 + i, n)]

        def add(dst, src, n):
            def body(i, _):
                dst[i] = (dst[i].astype(F32) + src[i].astype(F32)).astype(BF)
                return 0

            lax.fori_loop(0, n, body, 0)

        XY = 4 * Z
        ZB = XY + 6 * half

        def core_send_all():
            for c in range(4):
                core_send(c)

        def core_send(c):
            self.send(block(c, 1 - k, 0, Z), inslot(c * Z, Z), ss.at[c], rs.at[c], (self.core, z))

        def core_add(c):
            self.arrived(inslot(c * Z, Z), rs.at[c])
            add(block(c, k, 0, Z), inslot(c * Z, Z), Z)

        def xy_send(slot, c, lo, peer):
            i = XY + slot * half
            self.send(block(c, k, lo, half), inslot(i, half), ss.at[4 + slot], rs.at[4 + slot], (peer, z))

        def xy_add(slot, c, lo):
            i = XY + slot * half
            self.arrived(inslot(i, half), rs.at[4 + slot])
            add(block(c, k, lo, half), inslot(i, half), half)

        def first():
            core_add(cd)
            xy_send(0, cd, 0, self.xn)
            xy_send(2, cd, half, self.yn)
            core_add(cx)
            xy_send(1, cx, 0, self.xn)
            core_add(cy)
            xy_send(3, cy, half, self.yn)
            core_add(chip)

        def second():
            xy_add(0, cy, 0)
            xy_send(4, cy, 0, self.yn)
            xy_add(2, cx, half)
            xy_send(5, cx, half, self.xn)

        def second_own():
            xy_add(1, chip, 0)
            xy_add(3, chip, half)

        def third():
            xy_add(4, chip, 0)
            xy_add(5, chip, half)

        def z_send(slot, target, peer):
            box = inslot(ZB + slot, 1)
            self.send(block(chip, k, target, 1), box, ss.at[10 + slot], rs.at[10 + slot], (self.r, peer))

        def z_first():
            z_send(1, self.order[3], self.near)
            z_send(0, self.near, self.near)

        def z_second():
            self.arrived(inslot(ZB + 1, 1), rs.at[11])
            add(block(chip, k, self.far, 1), inslot(ZB + 1, 1), 1)
            z_send(2, self.far, self.far)

        def final():
            self.arrived(inslot(ZB, 1), rs.at[10])
            total[...] = block(chip, k, z, 1)[0].astype(F32) + inbox[box0 + ZB].astype(F32)
            self.arrived(inslot(ZB + 2, 1), rs.at[12])
            total[...] += inbox[box0 + ZB + 2].astype(F32)

        return core_send_all, first, second, second_own, third, z_first, z_second, final


def compute_kernel(x, mask, g_in, time, norm, wa, wm, out, gin, ga, gm, small, *scratch):
    names = ("g", "h", "n1", "qkv", "att", "mid", "n2", "act", "du", "soft", "dn", "gb", "turn", "sums")
    refs = dict(zip(names, scratch))
    sums = refs.pop("sums")
    pltpu.sync_copy(x, gin)
    pltpu.sync_copy(g_in, refs["g"])
    layer = Layer(
        x=gin, mask=mask, time=time, norm=norm, wa=wa, wm=wm, out=out, ga=ga, gm_down=gm, gm_up=gm, small=sums, lane=0, **refs
    )
    run_all(layer)
    for i in range(8):
        small[i : i + 1, :] = jnp.sum(sums[i], axis=0, keepdims=True)


def layer_scratch(T, D, S, L):
    heads = D // HEAD_DIM
    return dict(
        h=pltpu.VMEM((T, D), F32),
        n1=pltpu.VMEM((T, D), BF),
        qkv=pltpu.VMEM((T, 3 * D), BF),
        att=pltpu.VMEM((T, D), BF),
        mid=pltpu.VMEM((T, D), F32),
        n2=pltpu.VMEM((T, D), BF),
        act=pltpu.VMEM((FF // D * T, D), BF),
        du=pltpu.VMEM((T, FF), BF),
        soft=pltpu.VMEM((S * heads, L, L), BF),
        dn=pltpu.VMEM((T, D), F32),
        gb=pltpu.VMEM((T, D), BF),
        turn=pltpu.VMEM((D, D), BF),
        sums=pltpu.VMEM((8, 8, D), F32),
    )


def pad_rows(x):
    return jnp.pad(x, ((0, 8 - x.shape[0]), (0, 0)))


def rows_split(flat, groups, parts, D):
    return flat.reshape(groups, -1, parts, D).transpose(0, 2, 1, 3).reshape(groups, -1, D)


def rows_join(block, parts, D):
    groups = block.shape[0]
    return block.reshape(groups, parts, -1, D).transpose(0, 2, 1, 3).reshape(-1)


def adamw(master, moment_one, moment_two, gradient, step_rate):
    first_new = 0.5 * moment_one + 0.5 * gradient
    second_new = 0.5 * moment_two + 0.5 * gradient * gradient
    correct = 1.0 - 0.5**STEP
    update = first_new / correct / (jnp.sqrt(second_new / correct) + 1e-08)
    return (master - step_rate * (update + 0.1 * master), first_new, second_new)


def general(
    resid_in,
    mask,
    steps_row,
    cotangent,
    attn_master,
    attn_first,
    attn_second,
    mlp_master,
    mlp_first,
    mlp_second,
    norm_master,
    norm_first,
    norm_second,
    time_master,
    time_first,
    time_second,
):
    D = resid_in.shape[2]
    axes = ("rows", "seq")
    seq_count = lax.axis_size("seq")
    S = resid_in.shape[0] // seq_count
    L = resid_in.shape[1] * seq_count
    T = S * L
    attn_full = lax.all_gather(attn_master.astype(BF), axes, axis=0, tiled=True)
    mlp_full = lax.all_gather(mlp_master.astype(BF), axes, axis=0, tiled=True)
    inner = 3 * D * D
    wide = D * FF
    wa = jnp.concatenate(
        (rows_split(attn_full[:inner], 24, 3, D), attn_full[inner:].reshape(8, -1, D))
    )
    wm = jnp.concatenate((rows_split(mlp_full[:wide], 16, FF // D, D), mlp_full[wide:].reshape(16, -1, D)))
    exchange = functools.partial(lax.all_to_all, axis_name="seq", split_axis=0, concat_axis=1, tiled=True)
    x = exchange(resid_in).reshape(T, D)
    g = exchange(cotangent).reshape(T, D)
    mask_t = jnp.pad(exchange(mask.astype(BF)).T, ((0, 0), (0, LANES - S)))
    steps_use = lax.dynamic_slice_in_dim(steps_row, lax.axis_index("seq") * S, S, 0)
    time_rows = pad_rows(jnp.take(time_master, steps_use, axis=0))
    V = pl.BlockSpec(memory_space=pltpu.VMEM)
    A = pl.BlockSpec(memory_space=pl.ANY)
    shape = jax.ShapeDtypeStruct
    scratch = layer_scratch(T, D, S, L)
    out, gin, ga, gm, small = pl.pallas_call(
        compute_kernel,
        out_shape=(shape((T, D), BF), shape((T, D), BF), shape(wa.shape, BF), shape(wm.shape, BF), shape((8, D), F32)),
        in_specs=[A, V, A, V, V, V, V],
        out_specs=(V,) * 5,
        scratch_shapes=[pltpu.VMEM((T, D), BF)] + list(scratch.values()),
        compiler_params=pltpu.CompilerParams(vmem_limit_bytes=62 << 20),
    )(x, mask_t, g, time_rows, pad_rows(norm_master), wa, wm)
    attn_flat = jnp.concatenate((rows_join(ga[:24], 3, D), ga[24:].reshape(-1))).astype(F32)
    mlp_flat = jnp.concatenate((rows_join(gm[:16], FF // D, D), gm[16:].reshape(-1))).astype(F32)
    attn_grad = lax.psum_scatter(attn_flat, axes, scatter_dimension=0, tiled=True)
    mlp_grad = lax.psum_scatter(mlp_flat, axes, scatter_dimension=0, tiled=True)
    every = lax.all_gather(small, axes, axis=0)
    spread = functools.partial(lax.all_to_all, axis_name="seq", split_axis=1, concat_axis=0, tiled=True)
    return finish(
        spread(out.reshape(S, L, D)),
        spread(gin.reshape(S, L, D)),
        lax.all_gather(steps_row, "rows", axis=0, tiled=True),
        every,
        adamw(attn_master, attn_first, attn_second, attn_grad, 0.05),
        adamw(mlp_master, mlp_first, mlp_second, mlp_grad, 0.03),
        (norm_master, norm_first, norm_second),
        (time_master, time_first, time_second),
        S,
    )


def finish(resid_out, grad_in, steps, every, attn, mlp, norm, time, S):
    D = every.shape[2]
    norm_grad = jnp.sum(every[:, :5], axis=0)
    chosen = (jnp.arange(time[0].shape[0], dtype=jnp.int32)[:, None] == steps[None, :]).astype(F32)
    time_grad = jnp.dot(chosen, every[:, 5 : 5 + S].reshape(-1, D), precision=lax.Precision.HIGHEST)
    return (
        resid_out,
        grad_in,
        *attn,
        attn[0].astype(BF),
        *mlp,
        mlp[0].astype(BF),
        *adamw(*norm, norm_grad, 0.2),
        *adamw(*time, time_grad, 0.3),
    )


LAYER_REFS = ("h", "n1", "qkv", "att", "mid", "n2", "act", "du", "soft", "dn", "turn", "sums")


def whole_kernel(
    cfg, resid, cot, mask_in, time, tags, norm, sa, sm, resid_out, grad_in, ta, tm, every_out, *scratch
):
    Z, S, part = cfg
    names = (
        "wa", "wm", "inbox", "x", "g", "mask", "h", "n1",
        "qkv", "att", "mid", "n2", "act", "du", "soft", "dn",
        "turn", "sums", "every", "sem_a", "sem_m", "sem_e", "sem_in", "sem_cot",
        "sem_out", "sem_gin", "sem_mask", "loc", "sem_ra", "sem_rm", "credit", "total",
    )
    v = dict(zip(names, scratch))
    wm, ga = v["wm"], v["act"].reshape(GROUPS, v["wa"].shape[1], v["wa"].shape[2])
    half = GROUPS // 2
    grads = wm.at[pl.ds(half, GROUPS)]
    k = Layer(
        x=v["x"], out=v["x"], g=v["g"], mask=v["mask"], time=time, norm=norm, wa=v["wa"], wm=wm.at[pl.ds(0, GROUPS)],
        ga=ga, gm_up=grads, gm_down=grads, small=v["sums"], gb=v["n2"], lane=lax.axis_index("seq") * S,
        **{n: v[n] for n in LAYER_REFS[:-1]},
    )
    net = Links(Z, S, part)
    me = net.r * Z + net.z
    loc = v["loc"]
    own_a = pltpu.make_async_copy(sa, v["wa"].at[me], loc.at[4, 0])
    own_m = pltpu.make_async_copy(sm, wm.at[me], loc.at[4, 1])
    own_a.start()
    own_m.start()
    for i in range(8):
        k.small[i] = jnp.zeros(k.small.shape[1:], F32)
    net.barrier()
    own_a.wait()
    own_m.wait()

    def pair(name):
        return v[name].at[0], v[name].at[1]

    def pump(events, n=1):
        for _ in range(n):
            if events:
                events.pop(0)()

    a_own, a_side, a_far, a_last = net.gather(v["wa"], *pair("sem_a"))
    m_own, m_side, m_far, m_last = net.gather(wm, *pair("sem_m"))

    def stream(s):
        net.exchange_in(resid, k.x, *pair("sem_in"), loc.at[0], [s])

    a_own(0)
    m_own(0)
    for step in range(1, Z):
        to = lax.rem(net.z + step, Z)
        rows = pl.ds(net.z * part, part)
        net.send(mask_in, k.mask.at[rows], v["sem_mask"].at[0, step], v["sem_mask"].at[1, step], (net.r, to))
    own_mask = pltpu.make_async_copy(mask_in, k.mask.at[pl.ds(net.z * part, part)], loc.at[4, 2])
    own_mask.start()
    a_own(1)
    a_side(0)
    a_own(2)
    stream(0)
    a_side(1)
    a_far(0)
    m_own(1)
    a_own(3)
    a_side(2)
    a_far(1)
    m_side(0)
    m_own(2)
    stream(1)
    a_side(3)
    a_far(2)
    stream(2)
    a_far(3)
    a_last()
    net.exchange_in(cot, k.g, *pair("sem_cot"), loc.at[1], range(S))
    rm = [
        functools.partial(m_side, 1),
        functools.partial(m_own, 3),
        functools.partial(m_far, 0),
        functools.partial(m_side, 2),
        functools.partial(m_far, 1),
        functools.partial(m_side, 3),
        functools.partial(m_far, 2),
        functools.partial(m_far, 3),
        m_last,
    ]
    own_mask.wait()
    for step in range(1, Z):
        source = lax.rem(net.z + Z - step, Z)
        net.arrived(k.mask.at[pl.ds(source * part, part)], v["sem_mask"].at[1, step])

    for s in range(S):
        net.exchange_in_done(resid, k.x, v["sem_in"].at[1], loc.at[0], s)
        k.embed(s)
        pump(rm)
        k.project(s)
        pump(rm)
        k.attend_sequence(s)
        pump(rm)
        k.outer(s)
        k.second_norm(s)
    pump(rm, len(rm))
    k.up()
    k.down()
    for s in range(S):
        net.exchange_out(k.out, resid_out, *pair("sem_out"), loc.at[2], s)
    for s in range(S):
        net.exchange_in_done(cot, k.g, v["sem_cot"].at[1], loc.at[1], s)
    k.mask_cotangent()
    k.grad_pre()
    net.flush(wm)
    k.turn_activated()
    rows = sa.shape[0]
    parts = sm.shape[0] // rows
    boxes = v["inbox"].shape[0] // parts
    totals = [v["total"].at[pl.ds(p * rows, rows)] for p in range(parts + 1)]
    pieces = [
        net.scatter(wm, half, p, v["inbox"], p * boxes, v["sem_rm"].at[0, p], v["sem_rm"].at[1, p], totals[p])
        for p in range(parts)
    ]
    (p_core, p_first, p_second, p_own, p_third, p_z, p_zz, p_final) = pieces[0]
    (q_core, q_first, q_second, q_own, q_third, q_z, q_zz, q_final) = pieces[1]
    k.grad_down(0, parts)
    k.grad_up(0, parts)
    p_core()
    k.grad_down(1, parts)
    p_first()
    k.grad_up(1, parts)
    q_core()
    k.grad_normed_two()
    credit = v["credit"]
    peers = ((net.core, net.z), (net.xn, net.z), (net.yn, net.z), (net.r, net.near), (net.r, net.far))
    for peer in peers:
        pl.semaphore_signal(credit, 1, device_id=peer, device_id_type=pl.DeviceIdType.MESH)
    q_first()
    k.norm_two_back()
    k.grad_outer()
    k.grad_attended()
    net.flush(resid_out)
    for s in range(S):
        net.exchange_out_done(k.out, resid_out, v["sem_out"].at[1], loc.at[2], s)
    k.attend_back_sequence(0)
    p_second()
    k.grad_normed_one(0)
    k.norm_one_back(0)
    net.exchange_out(k.x, grad_in, *pair("sem_gin"), loc.at[3], 0)
    k.attend_back_sequence(1)
    p_own()
    q_second()
    k.grad_normed_one(1)
    k.norm_one_back(1)
    net.exchange_out(k.x, grad_in, *pair("sem_gin"), loc.at[3], 1)
    k.attend_back_sequence(2)
    p_third()
    p_z()
    k.grad_inner()
    pl.semaphore_wait(credit, len(peers))
    (a_core, a_first, a_second, a_own, a_third, a_z, a_zz, a_final) = net.scatter(
        ga, 0, 0, wm.reshape(wm.shape[0] * parts, rows, wm.shape[2]), 0, *pair("sem_ra"), totals[parts]
    )
    a_core()
    k.grad_normed_one(2)
    a_first()
    k.norm_one_back(2)
    net.exchange_out(k.x, grad_in, *pair("sem_gin"), loc.at[3], 2)
    for i in range(8):
        v["every"][me, i : i + 1, 0 : k.D] = jnp.sum(k.small[i], axis=0, keepdims=True)
    v["every"][me, :, k.D : k.D + LANES] = tags[...]
    e_z, e_spread, e_forward, e_corner, e_last = net.gather_small(v["every"], *pair("sem_e"))
    e_z()
    q_own()
    q_third()
    q_z()
    p_zz()
    e_spread()
    a_second()
    q_zz()
    e_forward()
    a_own()
    p_final()
    e_corner()
    a_third()
    a_z()
    q_final()
    a_zz()
    e_last()
    a_final()
    for s in range(S):
        net.exchange_out_done(k.x, grad_in, v["sem_gin"].at[1], loc.at[3], s)
    outs = [pltpu.make_async_copy(totals[parts], ta, loc.at[4, 0])]
    outs += [pltpu.make_async_copy(totals[p], tm.at[pl.ds(p * rows, rows)], loc.at[0, p]) for p in range(parts)]
    outs.append(pltpu.make_async_copy(v["every"], every_out, loc.at[4, 2]))
    for copy in outs:
        copy.start()
    for copy in outs:
        copy.wait()
    net.flush()


def walk(is_split, parts, rows, D, visit):
    per = D // LANES

    def split():
        n = rows // parts
        for j in range(parts):
            for c in range(per):
                visit(pl.ds(j * n, n), pl.ds(c * LANES, LANES), pl.ds(j * per + c, n, stride=parts * per))

    def plain():
        for c in range(per):
            visit(pl.ds(0, rows), pl.ds(c * LANES, LANES), pl.ds(c, rows, stride=per))

    pl.when(is_split)(split)
    pl.when(jnp.logical_not(is_split))(plain)


def device_kinds():
    Z, R = lax.axis_size("seq"), lax.axis_size("rows")
    device = lax.axis_index("rows") * Z + lax.axis_index("seq")
    return device < R * Z * 3 // 4, device < R * Z // 2


def before_kernel(S, steps, mask, time_master, attn, mlp, sa, sm, mask_out, time_rows, tags, board, sems):
    D = sa.shape[1]
    first = lax.axis_index("seq") * S
    time_rows[...] = jnp.zeros(time_rows.shape, F32)
    copies = [
        pltpu.make_async_copy(time_master.at[pl.ds(steps[first + s], 1)], time_rows.at[pl.ds(s, 1)], sems.at[s])
        for s in range(S)
    ]
    for copy in copies:
        copy.start()
    row = lax.broadcasted_iota(jnp.int32, tags.shape, 0)
    value = jnp.full(tags.shape, -1, jnp.int32)
    for s in range(S):
        value = jnp.where(row == 5 + s, steps[first + s], value)
    tags[...] = value.astype(F32)
    board[...] = jnp.zeros(board.shape, F32)
    board[0 : mask.shape[0], 0 : mask.shape[1]] = mask[...].astype(F32)
    mask_out[...] = board[...].T[0 : mask.shape[1], :].astype(BF)
    is_inner, is_up = device_kinds()

    def cast(src, dst):
        def visit(rows, cols, lines):
            dst[rows, cols] = src[lines, :].astype(BF)

        return visit

    walk(is_inner, 3, sa.shape[0], D, cast(attn, sa))
    walk(is_up, FF // D, sm.shape[0], D, cast(mlp, sm))
    for copy in copies:
        copy.wait()


def adamw_low(master, moment_one, moment_two, gradient, step_rate):
    first_new = 0.5 * moment_one + 0.5 * gradient
    second_new = 0.5 * moment_two + 0.5 * gradient * gradient
    scale = 1.0 / (1.0 - 0.5**STEP)
    update = (first_new * scale) / (jnp.sqrt(second_new * scale) + 1e-08)
    return master - step_rate * (update + 0.1 * master), first_new, second_new


def after_kernel(ta, tm, every, *refs):
    D = ta.shape[1]
    flat, norm, time, tokens = refs[0:6], refs[6:9], refs[9:12], refs[12:14]
    flat_out, norm_out, time_out, tokens_out = refs[14:22], refs[22:25], refs[25:28], refs[28:30]
    held, low, sems = refs[30:36], refs[36:38], refs[38]
    step = pl.program_id(0)
    is_inner, is_up = device_kinds()
    loads = [pltpu.make_async_copy(a, b, sems.at[i]) for i, (a, b) in enumerate(zip(flat, held))]
    ready = (*held[:3], low[0], *held[3:], low[1])
    stores = [pltpu.make_async_copy(a, b, sems.at[6 + i]) for i, (a, b) in enumerate(zip(ready, flat_out))]

    def update(kept, grad, rate):
        def visit(rows, cols, lines):
            values = adamw_low(*(old[lines, :] for old in kept), grad[rows, cols], rate)
            for new, value in zip(kept, values):
                new[lines, :] = value

        return visit

    for new, old in zip(tokens_out, tokens):
        new[...] = old[...]

    @pl.when(step == 0)
    def _():
        for copy in loads:
            copy.start()
        total = every[0, :, 0:D]
        for i in range(1, every.shape[0]):
            total = total + every[i, :, 0:D]
        values = adamw_low(*(old[...] for old in norm), total[0:5], 0.2)
        for new, value in zip(norm_out, values):
            new[...] = value

    @pl.when(step == 1)
    def _():
        for copy in loads:
            copy.wait()
        walk(is_inner, 3, ta.shape[0], D, update(held[:3], ta, 0.05))
        low[0][...] = held[0][...].astype(BF)
        walk(is_up, FF // D, tm.shape[0], D, update(held[3:], tm, 0.03))
        low[1][...] = held[3][...].astype(BF)
        for copy in stores:
            copy.start()

    @pl.when(step == pl.num_programs(0) - 1)
    def _():
        for copy in stores:
            copy.wait()

    n = time[0].shape[0]
    rows = every.shape[0] * every.shape[1]
    tag = every[:, :, D : D + LANES].reshape(rows, LANES)[:, 0:1]
    at = (lax.broadcasted_iota(jnp.int32, (rows, n), 1) + step * n).astype(F32)
    chosen = jnp.where(tag == at, 1.0, 0.0).astype(BF)
    rest = every[:, :, 0:D].reshape(rows, D)
    grad = None
    for _ in range(3):
        low = rest.astype(BF)
        rest = rest - low.astype(F32)
        y = dot(chosen, low, TN)
        grad = y if grad is None else grad + y
    values = adamw_low(*(old[...] for old in time), grad, 0.3)
    for new, value in zip(time_out, values):
        new[...] = value


def fast(
    resid_in,
    mask,
    steps_row,
    cotangent,
    attn_master,
    attn_first,
    attn_second,
    mlp_master,
    mlp_first,
    mlp_second,
    norm_master,
    norm_first,
    norm_second,
    time_master,
    time_first,
    time_second,
):
    D = resid_in.shape[2]
    Z = lax.axis_size("seq")
    R = lax.axis_size("rows")
    S = resid_in.shape[0] // Z
    part = resid_in.shape[1]
    L = part * Z
    T = S * L
    V = pl.BlockSpec(memory_space=pltpu.VMEM)
    A = pl.BlockSpec(memory_space=pl.ANY)
    shape = jax.ShapeDtypeStruct
    dma = pltpu.SemaphoreType.DMA
    attn = [a.reshape(-1, LANES) for a in (attn_master, attn_first, attn_second)]
    mlp = [a.reshape(-1, LANES) for a in (mlp_master, mlp_first, mlp_second)]
    sa_shape = (attn_master.shape[0] // D, D)
    sm_shape = (mlp_master.shape[0] // D, D)
    sa, sm, mask_in, time_rows, tags = pl.pallas_call(
        functools.partial(before_kernel, S),
        out_shape=(
            shape(sa_shape, BF),
            shape(sm_shape, BF),
            shape((part, LANES), BF),
            shape((8, D), F32),
            shape((8, LANES), F32),
        ),
        in_specs=[pl.BlockSpec(memory_space=pltpu.SMEM), V, A, V, V],
        out_specs=(V,) * 5,
        scratch_shapes=[pltpu.VMEM((LANES, LANES), F32), dma((S,))],
        compiler_params=pltpu.CompilerParams(vmem_limit_bytes=63 << 20),
    )(steps_row, mask, time_master, attn[0], mlp[0])
    sc = layer_scratch(T, D, S, L)
    scratch = [
        pltpu.VMEM((GROUPS, *sa.shape), BF),
        pltpu.VMEM((GROUPS * 3 // 2, *sm.shape), BF),
        pltpu.VMEM((sm.shape[0] // sa.shape[0] * (4 * Z + 6 * (Z // 2) + Z - 1), *sa.shape), BF),
        pltpu.VMEM((T, D), BF),
        pltpu.VMEM((T, D), BF),
        pltpu.VMEM((L, LANES), BF),
        *(sc[n] for n in LAYER_REFS),
        pltpu.VMEM((R * Z, 8, D + LANES), F32),
        *(dma((2, n)) for n in (40, 40, 12)),
        *(dma((2, S * (Z - 1))) for _ in range(4)),
        dma((2, Z)),
        dma((5, S)),
        dma((2, 16)),
        dma((2, sm.shape[0] // sa.shape[0], 16)),
        pltpu.SemaphoreType.REGULAR,
        pltpu.VMEM((sa.shape[0] + sm.shape[0], D), F32),
    ]
    resid_out, grad_in, ta, tm, every = pl.pallas_call(
        functools.partial(whole_kernel, (Z, S, part)),
        out_shape=(
            shape(resid_in.shape, BF),
            shape(resid_in.shape, BF),
            shape(sa.shape, F32),
            shape(sm.shape, F32),
            shape((R * Z, 8, D + LANES), F32),
        ),
        in_specs=[A, A, A, V, V, V, A, A],
        out_specs=(A,) * 5,
        scratch_shapes=scratch,
        compiler_params=pltpu.CompilerParams(
            collective_id=0, has_side_effects=True, vmem_limit_bytes=63 << 20
        ),
    )(resid_in, cotangent, mask_in, time_rows, tags, norm_master, sa, sm)
    steps = 5
    norm = (norm_master, norm_first, norm_second)
    time = (time_master, time_first, time_second)
    rows = time_master.shape[0] // steps
    moving = pl.BlockSpec((rows, D), lambda i: (i, 0))

    def fixed(a):
        return pl.BlockSpec(a.shape, lambda i: (0,) * len(a.shape))

    blocks = resid_in.shape[0] // S
    tokens = pl.BlockSpec((S, part, D), lambda i: (jnp.minimum(i, blocks - 1), 0, 0))
    outs = [shape(a.shape, F32) for a in attn] + [shape(attn[0].shape, BF)]
    outs += [shape(a.shape, F32) for a in mlp] + [shape(mlp[0].shape, BF)]
    news = pl.pallas_call(
        after_kernel,
        grid=(steps,),
        out_shape=(*outs, *(shape(a.shape, F32) for a in (*norm, *time)), *(shape(resid_in.shape, BF),) * 2),
        in_specs=[fixed(a) for a in (ta, tm, every)] + [A] * 6 + [fixed(a) for a in norm] + [moving] * 3 + [tokens] * 2,
        out_specs=(*(A,) * 8, *(fixed(a) for a in norm), *(moving,) * 3, tokens, tokens),
        scratch_shapes=[
            *(pltpu.VMEM(a.shape, F32) for a in (*attn, *mlp)),
            pltpu.VMEM(attn[0].shape, BF),
            pltpu.VMEM(mlp[0].shape, BF),
            dma((14,)),
        ],
        compiler_params=pltpu.CompilerParams(vmem_limit_bytes=63 << 20),
    )(ta, tm, every, *attn, *mlp, *norm, *time, resid_out, grad_in)
    return (*news[14:], *(a.reshape(-1) for a in news[:8]), *news[8:14])


def solution(mesh):
    flat, whole, tokens = P(("rows", "seq")), P(), P("rows", "seq", None)
    fits = mesh.shape["rows"] * mesh.shape["seq"] == GROUPS and mesh.shape["rows"] == 8
    return jax.shard_map(
        fast if fits else general,
        mesh=mesh,
        in_specs=(tokens, P("rows", "seq"), P("rows"), tokens) + (flat,) * 6 + (whole,) * 6,
        out_specs=(tokens, tokens) + (flat,) * 8 + (whole,) * 6,
        check_vma=False,
    )
```

```python
import functools

import jax
import jax.numpy as jnp
from jax import lax
from jax.experimental import pallas as pl
from jax.experimental.pallas import tpu as pltpu
from jax.sharding import PartitionSpec as P

HEAD_DIM = 64
FF = 3072
STEP = 10
NORM_EPSILON = 1e-05
GROUPS = 32
LANES = 128
TILE = 256
ROW_BLOCK = 64
GELU_C = 0.7978845608028654
GELU_A = 0.044715
LOG2E = 1.4426950408889634
BF = jnp.bfloat16
F32 = jnp.float32

NN = (((1,), (0,)), ((), ()))
NT = (((1,), (1,)), ((), ()))
TN = (((0,), (0,)), ((), ()))


def dot(a, b, dims=NN):
    return lax.dot_general(a, b, dims, preferred_element_type=F32)


def norm_stats(h):
    mean = jnp.mean(h, axis=-1, keepdims=True)
    centred = h - mean
    var = jnp.mean(centred * centred, axis=-1, keepdims=True)
    rs = lax.rsqrt(var + NORM_EPSILON)
    return centred * rs, rs


def fold(x):
    return jnp.sum(x.reshape(x.shape[0] // 8, 8, x.shape[1]), axis=0)


def add_small(small, which, x):
    small[which] = small[which] + fold(x)


class Layer:
    def __init__(self, **refs):
        self.__dict__.update(refs)
        self.T, self.D = self.h.shape
        self.L = self.mask.shape[0]
        self.S = self.T // self.L
        self.PAIRS = self.D // LANES
        self.NJ = FF // self.D

    def qkv_part(self, ref, j, c, n):
        rows = ref.shape[1] // 3
        used = self.D // rows
        return ref.at[pl.ds(0, used), pl.ds(pl.multiple_of(j * rows, rows), rows), pl.ds(pl.multiple_of(c, n), n)]

    def out_part(self, ref, c, n):
        rows = ref.shape[1]
        used = self.D // rows
        return ref.at[pl.ds(ref.shape[0] - used, used), :, pl.ds(pl.multiple_of(c, n), n)]

    def up_part(self, ref, j, c, n):
        rows = ref.shape[1] // self.NJ
        used = self.D // rows
        return ref.at[pl.ds(0, used), pl.ds(pl.multiple_of(j * rows, rows), rows), pl.ds(pl.multiple_of(c, n), n)]

    def down_part(self, ref, j, c, n):
        rows = ref.shape[1]
        used = self.D // rows
        return ref.at[pl.ds(ref.shape[0] // 2 + j * used, used), :, pl.ds(pl.multiple_of(c, n), n)]

    def mask_col(self, s, base, n):
        m = self.mask[pl.ds(base, n), :].astype(F32)
        lane = lax.broadcasted_iota(jnp.int32, m.shape, 1)
        return jnp.sum(jnp.where(lane == self.lane + s, m, 0.0), axis=-1, keepdims=True)

    def embed(self, s):
        def body(i, _):
            base = pl.multiple_of(i * ROW_BLOCK, ROW_BLOCK)
            rows = pl.ds(pl.multiple_of(s * self.L + base, ROW_BLOCK), ROW_BLOCK)
            m = self.mask_col(s, base, ROW_BLOCK)
            h = self.x[rows, :].astype(F32) + m * self.norm[4:5, :] + self.time[s : s + 1, :]
            self.h[rows, :] = h
            xhat, _ = norm_stats(h)
            self.n1[rows, :] = (xhat * self.norm[0:1, :] + self.norm[1:2, :]).astype(BF)
            return 0

        lax.fori_loop(0, self.L // ROW_BLOCK, body, 0)

    def project(self, s):
        per = self.D // TILE
        rows = pl.ds(s * self.L, self.L)

        def body(i, _):
            j, c = lax.div(i, per), lax.rem(i, per) * TILE
            w = self.qkv_part(self.wa, j, c, TILE)[...].reshape(self.D, TILE)
            y = dot(self.n1[rows, :], w)
            self.qkv[rows, pl.ds(pl.multiple_of(i * TILE, TILE), TILE)] = y.astype(BF)
            return 0

        lax.fori_loop(0, 3 * per, body, 0)

    def pair_slices(self, s, p):
        rows = pl.ds(pl.multiple_of(s * self.L, self.L), self.L)
        cols = [pl.ds(pl.multiple_of(k * self.D + p * LANES, LANES), LANES) for k in range(3)]
        return rows, cols

    def half(self, x, hh):
        first = lax.broadcasted_iota(jnp.int32, x.shape, 1) < HEAD_DIM
        zero = jnp.zeros_like(x)
        return jnp.where(first, zero, x) if hh else jnp.where(first, x, zero)

    def attend(self, s, p):
        rows, cols = self.pair_slices(s, p)
        q, k, v = (self.qkv[rows, c] for c in cols)
        total = None
        for hh in range(2):
            sc = dot(self.half(q, hh), k, NT)
            top = jnp.max(sc, axis=-1, keepdims=True)
            e = jnp.exp2((sc - top) * (HEAD_DIM**-0.5 * LOG2E))
            w = (e * (1.0 / jnp.sum(e, axis=-1, keepdims=True))).astype(BF)
            self.soft[s * 2 * self.PAIRS + p * 2 + hh] = w
            o = dot(w, self.half(v, hh))
            total = o if total is None else total + o
        self.att[rows, cols[0]] = total.astype(BF)

    def attend_sequence(self, s):
        def body(p, _):
            self.attend(s, p)
            return 0

        lax.fori_loop(0, self.PAIRS, body, 0)

    def outer(self, s):
        rows = pl.ds(s * self.L, self.L)

        def body(i, _):
            c = i * TILE
            cols = pl.ds(pl.multiple_of(c, TILE), TILE)
            w = self.out_part(self.wa, c, TILE)[...].reshape(self.D, TILE)
            self.mid[rows, cols] = self.h[rows, cols] + dot(self.att[rows, :], w)
            return 0

        lax.fori_loop(0, self.D // TILE, body, 0)

    def second_norm(self, s):
        def body(i, _):
            rows = pl.ds(pl.multiple_of(s * self.L + i * ROW_BLOCK, ROW_BLOCK), ROW_BLOCK)
            xhat, _ = norm_stats(self.mid[rows, :])
            self.n2[rows, :] = (xhat * self.norm[2:3, :] + self.norm[3:4, :]).astype(BF)
            return 0

        lax.fori_loop(0, self.L // ROW_BLOCK, body, 0)

    def up(self):
        per = self.D // TILE

        def body(i, _):
            j, c = lax.div(i, per), lax.rem(i, per) * TILE
            cols = pl.ds(pl.multiple_of(i * TILE, TILE), TILE)
            w = self.up_part(self.wm, j, c, TILE)[...].reshape(self.D, TILE)
            for s in range(self.S):
                rows = pl.ds(s * self.L, self.L)
                u = dot(self.n2[rows, :], w)
                uu = u * u
                t = jnp.tanh(GELU_C * (u * (1.0 + GELU_A * uu)))
                left = 0.5 * (1.0 + t)
                self.act[pl.ds(pl.multiple_of(j * self.T + s * self.L, self.L), self.L), pl.ds(pl.multiple_of(c, TILE), TILE)] = (u * left).astype(BF)
                slope = left + (0.5 * GELU_C) * u * (1.0 - t * t) * (1.0 + 3.0 * GELU_A * uu)
                self.du[rows, cols] = slope.astype(BF)
            return 0

        lax.fori_loop(0, self.NJ * per, body, 0)

    def down(self):
        per = self.D // TILE

        def body(i, _):
            c = i * TILE
            cols = pl.ds(pl.multiple_of(c, TILE), TILE)
            for s in range(self.S):
                rows = pl.ds(s * self.L, self.L)
                total = self.mid[rows, cols]
                for j in range(self.NJ):
                    w = self.down_part(self.wm, j, c, TILE)[...].reshape(self.D, TILE)
                    total = total + dot(self.act[pl.ds(j * self.T + s * self.L, self.L), :], w)
                self.out[rows, cols] = total.astype(BF)
            return 0

        lax.fori_loop(0, per, body, 0)

    def mask_cotangent(self):
        for s in range(self.S):
            def body(i, _, s=s):
                base = pl.multiple_of(i * ROW_BLOCK, ROW_BLOCK)
                rows = pl.ds(pl.multiple_of(s * self.L + base, ROW_BLOCK), ROW_BLOCK)
                m = self.mask_col(s, base, ROW_BLOCK)
                self.g[rows, :] = (self.g[rows, :].astype(F32) * m).astype(BF)
                return 0

            lax.fori_loop(0, self.L // ROW_BLOCK, body, 0)

    def grad_pre(self):
        per = self.D // TILE

        def body(i, _):
            cols = pl.ds(pl.multiple_of(i * (self.D // 2), self.D // 2), self.D // 2)
            rows_w = self.wm.shape[1]
            used = self.D // 2 // rows_w
            w = self.wm[pl.ds(self.wm.shape[0] // 2 + i * used, used)].reshape(self.D // 2, self.D)
            for s in range(self.S):
                rows = pl.ds(s * self.L, self.L)
                d = dot(self.g[rows, :], w, NT)
                self.du[rows, cols] = (d * self.du[rows, cols].astype(F32)).astype(BF)
            return 0

        lax.fori_loop(0, 2 * self.NJ, body, 0)

    def turn_activated(self):
        for j in range(self.NJ):
            rows = pl.ds(j * self.T, self.T)
            self.turn[...] = self.act[rows, :].T
            self.act[rows, :] = self.turn[...]
        self.turn[...] = self.n2[...].T

    def grad_down(self, part, parts):
        group = self.gm_down.shape[1]
        used = self.D // group
        n = group // parts
        per = self.D // TILE

        def body(i, _):
            j, c = lax.div(i, per), pl.multiple_of(lax.rem(i, per) * TILE, TILE)
            a = jnp.concatenate(
                [
                    self.act[pl.ds(pl.multiple_of(j * self.D + u * group + part * n, 16), n), :]
                    for u in range(used)
                ]
            )
            y = dot(a, self.g[:, pl.ds(c, TILE)]).astype(BF)
            ref = self.gm_down.at[pl.ds(self.gm_down.shape[0] // 2 + j * used, used), pl.ds(part * n, n), pl.ds(c, TILE)]
            ref[...] = y.reshape(used, n, TILE)
            return 0

        lax.fori_loop(0, self.NJ * per, body, 0)

    def grad_up(self, part, parts):
        per = self.D // TILE
        n = self.NJ * per // parts

        def body(i, _):
            j, c = lax.div(i, per), lax.rem(i, per) * TILE
            y = dot(self.turn[...], self.du[:, pl.ds(pl.multiple_of(i * TILE, TILE), TILE)])
            ref = self.up_part(self.gm_up, j, c, TILE)
            ref[...] = y.astype(BF).reshape(ref.shape)
            return 0

        lax.fori_loop(part * n, (part + 1) * n, body, 0)

    def grad_normed_two(self):
        rows_w = self.wm.shape[1] // self.NJ
        n = self.D // 2
        used = n // rows_w

        def body(i, _):
            cols = pl.ds(pl.multiple_of(i * n, n), n)
            for s in range(self.S):
                rows = pl.ds(s * self.L, self.L)
                total = None
                for j in range(self.NJ):
                    w = self.wm[pl.ds(i * used, used), pl.ds(j * rows_w, rows_w), :].reshape(n, self.D)
                    y = dot(self.du[rows, pl.ds(j * self.D, self.D)], w, NT)
                    total = y if total is None else total + y
                self.dn[rows, cols] = total
            return 0

        lax.fori_loop(0, 2, body, 0)

    def norm_two_back(self):
        def body(i, _):
            rows = pl.ds(pl.multiple_of(i * ROW_BLOCK, ROW_BLOCK), ROW_BLOCK)
            xhat, rs = norm_stats(self.mid[rows, :])
            dy = self.dn[rows, :]
            add_small(self.small, 2, dy * xhat)
            add_small(self.small, 3, dy)
            e = dy * self.norm[2:3, :]
            back = (e - jnp.mean(e, -1, keepdims=True) - xhat * jnp.mean(e * xhat, -1, keepdims=True)) * rs
            gm = self.g[rows, :].astype(F32) + back
            self.dn[rows, :] = gm
            self.gb[rows, :] = gm.astype(BF)
            return 0

        lax.fori_loop(0, self.T // ROW_BLOCK, body, 0)

    def grad_outer(self):
        self.turn[...] = self.att[...].T

        def body(i, _):
            c = pl.multiple_of(i * TILE, TILE)
            y = dot(self.turn[...], self.gb[:, pl.ds(c, TILE)])
            ref = self.out_part(self.ga, c, TILE)
            ref[...] = y.astype(BF).reshape(ref.shape)
            return 0

        lax.fori_loop(0, self.D // TILE, body, 0)

    def grad_attended(self):
        n = self.D // 2
        rows_w = self.wa.shape[1]
        used = n // rows_w
        first = self.wa.shape[0] - 2 * used

        def body(i, _):
            w = self.wa[pl.ds(first + i * used, used)].reshape(n, self.D)
            for s in range(self.S):
                rows = pl.ds(s * self.L, self.L)
                self.att[rows, pl.ds(pl.multiple_of(i * n, n), n)] = dot(self.gb[rows, :], w, NT).astype(BF)
            return 0

        lax.fori_loop(0, 2, body, 0)

    def attend_back(self, s, p):
        rows, cols = self.pair_slices(s, p)
        q, k, v = (self.qkv[rows, c] for c in cols)
        da = self.att[rows, cols[0]]
        dq = dk = dv = None
        for hh in range(2):
            w = self.soft[s * 2 * self.PAIRS + p * 2 + hh]
            da_h = self.half(da, hh)
            dp = dot(da_h, v, NT)
            wf = w.astype(F32)
            t = wf * dp
            ds = (t - wf * jnp.sum(t, axis=-1, keepdims=True)).astype(BF)
            parts = (dot(ds, self.half(k, hh)), dot(ds, self.half(q, hh), TN), dot(w, da_h, TN))
            dq, dk, dv = parts if dq is None else (dq + parts[0], dk + parts[1], dv + parts[2])
        scale = HEAD_DIM**-0.5
        self.qkv[rows, cols[0]] = (dq * scale).astype(BF)
        self.qkv[rows, cols[1]] = (dk * scale).astype(BF)
        self.qkv[rows, cols[2]] = dv.astype(BF)

    def attend_back_sequence(self, s):
        def body(p, _):
            self.attend_back(s, p)
            return 0

        lax.fori_loop(0, self.PAIRS, body, 0)

    def grad_normed_one(self, s):
        n = self.D // 3
        rows_w = self.wa.shape[1] // 3
        used = n // rows_w
        rows = pl.ds(s * self.L, self.L)

        def body(i, _):
            total = None
            for j in range(3):
                w = self.wa[pl.ds(i * used, used), pl.ds(j * rows_w, rows_w), :].reshape(n, self.D)
                y = dot(self.qkv[rows, pl.ds(j * self.D, self.D)], w, NT)
                total = y if total is None else total + y
            self.mid[rows, pl.ds(pl.multiple_of(i * n, n), n)] = total
            return 0

        lax.fori_loop(0, 3, body, 0)

    def norm_one_back(self, s):
        def body(i, _):
            base = pl.multiple_of(i * ROW_BLOCK, ROW_BLOCK)
            rows = pl.ds(pl.multiple_of(s * self.L + base, ROW_BLOCK), ROW_BLOCK)
            xhat, rs = norm_stats(self.h[rows, :])
            dy = self.mid[rows, :]
            add_small(self.small, 0, dy * xhat)
            add_small(self.small, 1, dy)
            e = dy * self.norm[0:1, :]
            back = (e - jnp.mean(e, -1, keepdims=True) - xhat * jnp.mean(e * xhat, -1, keepdims=True)) * rs
            gs = self.dn[rows, :] + back
            add_small(self.small, 5 + s, gs)
            add_small(self.small, 4, gs * self.mask_col(s, base, ROW_BLOCK))
            self.x[rows, :] = gs.astype(BF)
            return 0

        lax.fori_loop(0, self.L // ROW_BLOCK, body, 0)

    def grad_inner(self):
        per = self.D // TILE
        self.turn[...] = self.n1[...].T

        def body(i, _):
            j, c = lax.div(i, per), lax.rem(i, per) * TILE
            y = dot(self.turn[...], self.qkv[:, pl.ds(pl.multiple_of(i * TILE, TILE), TILE)])
            ref = self.qkv_part(self.ga, j, c, TILE)
            ref[...] = y.astype(BF).reshape(ref.shape)
            return 0

        lax.fori_loop(0, 3 * per, body, 0)


def run_all(k):
    for i in range(8):
        k.small[i] = jnp.zeros(k.small.shape[1:], F32)
    for s in range(k.S):
        k.embed(s)
        k.project(s)
        k.attend_sequence(s)
        k.outer(s)
        k.second_norm(s)
    k.up()
    k.down()
    k.mask_cotangent()
    k.grad_pre()
    k.turn_activated()
    k.grad_down(0, 1)
    k.grad_up(0, 1)
    k.grad_normed_two()
    k.norm_two_back()
    k.grad_outer()
    k.grad_attended()
    for s in range(k.S):
        k.attend_back_sequence(s)
        k.grad_normed_one(s)
        k.norm_one_back(s)
    k.grad_inner()


def flip(index, bit):
    return index + bit - 2 * bit * lax.rem(lax.div(index, bit), 2)


def pick(table, index):
    value = table[0]
    for i in range(1, len(table)):
        value = jnp.where(index == i, table[i], value)
    return value


class Links:
    def __init__(self, Z, S, part):
        self.Z, self.S, self.part = Z, S, part
        self.r, self.z = lax.axis_index("rows"), lax.axis_index("seq")
        r = self.r
        self.core, self.xn, self.yn = flip(r, 1), flip(r, 2), flip(r, 4)
        self.diag = flip(self.xn, 4)
        self.pending = []
        near, far = flip(self.z, 1), flip(self.z, 2)
        self.near, self.far = near, far
        self.order = [self.z, near, far, flip(near, 2)]

    def barrier(self):
        bar = pltpu.get_barrier_semaphore()
        peers = [(self.core, self.z), (self.xn, self.z), (self.yn, self.z)]
        peers += [(self.r, lax.rem(self.z + i, self.Z)) for i in range(1, self.Z)]
        for peer in peers:
            pl.semaphore_signal(bar, 1, device_id=peer, device_id_type=pl.DeviceIdType.MESH)
        pl.semaphore_wait(bar, len(peers))

    def send(self, src, dst, ss, rs, peer, cond=None, owner=None):
        copy = pltpu.make_async_remote_copy(
            src, dst, ss, rs, device_id=peer, device_id_type=pl.DeviceIdType.MESH
        )
        if cond is None:
            copy.start()
        else:
            pl.when(cond)(copy.start)
        self.pending.append((owner, cond, copy))

    def arrived(self, dst, rs, cond=None):
        copy = pltpu.make_async_remote_copy(
            dst, dst, rs, rs, device_id=(self.core, self.z), device_id_type=pl.DeviceIdType.MESH
        )
        if cond is None:
            copy.wait_recv()
        else:
            pl.when(cond)(copy.wait_recv)

    def flush(self, src=None):
        left = []
        for item in self.pending:
            owner, cond, copy = item
            if src is not None and owner is not src:
                left.append(item)
            elif cond is None:
                copy.wait_send()
            else:
                pl.when(cond)(copy.wait_send)
        self.pending = left

    def gather(self, w, ss, rs):
        Z, z = self.Z, self.z
        count = [0]

        def go(row, zz, peer, cond=None):
            i = row * Z + zz
            self.send(w.at[i], w.at[i], ss.at[count[0]], rs.at[i], peer, cond, w)
            count[0] += 1

        def got(row, zz):
            i = row * Z + zz
            self.arrived(w.at[i], rs.at[i])

        def own(i):
            zz = self.order[i]
            if i:
                got(self.r, zz)
            if i == 0:
                go(self.r, zz, (self.r, self.far))
            if i == 0 or i == 2:
                go(self.r, zz, (self.r, self.near))
            go(self.r, zz, (self.xn, z))
            go(self.r, zz, (self.yn, z))
            go(self.r, zz, (self.core, z))

        def side(i):
            zz = self.order[i]
            got(self.xn, zz)
            if i % 2 == 0:
                go(self.xn, zz, (self.yn, z))
            go(self.xn, zz, (self.core, z))
            got(self.yn, zz)
            if i % 2 == 1:
                go(self.yn, zz, (self.xn, z))
            go(self.yn, zz, (self.core, z))

        def far(i):
            zz = self.order[i]
            got(self.diag, zz)
            go(self.diag, zz, (self.core, z))

        def last():
            for row in (self.r, self.xn, self.yn, self.diag):
                for i in range(Z):
                    got(flip(row, 1), self.order[i])

        return own, side, far, last

    def gather_small(self, w, ss, rs):
        Z, z = self.Z, self.z
        half = Z // 2

        def block(row, lo=0, n=Z):
            return w.at[pl.ds(row * Z + lo, n)]

        def go(ref, n, peer):
            self.send(ref, ref, ss.at[n], rs.at[n], peer)

        def along_z():
            for step in range(1, Z):
                go(block(self.r, z, 1), step, (self.r, lax.rem(z + step, Z)))

        def spread():
            for step in range(1, Z):
                self.arrived(block(self.r, lax.rem(z + Z - step, Z), 1), rs.at[step])
            go(block(self.r), 4, (self.xn, z))
            go(block(self.r), 5, (self.yn, z))
            go(block(self.r), 6, (self.core, z))

        def forward():
            self.arrived(block(self.xn), rs.at[4])
            go(block(self.xn, 0, half), 7, (self.yn, z))
            self.arrived(block(self.yn), rs.at[5])
            go(block(self.yn, half, half), 8, (self.xn, z))
            go(block(self.xn), 9, (self.core, z))
            go(block(self.yn), 10, (self.core, z))

        def corner():
            self.arrived(block(self.diag, 0, half), rs.at[7])
            self.arrived(block(self.diag, half, half), rs.at[8])
            go(block(self.diag), 11, (self.core, z))

        def last():
            self.arrived(block(self.core), rs.at[6])
            self.arrived(block(flip(self.xn, 1)), rs.at[9])
            self.arrived(block(flip(self.yn, 1)), rs.at[10])
            self.arrived(block(flip(self.diag, 1)), rs.at[11])

        return along_z, spread, forward, corner, last

    def exchange_in(self, src, dst, ss, rs, local, seqs):
        L = self.part * self.Z
        for i in seqs:
            for step in range(1, self.Z):
                to = lax.rem(self.z + step, self.Z)
                rows = pl.ds(i * L + self.z * self.part, self.part)
                n = i * (self.Z - 1) + step - 1
                self.send(src.at[to * self.S + i], dst.at[rows], ss.at[n], rs.at[n], (self.r, to))
            rows = pl.ds(i * L + self.z * self.part, self.part)
            pltpu.make_async_copy(src.at[self.z * self.S + i], dst.at[rows], local.at[i]).start()

    def exchange_in_done(self, src, dst, rs, local, i):
        L = self.part * self.Z
        for step in range(1, self.Z):
            source = lax.rem(self.z + self.Z - step, self.Z)
            rows = pl.ds(i * L + source * self.part, self.part)
            self.arrived(dst.at[rows], rs.at[i * (self.Z - 1) + step - 1])
        rows = pl.ds(i * L + self.z * self.part, self.part)
        pltpu.make_async_copy(src.at[self.z * self.S + i], dst.at[rows], local.at[i]).wait()

    def exchange_out(self, src, dst, ss, rs, local, i):
        L = self.part * self.Z
        for step in range(1, self.Z):
            to = lax.rem(self.z + step, self.Z)
            rows = pl.ds(i * L + to * self.part, self.part)
            n = i * (self.Z - 1) + step - 1
            self.send(src.at[rows], dst.at[self.z * self.S + i], ss.at[n], rs.at[n], (self.r, to), None, dst)
        rows = pl.ds(i * L + self.z * self.part, self.part)
        pltpu.make_async_copy(src.at[rows], dst.at[self.z * self.S + i], local.at[i]).start()

    def exchange_out_done(self, src, dst, rs, local, i):
        L = self.part * self.Z
        for step in range(1, self.Z):
            source = lax.rem(self.z + self.Z - step, self.Z)
            self.arrived(dst.at[source * self.S + i], rs.at[i * (self.Z - 1) + step - 1])
        rows = pl.ds(i * L + self.z * self.part, self.part)
        pltpu.make_async_copy(src.at[rows], dst.at[self.z * self.S + i], local.at[i]).wait()

    def scatter(self, g, base, part, inbox, box0, ss, rs, total):
        Z, z = self.Z, self.z
        half = Z // 2
        chip = lax.div(self.r, 2)
        k = lax.rem(self.r, 2)
        cx, cy = flip(chip, 1), flip(chip, 2)
        cd = flip(cx, 2)
        rows = total.shape[0]

        def block(c, parity, lo, n):
            return g.at[pl.ds(base + (2 * c + parity) * Z + lo, n), pl.ds(part * rows, rows)]

        def inslot(i, n):
            return inbox.at[pl.ds(box0 + i, n)]

        def add(dst, src, n):
            def body(i, _):
                dst[i] = (dst[i].astype(F32) + src[i].astype(F32)).astype(BF)
                return 0

            lax.fori_loop(0, n, body, 0)

        XY = 4 * Z
        ZB = XY + 6 * half

        def core_send_all():
            for c in range(4):
                core_send(c)

        def core_send(c):
            self.send(block(c, 1 - k, 0, Z), inslot(c * Z, Z), ss.at[c], rs.at[c], (self.core, z))

        def core_add(c):
            self.arrived(inslot(c * Z, Z), rs.at[c])
            add(block(c, k, 0, Z), inslot(c * Z, Z), Z)

        def xy_send(slot, c, lo, peer):
            i = XY + slot * half
            self.send(block(c, k, lo, half), inslot(i, half), ss.at[4 + slot], rs.at[4 + slot], (peer, z))

        def xy_add(slot, c, lo):
            i = XY + slot * half
            self.arrived(inslot(i, half), rs.at[4 + slot])
            add(block(c, k, lo, half), inslot(i, half), half)

        def first():
            core_add(cd)
            xy_send(0, cd, 0, self.xn)
            xy_send(2, cd, half, self.yn)
            core_add(cx)
            xy_send(1, cx, 0, self.xn)
            core_add(cy)
            xy_send(3, cy, half, self.yn)
            core_add(chip)

        def second():
            xy_add(0, cy, 0)
            xy_send(4, cy, 0, self.yn)
            xy_add(2, cx, half)
            xy_send(5, cx, half, self.xn)

        def second_own():
            xy_add(1, chip, 0)
            xy_add(3, chip, half)

        def third():
            xy_add(4, chip, 0)
            xy_add(5, chip, half)

        def z_send(slot, target, peer):
            box = inslot(ZB + slot, 1)
            self.send(block(chip, k, target, 1), box, ss.at[10 + slot], rs.at[10 + slot], (self.r, peer))

        def z_first():
            z_send(1, self.order[3], self.near)
            z_send(0, self.near, self.near)

        def z_second():
            self.arrived(inslot(ZB + 1, 1), rs.at[11])
            add(block(chip, k, self.far, 1), inslot(ZB + 1, 1), 1)
            z_send(2, self.far, self.far)

        def final():
            self.arrived(inslot(ZB, 1), rs.at[10])
            total[...] = block(chip, k, z, 1)[0].astype(F32) + inbox[box0 + ZB].astype(F32)
            self.arrived(inslot(ZB + 2, 1), rs.at[12])
            total[...] += inbox[box0 + ZB + 2].astype(F32)

        return core_send_all, first, second, second_own, third, z_first, z_second, final


def compute_kernel(x, mask, g_in, time, norm, wa, wm, out, gin, ga, gm, small, *scratch):
    names = ("g", "h", "n1", "qkv", "att", "mid", "n2", "act", "du", "soft", "dn", "gb", "turn", "sums")
    refs = dict(zip(names, scratch))
    sums = refs.pop("sums")
    pltpu.sync_copy(x, gin)
    pltpu.sync_copy(g_in, refs["g"])
    layer = Layer(
        x=gin, mask=mask, time=time, norm=norm, wa=wa, wm=wm, out=out, ga=ga, gm_down=gm, gm_up=gm, small=sums, lane=0, **refs
    )
    run_all(layer)
    for i in range(8):
        small[i : i + 1, :] = jnp.sum(sums[i], axis=0, keepdims=True)


def layer_scratch(T, D, S, L):
    heads = D // HEAD_DIM
    return dict(
        h=pltpu.VMEM((T, D), F32),
        n1=pltpu.VMEM((T, D), BF),
        qkv=pltpu.VMEM((T, 3 * D), BF),
        att=pltpu.VMEM((T, D), BF),
        mid=pltpu.VMEM((T, D), F32),
        n2=pltpu.VMEM((T, D), BF),
        act=pltpu.VMEM((FF // D * T, D), BF),
        du=pltpu.VMEM((T, FF), BF),
        soft=pltpu.VMEM((S * heads, L, L), BF),
        dn=pltpu.VMEM((T, D), F32),
        gb=pltpu.VMEM((T, D), BF),
        turn=pltpu.VMEM((D, D), BF),
        sums=pltpu.VMEM((8, 8, D), F32),
    )


def pad_rows(x):
    return jnp.pad(x, ((0, 8 - x.shape[0]), (0, 0)))


def rows_split(flat, groups, parts, D):
    return flat.reshape(groups, -1, parts, D).transpose(0, 2, 1, 3).reshape(groups, -1, D)


def rows_join(block, parts, D):
    groups = block.shape[0]
    return block.reshape(groups, parts, -1, D).transpose(0, 2, 1, 3).reshape(-1)


def adamw(master, moment_one, moment_two, gradient, step_rate):
    first_new = 0.5 * moment_one + 0.5 * gradient
    second_new = 0.5 * moment_two + 0.5 * gradient * gradient
    correct = 1.0 - 0.5**STEP
    update = first_new / correct / (jnp.sqrt(second_new / correct) + 1e-08)
    return (master - step_rate * (update + 0.1 * master), first_new, second_new)


def general(
    resid_in,
    mask,
    steps_row,
    cotangent,
    attn_master,
    attn_first,
    attn_second,
    mlp_master,
    mlp_first,
    mlp_second,
    norm_master,
    norm_first,
    norm_second,
    time_master,
    time_first,
    time_second,
):
    D = resid_in.shape[2]
    axes = ("rows", "seq")
    seq_count = lax.axis_size("seq")
    S = resid_in.shape[0] // seq_count
    L = resid_in.shape[1] * seq_count
    T = S * L
    attn_full = lax.all_gather(attn_master.astype(BF), axes, axis=0, tiled=True)
    mlp_full = lax.all_gather(mlp_master.astype(BF), axes, axis=0, tiled=True)
    inner = 3 * D * D
    wide = D * FF
    wa = jnp.concatenate(
        (rows_split(attn_full[:inner], 24, 3, D), attn_full[inner:].reshape(8, -1, D))
    )
    wm = jnp.concatenate((rows_split(mlp_full[:wide], 16, FF // D, D), mlp_full[wide:].reshape(16, -1, D)))
    exchange = functools.partial(lax.all_to_all, axis_name="seq", split_axis=0, concat_axis=1, tiled=True)
    x = exchange(resid_in).reshape(T, D)
    g = exchange(cotangent).reshape(T, D)
    mask_t = jnp.pad(exchange(mask.astype(BF)).T, ((0, 0), (0, LANES - S)))
    steps_use = lax.dynamic_slice_in_dim(steps_row, lax.axis_index("seq") * S, S, 0)
    time_rows = pad_rows(jnp.take(time_master, steps_use, axis=0))
    V = pl.BlockSpec(memory_space=pltpu.VMEM)
    A = pl.BlockSpec(memory_space=pl.ANY)
    shape = jax.ShapeDtypeStruct
    scratch = layer_scratch(T, D, S, L)
    out, gin, ga, gm, small = pl.pallas_call(
        compute_kernel,
        out_shape=(shape((T, D), BF), shape((T, D), BF), shape(wa.shape, BF), shape(wm.shape, BF), shape((8, D), F32)),
        in_specs=[A, V, A, V, V, V, V],
        out_specs=(V,) * 5,
        scratch_shapes=[pltpu.VMEM((T, D), BF)] + list(scratch.values()),
        compiler_params=pltpu.CompilerParams(vmem_limit_bytes=62 << 20),
    )(x, mask_t, g, time_rows, pad_rows(norm_master), wa, wm)
    attn_flat = jnp.concatenate((rows_join(ga[:24], 3, D), ga[24:].reshape(-1))).astype(F32)
    mlp_flat = jnp.concatenate((rows_join(gm[:16], FF // D, D), gm[16:].reshape(-1))).astype(F32)
    attn_grad = lax.psum_scatter(attn_flat, axes, scatter_dimension=0, tiled=True)
    mlp_grad = lax.psum_scatter(mlp_flat, axes, scatter_dimension=0, tiled=True)
    every = lax.all_gather(small, axes, axis=0)
    spread = functools.partial(lax.all_to_all, axis_name="seq", split_axis=1, concat_axis=0, tiled=True)
    return finish(
        spread(out.reshape(S, L, D)),
        spread(gin.reshape(S, L, D)),
        lax.all_gather(steps_row, "rows", axis=0, tiled=True),
        every,
        adamw(attn_master, attn_first, attn_second, attn_grad, 0.05),
        adamw(mlp_master, mlp_first, mlp_second, mlp_grad, 0.03),
        (norm_master, norm_first, norm_second),
        (time_master, time_first, time_second),
        S,
    )


def finish(resid_out, grad_in, steps, every, attn, mlp, norm, time, S):
    D = every.shape[2]
    norm_grad = jnp.sum(every[:, :5], axis=0)
    chosen = (jnp.arange(time[0].shape[0], dtype=jnp.int32)[:, None] == steps[None, :]).astype(F32)
    time_grad = jnp.dot(chosen, every[:, 5 : 5 + S].reshape(-1, D), precision=lax.Precision.HIGHEST)
    return (
        resid_out,
        grad_in,
        *attn,
        attn[0].astype(BF),
        *mlp,
        mlp[0].astype(BF),
        *adamw(*norm, norm_grad, 0.2),
        *adamw(*time, time_grad, 0.3),
    )


LAYER_REFS = ("h", "n1", "qkv", "att", "mid", "n2", "act", "du", "soft", "dn", "turn", "sums")


def whole_kernel(
    cfg, resid, cot, mask_in, time, tags, norm, sa, sm, resid_out, grad_in, ta, tm, every_out, *scratch
):
    Z, S, part = cfg
    names = (
        "wa", "wm", "inbox", "x", "g", "mask", "h", "n1",
        "qkv", "att", "mid", "n2", "act", "du", "soft", "dn",
        "turn", "sums", "every", "sem_a", "sem_m", "sem_e", "sem_in", "sem_cot",
        "sem_out", "sem_gin", "sem_mask", "loc", "sem_ra", "sem_rm", "credit", "total",
    )
    v = dict(zip(names, scratch))
    wm, ga = v["wm"], v["act"].reshape(GROUPS, v["wa"].shape[1], v["wa"].shape[2])
    half = GROUPS // 2
    grads = wm.at[pl.ds(half, GROUPS)]
    k = Layer(
        x=v["x"], out=v["x"], g=v["g"], mask=v["mask"], time=time, norm=norm, wa=v["wa"], wm=wm.at[pl.ds(0, GROUPS)],
        ga=ga, gm_up=grads, gm_down=grads, small=v["sums"], gb=v["n2"], lane=lax.axis_index("seq") * S,
        **{n: v[n] for n in LAYER_REFS[:-1]},
    )
    net = Links(Z, S, part)
    me = net.r * Z + net.z
    loc = v["loc"]
    own_a = pltpu.make_async_copy(sa, v["wa"].at[me], loc.at[4, 0])
    own_m = pltpu.make_async_copy(sm, wm.at[me], loc.at[4, 1])
    own_a.start()
    own_m.start()
    for i in range(8):
        k.small[i] = jnp.zeros(k.small.shape[1:], F32)
    net.barrier()
    own_a.wait()
    own_m.wait()

    def pair(name):
        return v[name].at[0], v[name].at[1]

    def pump(events, n=1):
        for _ in range(n):
            if events:
                events.pop(0)()

    a_own, a_side, a_far, a_last = net.gather(v["wa"], *pair("sem_a"))
    m_own, m_side, m_far, m_last = net.gather(wm, *pair("sem_m"))

    def stream(s):
        net.exchange_in(resid, k.x, *pair("sem_in"), loc.at[0], [s])

    a_own(0)
    m_own(0)
    for step in range(1, Z):
        to = lax.rem(net.z + step, Z)
        rows = pl.ds(net.z * part, part)
        net.send(mask_in, k.mask.at[rows], v["sem_mask"].at[0, step], v["sem_mask"].at[1, step], (net.r, to))
    own_mask = pltpu.make_async_copy(mask_in, k.mask.at[pl.ds(net.z * part, part)], loc.at[4, 2])
    own_mask.start()
    a_own(1)
    a_side(0)
    a_own(2)
    stream(0)
    a_side(1)
    a_far(0)
    m_own(1)
    a_own(3)
    a_side(2)
    a_far(1)
    m_side(0)
    m_own(2)
    stream(1)
    a_side(3)
    a_far(2)
    stream(2)
    a_far(3)
    a_last()
    net.exchange_in(cot, k.g, *pair("sem_cot"), loc.at[1], range(S))
    rm = [
        functools.partial(m_side, 1),
        functools.partial(m_own, 3),
        functools.partial(m_far, 0),
        functools.partial(m_side, 2),
        functools.partial(m_far, 1),
        functools.partial(m_side, 3),
        functools.partial(m_far, 2),
        functools.partial(m_far, 3),
        m_last,
    ]
    own_mask.wait()
    for step in range(1, Z):
        source = lax.rem(net.z + Z - step, Z)
        net.arrived(k.mask.at[pl.ds(source * part, part)], v["sem_mask"].at[1, step])

    for s in range(S):
        net.exchange_in_done(resid, k.x, v["sem_in"].at[1], loc.at[0], s)
        k.embed(s)
        pump(rm)
        k.project(s)
        pump(rm)
        k.attend_sequence(s)
        pump(rm)
        k.outer(s)
        k.second_norm(s)
    pump(rm, len(rm))
    k.up()
    k.down()
    for s in range(S):
        net.exchange_out(k.out, resid_out, *pair("sem_out"), loc.at[2], s)
    for s in range(S):
        net.exchange_in_done(cot, k.g, v["sem_cot"].at[1], loc.at[1], s)
    k.mask_cotangent()
    k.grad_pre()
    net.flush(wm)
    k.turn_activated()
    rows = sa.shape[0]
    parts = sm.shape[0] // rows
    boxes = v["inbox"].shape[0] // parts
    totals = [v["total"].at[pl.ds(p * rows, rows)] for p in range(parts + 1)]
    pieces = [
        net.scatter(wm, half, p, v["inbox"], p * boxes, v["sem_rm"].at[0, p], v["sem_rm"].at[1, p], totals[p])
        for p in range(parts)
    ]
    (p_core, p_first, p_second, p_own, p_third, p_z, p_zz, p_final) = pieces[0]
    (q_core, q_first, q_second, q_own, q_third, q_z, q_zz, q_final) = pieces[1]
    k.grad_down(0, parts)
    k.grad_up(0, parts)
    p_core()
    k.grad_down(1, parts)
    p_first()
    k.grad_up(1, parts)
    q_core()
    k.grad_normed_two()
    credit = v["credit"]
    peers = ((net.core, net.z), (net.xn, net.z), (net.yn, net.z), (net.r, net.near), (net.r, net.far))
    for peer in peers:
        pl.semaphore_signal(credit, 1, device_id=peer, device_id_type=pl.DeviceIdType.MESH)
    q_first()
    k.norm_two_back()
    k.grad_outer()
    k.grad_attended()
    net.flush(resid_out)
    for s in range(S):
        net.exchange_out_done(k.out, resid_out, v["sem_out"].at[1], loc.at[2], s)
    k.attend_back_sequence(0)
    p_second()
    k.grad_normed_one(0)
    k.norm_one_back(0)
    net.exchange_out(k.x, grad_in, *pair("sem_gin"), loc.at[3], 0)
    k.attend_back_sequence(1)
    p_own()
    q_second()
    k.grad_normed_one(1)
    k.norm_one_back(1)
    net.exchange_out(k.x, grad_in, *pair("sem_gin"), loc.at[3], 1)
    k.attend_back_sequence(2)
    k.grad_inner()
    pl.semaphore_wait(credit, len(peers))
    (a_core, a_first, a_second, a_own, a_third, a_z, a_zz, a_final) = net.scatter(
        ga, 0, 0, wm.reshape(wm.shape[0] * parts, rows, wm.shape[2]), 0, *pair("sem_ra"), totals[parts]
    )
    a_core()
    p_third()
    p_z()
    k.grad_normed_one(2)
    a_first()
    k.norm_one_back(2)
    net.exchange_out(k.x, grad_in, *pair("sem_gin"), loc.at[3], 2)
    for i in range(8):
        v["every"][me, i : i + 1, 0 : k.D] = jnp.sum(k.small[i], axis=0, keepdims=True)
    v["every"][me, :, k.D : k.D + LANES] = tags[...]
    e_z, e_spread, e_forward, e_corner, e_last = net.gather_small(v["every"], *pair("sem_e"))
    e_z()
    q_own()
    q_third()
    q_z()
    p_zz()
    a_second()
    e_spread()
    q_zz()
    e_forward()
    a_own()
    p_final()
    e_corner()
    a_third()
    a_z()
    q_final()
    a_zz()
    e_last()
    a_final()
    for s in range(S):
        net.exchange_out_done(k.x, grad_in, v["sem_gin"].at[1], loc.at[3], s)
    outs = [pltpu.make_async_copy(totals[parts], ta, loc.at[4, 0])]
    outs += [pltpu.make_async_copy(totals[p], tm.at[pl.ds(p * rows, rows)], loc.at[0, p]) for p in range(parts)]
    outs.append(pltpu.make_async_copy(v["every"], every_out, loc.at[4, 2]))
    for copy in outs:
        copy.start()
    for copy in outs:
        copy.wait()
    net.flush()


def walk(is_split, parts, rows, D, visit):
    per = D // LANES

    def split():
        n = rows // parts
        for j in range(parts):
            for c in range(per):
                visit(pl.ds(j * n, n), pl.ds(c * LANES, LANES), pl.ds(j * per + c, n, stride=parts * per))

    def plain():
        for c in range(per):
            visit(pl.ds(0, rows), pl.ds(c * LANES, LANES), pl.ds(c, rows, stride=per))

    pl.when(is_split)(split)
    pl.when(jnp.logical_not(is_split))(plain)


def device_kinds():
    Z, R = lax.axis_size("seq"), lax.axis_size("rows")
    device = lax.axis_index("rows") * Z + lax.axis_index("seq")
    return device < R * Z * 3 // 4, device < R * Z // 2


def before_kernel(S, steps, mask, time_master, attn, mlp, sa, sm, mask_out, time_rows, tags, board, sems):
    D = sa.shape[1]
    first = lax.axis_index("seq") * S
    time_rows[...] = jnp.zeros(time_rows.shape, F32)
    copies = [
        pltpu.make_async_copy(time_master.at[pl.ds(steps[first + s], 1)], time_rows.at[pl.ds(s, 1)], sems.at[s])
        for s in range(S)
    ]
    for copy in copies:
        copy.start()
    row = lax.broadcasted_iota(jnp.int32, tags.shape, 0)
    value = jnp.full(tags.shape, -1, jnp.int32)
    for s in range(S):
        value = jnp.where(row == 5 + s, steps[first + s], value)
    tags[...] = value.astype(F32)
    board[...] = jnp.zeros(board.shape, F32)
    board[0 : mask.shape[0], 0 : mask.shape[1]] = mask[...].astype(F32)
    mask_out[...] = board[...].T[0 : mask.shape[1], :].astype(BF)
    is_inner, is_up = device_kinds()

    def cast(src, dst):
        def visit(rows, cols, lines):
            dst[rows, cols] = src[lines, :].astype(BF)

        return visit

    walk(is_inner, 3, sa.shape[0], D, cast(attn, sa))
    walk(is_up, FF // D, sm.shape[0], D, cast(mlp, sm))
    for copy in copies:
        copy.wait()


def adamw_low(master, moment_one, moment_two, gradient, step_rate):
    first_new = 0.5 * moment_one + 0.5 * gradient
    second_new = 0.5 * moment_two + 0.5 * gradient * gradient
    scale = 1.0 / (1.0 - 0.5**STEP)
    update = (first_new * scale) / (jnp.sqrt(second_new * scale) + 1e-08)
    return master - step_rate * (update + 0.1 * master), first_new, second_new


def after_kernel(ta, tm, every, *refs):
    D = ta.shape[1]
    flat, norm, time, tokens = refs[0:6], refs[6:9], refs[9:12], refs[12:14]
    flat_out, norm_out, time_out, tokens_out = refs[14:22], refs[22:25], refs[25:28], refs[28:30]
    held, low, sems = refs[30:36], refs[36:38], refs[38]
    step = pl.program_id(0)
    is_inner, is_up = device_kinds()
    loads = [pltpu.make_async_copy(a, b, sems.at[i]) for i, (a, b) in enumerate(zip(flat, held))]
    ready = (*held[:3], low[0], *held[3:], low[1])
    stores = [pltpu.make_async_copy(a, b, sems.at[6 + i]) for i, (a, b) in enumerate(zip(ready, flat_out))]

    def update(kept, grad, rate):
        def visit(rows, cols, lines):
            values = adamw_low(*(old[lines, :] for old in kept), grad[rows, cols], rate)
            for new, value in zip(kept, values):
                new[lines, :] = value

        return visit

    for new, old in zip(tokens_out, tokens):
        new[...] = old[...]

    @pl.when(step == 0)
    def _():
        for copy in loads:
            copy.start()
        total = every[0, :, 0:D]
        for i in range(1, every.shape[0]):
            total = total + every[i, :, 0:D]
        values = adamw_low(*(old[...] for old in norm), total[0:5], 0.2)
        for new, value in zip(norm_out, values):
            new[...] = value

    @pl.when(step == 1)
    def _():
        for copy in loads:
            copy.wait()
        walk(is_inner, 3, ta.shape[0], D, update(held[:3], ta, 0.05))
        low[0][...] = held[0][...].astype(BF)
        walk(is_up, FF // D, tm.shape[0], D, update(held[3:], tm, 0.03))
        low[1][...] = held[3][...].astype(BF)
        for copy in stores:
            copy.start()

    @pl.when(step == pl.num_programs(0) - 1)
    def _():
        for copy in stores:
            copy.wait()

    n = time[0].shape[0]
    rows = every.shape[0] * every.shape[1]
    tag = every[:, :, D : D + LANES].reshape(rows, LANES)[:, 0:1]
    at = (lax.broadcasted_iota(jnp.int32, (rows, n), 1) + step * n).astype(F32)
    chosen = jnp.where(tag == at, 1.0, 0.0).astype(BF)
    rest = every[:, :, 0:D].reshape(rows, D)
    grad = None
    for _ in range(3):
        low = rest.astype(BF)
        rest = rest - low.astype(F32)
        y = dot(chosen, low, TN)
        grad = y if grad is None else grad + y
    values = adamw_low(*(old[...] for old in time), grad, 0.3)
    for new, value in zip(time_out, values):
        new[...] = value


def fast(
    resid_in,
    mask,
    steps_row,
    cotangent,
    attn_master,
    attn_first,
    attn_second,
    mlp_master,
    mlp_first,
    mlp_second,
    norm_master,
    norm_first,
    norm_second,
    time_master,
    time_first,
    time_second,
):
    D = resid_in.shape[2]
    Z = lax.axis_size("seq")
    R = lax.axis_size("rows")
    S = resid_in.shape[0] // Z
    part = resid_in.shape[1]
    L = part * Z
    T = S * L
    V = pl.BlockSpec(memory_space=pltpu.VMEM)
    A = pl.BlockSpec(memory_space=pl.ANY)
    shape = jax.ShapeDtypeStruct
    dma = pltpu.SemaphoreType.DMA
    attn = [a.reshape(-1, LANES) for a in (attn_master, attn_first, attn_second)]
    mlp = [a.reshape(-1, LANES) for a in (mlp_master, mlp_first, mlp_second)]
    sa_shape = (attn_master.shape[0] // D, D)
    sm_shape = (mlp_master.shape[0] // D, D)
    sa, sm, mask_in, time_rows, tags = pl.pallas_call(
        functools.partial(before_kernel, S),
        out_shape=(
            shape(sa_shape, BF),
            shape(sm_shape, BF),
            shape((part, LANES), BF),
            shape((8, D), F32),
            shape((8, LANES), F32),
        ),
        in_specs=[pl.BlockSpec(memory_space=pltpu.SMEM), V, A, V, V],
        out_specs=(V,) * 5,
        scratch_shapes=[pltpu.VMEM((LANES, LANES), F32), dma((S,))],
        compiler_params=pltpu.CompilerParams(vmem_limit_bytes=63 << 20),
    )(steps_row, mask, time_master, attn[0], mlp[0])
    sc = layer_scratch(T, D, S, L)
    scratch = [
        pltpu.VMEM((GROUPS, *sa.shape), BF),
        pltpu.VMEM((GROUPS * 3 // 2, *sm.shape), BF),
        pltpu.VMEM((sm.shape[0] // sa.shape[0] * (4 * Z + 6 * (Z // 2) + Z - 1), *sa.shape), BF),
        pltpu.VMEM((T, D), BF),
        pltpu.VMEM((T, D), BF),
        pltpu.VMEM((L, LANES), BF),
        *(sc[n] for n in LAYER_REFS),
        pltpu.VMEM((R * Z, 8, D + LANES), F32),
        *(dma((2, n)) for n in (40, 40, 12)),
        *(dma((2, S * (Z - 1))) for _ in range(4)),
        dma((2, Z)),
        dma((5, S)),
        dma((2, 16)),
        dma((2, sm.shape[0] // sa.shape[0], 16)),
        pltpu.SemaphoreType.REGULAR,
        pltpu.VMEM((sa.shape[0] + sm.shape[0], D), F32),
    ]
    resid_out, grad_in, ta, tm, every = pl.pallas_call(
        functools.partial(whole_kernel, (Z, S, part)),
        out_shape=(
            shape(resid_in.shape, BF),
            shape(resid_in.shape, BF),
            shape(sa.shape, F32),
            shape(sm.shape, F32),
            shape((R * Z, 8, D + LANES), F32),
        ),
        in_specs=[A, A, A, V, V, V, A, A],
        out_specs=(A,) * 5,
        scratch_shapes=scratch,
        compiler_params=pltpu.CompilerParams(
            collective_id=0, has_side_effects=True, vmem_limit_bytes=63 << 20
        ),
    )(resid_in, cotangent, mask_in, time_rows, tags, norm_master, sa, sm)
    steps = 5
    norm = (norm_master, norm_first, norm_second)
    time = (time_master, time_first, time_second)
    rows = time_master.shape[0] // steps
    moving = pl.BlockSpec((rows, D), lambda i: (i, 0))

    def fixed(a):
        return pl.BlockSpec(a.shape, lambda i: (0,) * len(a.shape))

    blocks = resid_in.shape[0] // S
    tokens = pl.BlockSpec((S, part, D), lambda i: (jnp.minimum(i, blocks - 1), 0, 0))
    outs = [shape(a.shape, F32) for a in attn] + [shape(attn[0].shape, BF)]
    outs += [shape(a.shape, F32) for a in mlp] + [shape(mlp[0].shape, BF)]
    news = pl.pallas_call(
        after_kernel,
        grid=(steps,),
        out_shape=(*outs, *(shape(a.shape, F32) for a in (*norm, *time)), *(shape(resid_in.shape, BF),) * 2),
        in_specs=[fixed(a) for a in (ta, tm, every)] + [A] * 6 + [fixed(a) for a in norm] + [moving] * 3 + [tokens] * 2,
        out_specs=(*(A,) * 8, *(fixed(a) for a in norm), *(moving,) * 3, tokens, tokens),
        scratch_shapes=[
            *(pltpu.VMEM(a.shape, F32) for a in (*attn, *mlp)),
            pltpu.VMEM(attn[0].shape, BF),
            pltpu.VMEM(mlp[0].shape, BF),
            dma((14,)),
        ],
        compiler_params=pltpu.CompilerParams(vmem_limit_bytes=63 << 20),
    )(ta, tm, every, *attn, *mlp, *norm, *time, resid_out, grad_in)
    return (*news[14:], *(a.reshape(-1) for a in news[:8]), *news[8:14])


def solution(mesh):
    flat, whole, tokens = P(("rows", "seq")), P(), P("rows", "seq", None)
    fits = mesh.shape["rows"] * mesh.shape["seq"] == GROUPS and mesh.shape["rows"] == 8
    return jax.shard_map(
        fast if fits else general,
        mesh=mesh,
        in_specs=(tokens, P("rows", "seq"), P("rows"), tokens) + (flat,) * 6 + (whole,) * 6,
        out_specs=(tokens, tokens) + (flat,) * 8 + (whole,) * 6,
        check_vma=False,
    )
```
